128 devices in a mesh: fsdp: 16 (over x_hi, z, core), seq: 8 (over x_lo, y).
Axes of the slice: x: 4 (x_hi: 2, x_lo: 2; x = x_hi * 2 + x_lo), y: 4, z: 4, core: 2. Of those that a mesh axis runs over, the one named last changes fastest.
Arguments:
- tokens: bfloat16 [16384, 1536], P(('fsdp', 'seq')), may hold values from -6 to 6
- gain_one: bfloat16 [1536], P(('fsdp', 'seq')), may hold values from 0.099609375 to 1.8984375
- w_qkv: bfloat16 [1536, 2560], P(('fsdp', 'seq')), may hold values from -0.21875 to 0.21875
- w_out: bfloat16 [1536, 1536], P(('fsdp', 'seq')), may hold values from -0.625 to 0.625
- gain_two: bfloat16 [1536], P(('fsdp', 'seq')), may hold values from 0.099609375 to 1.8984375
- w_router: bfloat16 [1536, 4], P(('fsdp', 'seq')), may hold values from -0.109375 to 0.109375
- w_gate: bfloat16 [4, 1536, 1024], P(None, ('fsdp', 'seq')), may hold values from -0.15625 to 0.15625
- w_up: bfloat16 [4, 1536, 1024], P(None, ('fsdp', 'seq')), may hold values from -0.15625 to 0.15625
- w_down: bfloat16 [4, 1024, 1536], P(None, ('fsdp', 'seq')), may hold values from -0.375 to 0.375
- doc_starts: int32 [34], replicated, may hold values from 0 to 16384, as said below
- routes: int32 [16384, 2], P(('fsdp', 'seq')), may hold values from 0 to 3, all different within a row; in each aligned block of 128 rows (0 to 127, 128 to 255, ...) at most 80 rows name the same one
- cotangent: bfloat16 [16384, 1536], P(('fsdp', 'seq')), may hold values from -6 to 6
Outputs:
- output: bfloat16 [16384, 1536], P(('fsdp', 'seq'))
- grad_input: float32 [16384, 1536], P(('fsdp', 'seq'))
- grad_gain_one: float32 [1536], P(('fsdp', 'seq'))
- grad_w_qkv: float32 [1536, 2560], P(('fsdp', 'seq'))
- grad_w_out: float32 [1536, 1536], P(('fsdp', 'seq'))
- grad_gain_two: float32 [1536], P(('fsdp', 'seq'))
- grad_w_router: float32 [1536, 4], P(('fsdp', 'seq'))
- grad_w_gate: float32 [4, 1536, 1024], P(None, ('fsdp', 'seq'))
- grad_w_up: float32 [4, 1536, 1024], P(None, ('fsdp', 'seq'))
- grad_w_down: float32 [4, 1024, 1536], P(None, ('fsdp', 'seq'))
The draws below stay inside these ranges and needn't reach their ends.
Inputs may be any that keep to these rules, and one draw needn't show every extreme that they name: Sorted, not falling, with doc_starts[0] = 0; entries equal to 16384 start no document. A document runs from one start to the next larger one, the last to 16384; each has at most 4096 tokens and one has exactly 4096. Outside that one, each group of 8 devices along seq holds one start on its first device and one on its last. `routes`: A token's two experts differ. At most 80 of one device's 128 tokens name one expert, and on some devices one expert is named by exactly 80.
All inputs are finite; a program needn't handle non-finite values.
Results may differ from the reference program's by a relative error of at most 0.02.
The reference program's roundings to bfloat16 on the way count: a program that leaves them out, or rounds other values in their place, can miss the bound.
Values may be sent and summed in bfloat16 or wider, within the bound.
A program may use at most 320 MiB of HBM per device.

```python
import math
from functools import partial
import jax
import jax.numpy as jnp
import numpy as np
from jax import lax

D = 1536
QUERY_HEADS = 24
KEY_VALUE_HEADS = 8
HEAD_WIDTH = 64
FF = 1024
EXPERTS = 4
TOP = 2
LOOK = 4
TOK_DEV = 128
STREAM_TOKENS = 16384
DOCUMENT_LIMIT = 4096
CAP = 80
QKVW = 2560
N_FSDP = 16
N_SEQ = 8


def draw_doc_starts(key, part):
    key = jax.random.fold_in(key, 17)
    group_rows = TOK_DEV * N_SEQ
    key_first, key_last, key_lead, key_offset = jax.random.split(key, 4)
    group_ids = jnp.arange(N_FSDP, dtype=jnp.int32)
    first_start = jax.random.randint(key_first, (N_FSDP,), 0, TOK_DEV, dtype=jnp.int32)
    first_start = jnp.where(group_ids == 0, 0, first_start)
    last_start = jax.random.randint(key_last, (N_FSDP,), 1, TOK_DEV, dtype=jnp.int32)
    group_base = group_ids * group_rows
    candidates = jnp.concatenate([group_base + first_start, group_base + (N_SEQ - 1) * TOK_DEV + last_start])
    lead_group = jax.random.randint(key_lead, (), 0, N_FSDP - LOOK, dtype=jnp.int32)
    offset = jax.random.randint(key_offset, (), 0, TOK_DEV, dtype=jnp.int32)
    begin = lead_group * group_rows + offset
    finish = begin + LOOK * group_rows
    inside = (candidates > begin) & (candidates < finish)
    candidates = jnp.where(inside, STREAM_TOKENS, candidates)
    every_start = jnp.concatenate([candidates, jnp.stack([begin, finish])])
    return jnp.sort(every_start).astype(jnp.int32)


def levels(own_key, shape, shards, least, high):
    factor_of, own = 1.0, jax.random.fold_in(own_key, 6)
    for position, parts in shards:
        steps = jnp.exp(jax.random.uniform(jax.random.fold_in(own, position), (parts,), jnp.float32, least / len(shards), high / len(shards)))
        factor_of = factor_of * jnp.repeat(steps, shape[position] // parts).reshape([-1 if axis == position else 1 for axis in range(len(shape))])
    return factor_of


def routed_block(key, own, number, rows, number_of, top, limit, lean):
    sequence = jax.random.permutation(key, number_of)
    heavy_load, common = shares(number_of, rows * top, limit, lean, True), shares(number_of, rows * top, limit, lean, False)
    places = jnp.arange(number_of)

    def named(lengths, offset_by):
        used = int((lengths > 0).sum())
        fixed = max(1, used // 4)
        moved = fixed + (places - fixed + offset_by * (used - fixed)) % max(1, number_of - fixed)
        return jnp.zeros((number_of,), jnp.int32).at[sequence[jnp.where(places < fixed, places, moved)]].set(jnp.asarray(lengths, jnp.int32))

    lengths = jnp.where(number % 4 == 0, named(heavy_load, number // 4), named(common, number - number // 4 - 1))
    mixed = jax.random.permutation(jax.random.fold_in(own, 3), number_of)
    donor, taker = mixed[0:number_of // 2 * 2:2], mixed[1:number_of // 2 * 2:2]
    room = jnp.minimum(lengths[donor] - 1, limit - lengths[taker]) // 2
    room = jnp.where((donor == sequence[0]) | (taker == sequence[0]) | (lengths[taker] == 0), 0, jnp.maximum(room, 0))
    moved = jax.random.randint(jax.random.fold_in(own, 4), (number_of // 2,), 0, 1 << 20) % (room + 1)
    lengths = lengths.at[donor].add(-moved).at[taker].add(moved)
    members = jnp.searchsorted(jnp.cumsum(lengths), jnp.arange(rows * top), side="right").astype(jnp.int32)
    listing = members.reshape(top, rows).T
    listing = listing[jax.random.permutation(jax.random.fold_in(own, 1), rows)]
    offset_by = jax.random.randint(jax.random.fold_in(own, 2), (rows, 1), 0, top)
    return jnp.take_along_axis(listing, (jnp.arange(top)[None, :] + offset_by) % top, axis=1)


def shares(amount, total, most, slope, full):
    portions = [(1 << 20) // math.isqrt(standing ** slope) + 1 for standing in range(1, amount + 1)]
    largest = most if full else min(most, max(-(-total // amount), total * portions[0] // sum(portions)))
    least = 1 if total - largest >= amount - 1 else 0
    holding, rest = [largest] + [least] * (amount - 1), total - largest - least * (amount - 1)
    while rest > 0:
        movable = [i for i in range(1, amount) if holding[i] < largest] or [i for i in range(1, amount) if holding[i] < most]
        mass, remaining = sum([portions[i] for i in movable]), rest
        for i in movable:
            more = min(most - holding[i], max(1, remaining * portions[i] // mass), rest)
            holding[i] = holding[i] + more
            rest = rest - more
    return np.array(holding)


def centred(key, dims, width, limit, cuts=(), kind=jnp.bfloat16):
    factor_of = levels(key, dims, cuts, -0.22, 0.18) if cuts else 1.0
    result = jax.random.normal(key, dims, jnp.float32) * width * factor_of
    return jnp.minimum(jnp.maximum(result, -limit), limit).astype(kind)


def setup_inputs(seed: int = 0) -> dict:
    splits = jax.random.split(jax.random.key(seed), 13)
    tokens = centred(splits[0], (STREAM_TOKENS, D), 1.0, 6.0, ((0, 128),))
    gain_one = jnp.clip(1.0 + 0.18 * jax.random.normal(splits[1], (D,), jnp.float32), 0.099609375, 1.8984375).astype(jnp.bfloat16)
    w_qkv = centred(splits[2], (D, QKVW), (D // 2) ** -0.5, 0.21875, ((0, 128),))
    w_out = centred(splits[3], (QUERY_HEADS * HEAD_WIDTH, D), (QUERY_HEADS * HEAD_WIDTH // 16) ** -0.5, 0.625, ((0, 128),))
    gain_two = jnp.clip(1.0 + 0.18 * jax.random.normal(splits[4], (D,), jnp.float32), 0.099609375, 1.8984375).astype(jnp.bfloat16)
    w_router = centred(splits[5], (D, EXPERTS), (2 * D) ** -0.5, 0.109375, ((0, 128),))
    w_gate = centred(splits[6], (EXPERTS, D, FF), D ** -0.5, 0.15625, ((1, 128),))
    w_up = centred(splits[7], (EXPERTS, D, FF), D ** -0.5, 0.15625, ((1, 128),))
    w_down = centred(splits[8], (EXPERTS, FF, D), (FF // 4) ** -0.5, 0.375, ((1, 128),))
    doc_starts = draw_doc_starts(jax.random.fold_in(splits[12], 71), 0)
    routes_keys = jax.random.split(jax.random.fold_in(splits[10], 1), STREAM_TOKENS // TOK_DEV)
    routes_turns = jax.random.permutation(jax.random.fold_in(splits[10], 3), STREAM_TOKENS // TOK_DEV)
    routes = jax.vmap(lambda own, number: routed_block(jax.random.fold_in(splits[10], 2), own, number, TOK_DEV, EXPERTS, TOP, CAP, 2))(routes_keys, routes_turns).reshape((STREAM_TOKENS, TOP))
    cotangent = centred(splits[11], (STREAM_TOKENS, D), 1.0, 6.0, ((0, 128),))
    return {"tokens": tokens, "gain_one": gain_one, "w_qkv": w_qkv, "w_out": w_out, "gain_two": gain_two, "w_router": w_router, "w_gate": w_gate, "w_up": w_up, "w_down": w_down, "doc_starts": doc_starts, "routes": routes, "cotangent": cotangent}


@jax.custom_vjp
def low(v):
    return lax.optimization_barrier(v.astype(jnp.bfloat16)).astype(jnp.float32)

@jax.custom_vjp
def low_back(v):
    return v

def low_keep(v):
    return (low(v), None)

def low_pass(kept, grad):
    return (grad,)

def back_keep(v):
    return (v, None)

def back_low(kept, grad):
    return (low(grad),)
low.defvjp(low_keep, low_pass)
low_back.defvjp(back_keep, back_low)
EPS = 1e-06
NEGATIVE = -1e+30
HIGH = lax.Precision.HIGHEST

def unit_rms(values, gain):
    return values * lax.rsqrt(lax.optimization_barrier(jnp.mean(values * values, axis=-1, keepdims=True)) + EPS) * gain

def doc_number(doc_starts, positions):
    return lax.optimization_barrier(jnp.sum((doc_starts[None, :] <= positions[:, None]).astype(jnp.int32), axis=1))

def attention(query_rows, rows_of_keys, rows_of_values, token_doc):
    rows_per_block = min(512, STREAM_TOKENS)
    count_of_blocks = STREAM_TOKENS // rows_per_block
    reach = DOCUMENT_LIMIT + rows_per_block
    padded_key_rows = jnp.concatenate([jnp.zeros((DOCUMENT_LIMIT, KEY_VALUE_HEADS, HEAD_WIDTH), jnp.float32), rows_of_keys], axis=0)
    padded_value_rows = jnp.concatenate([jnp.zeros((DOCUMENT_LIMIT, KEY_VALUE_HEADS, HEAD_WIDTH), jnp.float32), rows_of_values], axis=0)
    pad_doc = jnp.concatenate([jnp.zeros((DOCUMENT_LIMIT,), jnp.int32), token_doc], axis=0)
    blocked_queries = query_rows.reshape(count_of_blocks, rows_per_block, KEY_VALUE_HEADS, QUERY_HEADS // KEY_VALUE_HEADS, HEAD_WIDTH)

    def one_block(pieces):
        query_blk, block_index = pieces
        start = block_index * rows_per_block
        key_blk = lax.dynamic_slice_in_dim(padded_key_rows, start, reach, 0)
        value_blk = lax.dynamic_slice_in_dim(padded_value_rows, start, reach, 0)
        key_doc = lax.dynamic_slice_in_dim(pad_doc, start, reach, 0)
        query_doc = lax.dynamic_slice_in_dim(token_doc, start, rows_per_block, 0)
        query_pos = start + jnp.arange(rows_per_block, dtype=jnp.int32)
        key_pos = start - DOCUMENT_LIMIT + jnp.arange(reach, dtype=jnp.int32)
        visible = (query_doc[:, None] == key_doc[None, :]) & (key_pos[None, :] <= query_pos[:, None])
        scores = low_back(jnp.einsum('qgrh,kgh->grqk', query_blk, key_blk, precision=HIGH) * HEAD_WIDTH ** (-0.5))
        scores = jnp.where(visible, scores, NEGATIVE)
        row_peak = lax.optimization_barrier(jnp.max(scores, axis=-1, keepdims=True))
        exp_scores = jnp.exp(scores - row_peak)
        attn_probs = low(exp_scores / lax.optimization_barrier(jnp.sum(exp_scores, axis=-1, keepdims=True)))
        return jnp.einsum('grqk,kgh->qgrh', attn_probs, value_blk, precision=HIGH)
    indices = jnp.arange(count_of_blocks, dtype=jnp.int32)
    out_blocks = lax.map(jax.checkpoint(one_block), (blocked_queries, indices))
    return out_blocks.reshape(STREAM_TOKENS, QUERY_HEADS * HEAD_WIDTH)

def forward(inputs, gain_one, w_qkv, w_out, gain_two, w_router, w_gate, w_up, w_down, token_doc, chosen):
    normed_one = low(unit_rms(inputs, gain_one))
    query_key_value_rows = low(low_back(jnp.dot(normed_one, w_qkv, precision=HIGH)))
    head_layout = query_key_value_rows.reshape(STREAM_TOKENS, KEY_VALUE_HEADS, QUERY_HEADS // KEY_VALUE_HEADS + 2, HEAD_WIDTH)
    attended = attention(head_layout[:, :, :-2, :], head_layout[:, :, -2, :], head_layout[:, :, -1, :], token_doc)
    attended = low(low_back(attended))
    branch = low_back(jnp.dot(attended, w_out, precision=HIGH))
    residual = inputs + branch
    normed_two = low(unit_rms(residual, gain_two))
    router_logits = low_back(jnp.dot(normed_two, w_router, precision=HIGH))
    router_probs = jax.nn.softmax(router_logits, axis=-1)
    expert_share = router_probs * chosen
    moe_out = jnp.zeros_like(residual)
    for expert in range(EXPERTS):
        gate_pre = low_back(jnp.dot(normed_two, w_gate[expert], precision=HIGH))
        up_pre = low_back(jnp.dot(normed_two, w_up[expert], precision=HIGH))
        hidden = low(jax.nn.silu(gate_pre) * up_pre)
        expert_out = low_back(jnp.dot(hidden, w_down[expert], precision=HIGH))
        moe_out = moe_out + expert_share[:, expert:expert + 1] * expert_out
    return residual + moe_out

def reference(tokens, gain_one, w_qkv, w_out, gain_two, w_router, w_gate, w_up, w_down, doc_starts, routes, cotangent):
    token_doc = doc_number(doc_starts, jnp.arange(STREAM_TOKENS, dtype=jnp.int32))
    expert_ids = jnp.arange(EXPERTS, dtype=jnp.int32)
    chosen = lax.optimization_barrier(jnp.sum((routes[:, :, None] == expert_ids[None, None, :]).astype(jnp.float32), axis=1))
    bound = partial(forward, token_doc=token_doc, chosen=chosen)
    output, pullback = jax.vjp(bound, tokens.astype(jnp.float32), gain_one.astype(jnp.float32), w_qkv.astype(jnp.float32), w_out.astype(jnp.float32), gain_two.astype(jnp.float32), w_router.astype(jnp.float32), w_gate.astype(jnp.float32), w_up.astype(jnp.float32), w_down.astype(jnp.float32))
    grads = pullback(cotangent.astype(jnp.float32))
    return (output.astype(jnp.bfloat16), grads[0], grads[1], grads[2], grads[3], grads[4], grads[5], grads[6], grads[7], grads[8])
```

```python
import functools

import jax
import jax.numpy as jnp
import numpy as np
from jax import lax
from jax.experimental import pallas as pl
from jax.experimental.pallas import tpu as pltpu
from jax.sharding import PartitionSpec as P

WIDTH = 64
LOOK = 4
EXPERTS = 4
EPS = 1e-06
NEGATIVE = -1e30
BQ = 256
BK = 512
BOTH = ("fsdp", "seq")


def nt(a, b):
    return lax.dot_general(a, b, (((1,), (1,)), ((), ())), preferred_element_type=jnp.float32)


def tn(a, b):
    return lax.dot_general(a, b, (((0,), (0,)), ((), ())), preferred_element_type=jnp.float32)


def nn(a, b):
    return jnp.dot(a, b, preferred_element_type=jnp.float32)


def stack_heads(rows, low):
    heads = rows.shape[1] // WIDTH
    zero = jnp.zeros((rows.shape[0], WIDTH), rows.dtype)
    parts = []
    for h in range(heads):
        part = rows[:, h * WIDTH : (h + 1) * WIDTH]
        parts.append(jnp.concatenate([part, zero] if low else [zero, part], axis=1))
    return jnp.concatenate(parts, axis=0)


def chunk_loops(bounds_ref, step):
    b = pl.program_id(0)
    first, full, diag, end = (bounds_ref[b, i] for i in range(4))
    pl.loop(first, full)(lambda c: step(c, True))
    pl.loop(full, diag)(lambda c: step(c, False))
    pl.loop(diag, end)(lambda c: step(c, True))


def attention_kernel(bounds_ref, lo_ref, q_ref, kv_ref, out_ref, lse_ref, m_ref, l_ref, acc_ref):
    heads = q_ref.shape[1] // WIDTH
    queries = stack_heads(q_ref[...] * 0.125, True)
    m_ref[...] = jnp.full_like(m_ref, NEGATIVE)
    l_ref[...] = jnp.zeros_like(l_ref)
    acc_ref[...] = jnp.zeros_like(acc_ref)
    base = LOOK * 1024 + pl.program_id(0) * BQ

    def step(c, masked):
        start = pl.multiple_of(c * BK, BK)
        rows = kv_ref[pl.ds(start, BK), :]
        scores = nt(queries, rows)
        if masked:
            key = start + lax.broadcasted_iota(jnp.int32, (BQ, BK), 1)
            query = base + lax.broadcasted_iota(jnp.int32, (BQ, BK), 0)
            seen = (key >= lo_ref[...]) & (key <= query)
            scores = jnp.where(jnp.concatenate([seen] * heads, axis=0), scores, NEGATIVE)
        old = m_ref[...]
        new = jnp.maximum(old, jnp.max(scores, axis=1, keepdims=True))
        probs = jnp.exp(scores - new)
        fade = jnp.exp(old - new)
        m_ref[...] = new
        l_ref[...] = l_ref[...] * fade + jnp.sum(probs, axis=1, keepdims=True)
        acc_ref[...] = acc_ref[...] * fade + nn(probs.astype(jnp.bfloat16), rows)

    chunk_loops(bounds_ref, step)
    total = l_ref[...]
    result = acc_ref[...] / total
    out_ref[...] = jnp.concatenate(
        [result[h * BQ : (h + 1) * BQ, WIDTH:] for h in range(heads)], axis=1
    ).astype(jnp.bfloat16)
    lse = jnp.broadcast_to(m_ref[...] + jnp.log(total), acc_ref.shape)
    lse_ref[...] = jnp.transpose(lse)[:8, :]


def attention(bounds, lo, q, kv):
    rows, width = q.shape
    heads = width // WIDTH
    blocks = rows // BQ
    return pl.pallas_call(
        attention_kernel,
        grid=(blocks,),
        in_specs=[
            pl.BlockSpec(memory_space=pltpu.SMEM),
            pl.BlockSpec((BQ, 1), lambda b: (b, 0)),
            pl.BlockSpec((BQ, width), lambda b: (b, 0)),
            pl.BlockSpec(memory_space=pltpu.VMEM),
        ],
        out_specs=[
            pl.BlockSpec((BQ, width), lambda b: (b, 0)),
            pl.BlockSpec((None, 8, heads * BQ), lambda b: (b, 0, 0)),
        ],
        out_shape=[
            jax.ShapeDtypeStruct((rows, width), jnp.bfloat16),
            jax.ShapeDtypeStruct((blocks, 8, heads * BQ), jnp.float32),
        ],
        scratch_shapes=[
            pltpu.VMEM((heads * BQ, 1), jnp.float32),
            pltpu.VMEM((heads * BQ, 1), jnp.float32),
            pltpu.VMEM((heads * BQ, 2 * WIDTH), jnp.float32),
        ],
        compiler_params=pltpu.CompilerParams(vmem_limit_bytes=48 << 20),
        cost_estimate=pl.CostEstimate(
            flops=4 * rows * 4096 * width, bytes_accessed=4 << 20, transcendentals=rows * 4096 * 3
        ),
        name="attention",
    )(bounds, lo, q, kv)


def attention_back_kernel(
    bounds_ref, lo_ref, q_ref, kv_ref, out_ref, dout_ref, lse_ref, dq_ref, dkv_ref, acc_ref
):
    heads = q_ref.shape[1] // WIDTH
    queries = stack_heads(q_ref[...] * 0.125, True)
    douts = stack_heads(dout_ref[...], False)
    outs = stack_heads(out_ref[...], False)
    delta = jnp.sum(
        jnp.transpose(douts.astype(jnp.float32) * outs.astype(jnp.float32)), axis=0, keepdims=True
    )
    lse = lse_ref[:1, :]
    acc_ref[...] = jnp.zeros_like(acc_ref)
    base = LOOK * 1024 + pl.program_id(0) * BQ

    @pl.when(pl.program_id(0) == 0)
    def _():
        dkv_ref[...] = jnp.zeros_like(dkv_ref)

    def step(c, masked):
        start = pl.multiple_of(c * BK, BK)
        rows = kv_ref[pl.ds(start, BK), :]
        scores = nt(rows, queries)
        if masked:
            key = start + lax.broadcasted_iota(jnp.int32, (BK, BQ), 0)
            query = base + lax.broadcasted_iota(jnp.int32, (BK, BQ), 1)
            seen = (key >= lo_ref[...]) & (key <= query)
            scores = jnp.where(jnp.concatenate([seen] * heads, axis=1), scores, NEGATIVE)
        probs = jnp.exp(scores - lse)
        d_scores = (probs * (nt(rows, douts) - delta)).astype(jnp.bfloat16)
        dkv_ref[pl.ds(start, BK), :] += nn(d_scores, queries) + nn(
            probs.astype(jnp.bfloat16), douts
        )
        acc_ref[...] += tn(d_scores, rows)

    chunk_loops(bounds_ref, step)
    result = acc_ref[...] * 0.125
    dq_ref[...] = jnp.concatenate(
        [result[h * BQ : (h + 1) * BQ, :WIDTH] for h in range(heads)], axis=1
    ).astype(jnp.bfloat16)


def attention_back(bounds, lo_row, q, kv, out, dout, lse):
    rows, width = q.shape
    heads = width // WIDTH
    blocks = rows // BQ
    row_block = pl.BlockSpec((BQ, width), lambda b: (b, 0))
    return pl.pallas_call(
        attention_back_kernel,
        grid=(blocks,),
        in_specs=[
            pl.BlockSpec(memory_space=pltpu.SMEM),
            pl.BlockSpec((1, BQ), lambda b: (0, b)),
            row_block,
            pl.BlockSpec(memory_space=pltpu.VMEM),
            row_block,
            row_block,
            pl.BlockSpec((None, 8, heads * BQ), lambda b: (b, 0, 0)),
        ],
        out_specs=[
            row_block,
            pl.BlockSpec(kv.shape, lambda b: (0, 0)),
        ],
        out_shape=[
            jax.ShapeDtypeStruct((rows, width), jnp.bfloat16),
            jax.ShapeDtypeStruct(kv.shape, jnp.float32),
        ],
        scratch_shapes=[pltpu.VMEM((heads * BQ, 2 * WIDTH), jnp.float32)],
        compiler_params=pltpu.CompilerParams(vmem_limit_bytes=48 << 20),
        cost_estimate=pl.CostEstimate(
            flops=10 * rows * 4096 * width, bytes_accessed=8 << 20, transcendentals=rows * 4096 * 3
        ),
        name="attention_back",
    )(bounds, lo_row, q, kv, out, dout, lse)


def from_behind(x, by):
    peers = lax.axis_size("fsdp")
    pairs = [(i, i + by) for i in range(peers) if 0 <= i + by < peers]
    return lax.ppermute(x, "fsdp", pairs)


def gather_seq(x):
    return lax.all_gather(x, "seq", axis=0, tiled=True)


def scatter_seq(x):
    return lax.psum_scatter(x.astype(jnp.bfloat16), "seq", scatter_dimension=0, tiled=True)


def gather_fsdp(x, dim=0):
    return lax.all_gather(x, "fsdp", axis=dim, tiled=True)


def scatter_fsdp(x, dim=0):
    return lax.psum_scatter(x.astype(jnp.bfloat16), "fsdp", scatter_dimension=dim, tiled=True)


def head_rows_order(fsdp, seq):
    per = fsdp // seq
    return [(f * seq + s, ((f % per) * seq + s) * seq + f // per) for f in range(fsdp) for s in range(seq)]


def columns_by_owner(fsdp, seq, total):
    inner = total // (fsdp * seq)
    place = np.arange(total).reshape(fsdp, seq, inner).transpose(1, 0, 2).reshape(-1)
    one_hot = np.zeros((total, total), np.float32)
    one_hot[place, np.arange(total)] = 1
    return jnp.asarray(one_hot, jnp.bfloat16)


def scale_of(values):
    return lax.rsqrt(jnp.mean(values * values, axis=-1, keepdims=True) + EPS)


def rms_back(d_normed, unit, scale, gain):
    d_unit = d_normed * gain
    return scale * (d_unit - unit * jnp.mean(d_unit * unit, axis=-1, keepdims=True))


def on_device(
    tokens,
    gain_one,
    w_qkv,
    w_out,
    gain_two,
    w_router,
    w_gate,
    w_up,
    w_down,
    doc_starts,
    routes,
    cotangent,
):
    fsdp, seq = lax.axis_size("fsdp"), lax.axis_size("seq")
    group_index = lax.axis_index("fsdp")
    seq_index = lax.axis_index("seq")
    own, model = tokens.shape
    group_rows = own * seq
    experts, own_model, ff = w_gate.shape
    own_ff = ff // seq
    qkv_width = w_qkv.shape[1] // seq
    head_rows = w_out.shape[0] * fsdp
    order = columns_by_owner(fsdp, seq, ff)

    gate_up = nn(
        jnp.concatenate([w_gate, w_up], axis=0).reshape(2 * experts * own_model, ff), order
    ).astype(jnp.bfloat16)
    gate_up = gate_up.reshape(2 * experts, own_model, seq, own_ff)
    to_heads = jnp.concatenate(
        [
            w_qkv.reshape(own_model, seq, qkv_width),
            jnp.transpose(gate_up, (1, 2, 0, 3)).reshape(own_model, seq, 2 * experts * own_ff),
        ],
        axis=2,
    )
    by_heads = lax.all_to_all(to_heads, "seq", split_axis=1, concat_axis=0, tiled=True)
    by_heads = by_heads.reshape(own_model * seq, -1)
    qkv_weight = gather_fsdp(by_heads[:, :qkv_width])
    small = jnp.concatenate([gain_one[:, None], gain_two[:, None], w_router], axis=1)
    small = lax.all_gather(small, BOTH, axis=0, tiled=True)
    gain_first = small[:, 0].astype(jnp.float32)
    gain_second = small[:, 1].astype(jnp.float32)
    router_weight = small[:, 2:]
    out_weight = gather_fsdp(lax.ppermute(w_out, BOTH, head_rows_order(fsdp, seq)))
    expert_weight = gather_fsdp(by_heads[:, qkv_width:])
    gate_weight, up_weight = jnp.split(expert_weight, 2, axis=1)
    down_weight = gather_fsdp(w_down, 1).reshape(experts * own_ff, model)
    grad_all = gather_seq(cotangent)

    tokens_all = gather_seq(tokens).astype(jnp.float32)
    normed_one = (tokens_all * scale_of(tokens_all) * gain_first).astype(jnp.bfloat16)
    qkv = nn(normed_one, qkv_weight).astype(jnp.bfloat16)
    queries, keyval = qkv[:, : 3 * WIDTH], qkv[:, 3 * WIDTH :]
    window = jnp.concatenate([from_behind(keyval, LOOK - i) for i in range(LOOK)] + [keyval], axis=0)
    positions = group_index * group_rows + jnp.arange(group_rows, dtype=jnp.int32)
    begins = jnp.max(
        jnp.where(doc_starts[None, :] <= positions[:, None], doc_starts[None, :], 0), axis=1
    )
    lo = begins - (group_index - LOOK) * group_rows
    blocks = group_rows // BQ
    lo_blocks = lo.reshape(blocks, BQ)
    diag = (LOOK * group_rows + jnp.arange(blocks, dtype=jnp.int32) * BQ) // BK
    end = (LOOK * group_rows + (jnp.arange(blocks, dtype=jnp.int32) + 1) * BQ + BK - 1) // BK
    first = jnp.minimum(lo_blocks[:, 0] // BK, diag)
    full = jnp.minimum((lo_blocks[:, -1] + BK - 1) // BK, diag)
    bounds = jnp.stack([first, full, diag, end], axis=1)
    attended, lse = attention(bounds, lo[:, None], queries, window)
    branch = scatter_seq(nn(attended, out_weight))
    inputs = tokens.astype(jnp.float32)
    residual = inputs + branch.astype(jnp.float32)
    scale_second = scale_of(residual)
    unit_second = residual * scale_second
    normed_two = (unit_second * gain_second).astype(jnp.bfloat16)

    normed_all = gather_seq(normed_two)
    routes_all = gather_seq(routes)
    expert_ids = jnp.arange(experts, dtype=jnp.int32)
    chosen = jnp.sum((routes_all[:, :, None] == expert_ids).astype(jnp.float32), axis=1)
    probs_all = jax.nn.softmax(nn(normed_all, router_weight), axis=-1)
    share = jnp.repeat(probs_all * chosen, own_ff, axis=1)
    gate_pre = nn(normed_all, gate_weight)
    up_pre = nn(normed_all, up_weight)
    sigmoid = jax.nn.sigmoid(gate_pre)
    silu = gate_pre * sigmoid
    hidden = (silu * up_pre).astype(jnp.bfloat16)
    shared = (hidden.astype(jnp.float32) * share).astype(jnp.bfloat16)
    moe_out = scatter_seq(nn(shared, down_weight))
    output = (residual + moe_out.astype(jnp.float32)).astype(jnp.bfloat16)
    d_plain = nt(grad_all, down_weight)
    d_share = jnp.sum(
        (d_plain * hidden.astype(jnp.float32)).reshape(group_rows, experts, own_ff), axis=2
    )
    d_hidden = d_plain * share
    d_gate = (d_hidden * up_pre * sigmoid * (1.0 + gate_pre * (1.0 - sigmoid))).astype(jnp.bfloat16)
    d_up = (d_hidden * silu).astype(jnp.bfloat16)
    d_normed_two = nt(d_gate, gate_weight) + nt(d_up, up_weight)
    d_router = lax.psum_scatter(d_share, "seq", scatter_dimension=0, tiled=True)
    d_normed_two = scatter_seq(d_normed_two).astype(jnp.float32)
    grad_down = tn(shared, grad_all)
    grad_gate_up = jnp.concatenate([tn(normed_all, d_gate), tn(normed_all, d_up)], axis=1)

    chosen_own = jnp.sum((routes[:, :, None] == expert_ids).astype(jnp.float32), axis=1)
    probs_own = jax.nn.softmax(nn(normed_two, router_weight), axis=-1)
    d_router = d_router * chosen_own
    d_logits = (
        probs_own * (d_router - jnp.sum(probs_own * d_router, axis=-1, keepdims=True))
    ).astype(jnp.bfloat16)
    d_normed_two = d_normed_two + nt(d_logits, router_weight)
    grad_out = cotangent.astype(jnp.float32)
    d_resid = grad_out + rms_back(d_normed_two, unit_second, scale_second, gain_second)
    d_branch_all = gather_seq(d_resid.astype(jnp.bfloat16))

    grad_w_out = tn(attended, d_branch_all)
    d_attended = nt(d_branch_all, out_weight).astype(jnp.bfloat16)
    d_queries, d_window = attention_back(
        bounds, lo[None, :], queries, window, attended, d_attended, lse
    )
    d_keyval = d_window[LOOK * group_rows :]
    for distance in range(1, LOOK + 1):
        piece = d_window[(LOOK - distance) * group_rows : (LOOK - distance + 1) * group_rows]
        d_keyval = d_keyval + from_behind(piece.astype(jnp.bfloat16), -distance).astype(jnp.float32)
    d_qkv = jnp.concatenate([d_queries, d_keyval.astype(jnp.bfloat16)], axis=1)
    grad_w_qkv = tn(normed_one, d_qkv)
    d_normed_one = scatter_seq(nt(d_qkv, qkv_weight)).astype(jnp.float32)
    scale_first = scale_of(inputs)
    grad_input = d_resid + rms_back(d_normed_one, inputs * scale_first, scale_first, gain_first)

    shard_down = scatter_fsdp(
        grad_down.reshape(experts, own_ff, model), 1
    ).astype(jnp.float32)
    shard_out = lax.ppermute(
        scatter_fsdp(grad_w_out), BOTH, [(b, a) for a, b in head_rows_order(fsdp, seq)]
    ).astype(jnp.float32)
    grad_cols = jnp.concatenate([grad_w_qkv, grad_gate_up], axis=1)
    grad_cols = scatter_fsdp(grad_cols).reshape(seq, own_model, -1)
    grad_cols = lax.all_to_all(grad_cols, "seq", split_axis=0, concat_axis=0, tiled=True)
    shard_qkv = jnp.transpose(grad_cols[:, :, :qkv_width], (1, 0, 2)).reshape(own_model, -1)
    shard_qkv = shard_qkv.astype(jnp.float32)
    back = grad_cols[:, :, qkv_width:].reshape(seq, own_model, 2 * experts, own_ff)
    back = jnp.transpose(back, (2, 1, 0, 3)).reshape(2 * experts * own_model, ff)
    back = nt(back, order).reshape(2 * experts, own_model, ff)
    shard_gate, shard_up = back[:experts], back[experts:]
    grad_router = tn(normed_two, d_logits)
    shard_router = lax.psum_scatter(grad_router, BOTH, scatter_dimension=0, tiled=True)

    shard_gain_one = jnp.sum(w_qkv.astype(jnp.float32) * shard_qkv, axis=1)
    shard_gain_one = shard_gain_one / gain_one.astype(jnp.float32)
    shard_gain_two = jnp.sum(w_router.astype(jnp.float32) * shard_router, axis=1)
    shard_gain_two += jnp.sum(w_gate.astype(jnp.float32) * shard_gate, axis=(0, 2))
    shard_gain_two += jnp.sum(w_up.astype(jnp.float32) * shard_up, axis=(0, 2))
    shard_gain_two = shard_gain_two / gain_two.astype(jnp.float32)
    return (
        output,
        grad_input,
        shard_gain_one,
        shard_qkv,
        shard_out,
        shard_gain_two,
        shard_router,
        shard_gate,
        shard_up,
        shard_down,
    )


def solution(mesh):
    rows, vector = P(BOTH, None), P(BOTH)
    middle = P(None, BOTH, None)
    in_specs = (
        rows, vector, rows, rows, vector, rows, middle, middle, middle, P(), rows, rows,
    )
    out_specs = (rows, rows, vector, rows, rows, vector, rows, middle, middle, middle)
    return jax.shard_map(
        on_device, mesh=mesh, in_specs=in_specs, out_specs=out_specs, check_vma=False
    )
```

```python
import functools

import jax
import jax.numpy as jnp
import numpy as np
from jax import lax
from jax.experimental import pallas as pl
from jax.experimental.pallas import tpu as pltpu
from jax.sharding import PartitionSpec as P

WIDTH = 64
LOOK = 4
EXPERTS = 4
EPS = 1e-06
NEGATIVE = -1e30
BQ = 256
BK = 512
BOTH = ("fsdp", "seq")


def nt(a, b):
    return lax.dot_general(a, b, (((1,), (1,)), ((), ())), preferred_element_type=jnp.float32)


def tn(a, b):
    return lax.dot_general(a, b, (((0,), (0,)), ((), ())), preferred_element_type=jnp.float32)


def nn(a, b):
    return jnp.dot(a, b, preferred_element_type=jnp.float32)


def stack_heads(rows, low):
    heads = rows.shape[1] // WIDTH
    zero = jnp.zeros((rows.shape[0], WIDTH), rows.dtype)
    parts = []
    for h in range(heads):
        part = rows[:, h * WIDTH : (h + 1) * WIDTH]
        parts.append(jnp.concatenate([part, zero] if low else [zero, part], axis=1))
    return jnp.concatenate(parts, axis=0)


def chunk_loops(bounds_ref, step):
    b = pl.program_id(0)
    first, full, diag, end = (bounds_ref[b, i] for i in range(4))
    pl.loop(first, full)(lambda c: step(c, True))
    pl.loop(full, diag)(lambda c: step(c, False))
    pl.loop(diag, end)(lambda c: step(c, True))


def attention_kernel(bounds_ref, lo_ref, q_ref, kv_ref, out_ref, lse_ref, m_ref, l_ref, acc_ref):
    heads = q_ref.shape[1] // WIDTH
    queries = stack_heads(q_ref[...] * 0.125, True)
    m_ref[...] = jnp.full_like(m_ref, NEGATIVE)
    l_ref[...] = jnp.zeros_like(l_ref)
    acc_ref[...] = jnp.zeros_like(acc_ref)
    base = LOOK * 1024 + pl.program_id(0) * BQ

    def step(c, masked):
        start = pl.multiple_of(c * BK, BK)
        rows = kv_ref[pl.ds(start, BK), :]
        scores = nt(rows, queries)
        if masked:
            key = start + lax.broadcasted_iota(jnp.int32, (BK, BQ), 0)
            query = base + lax.broadcasted_iota(jnp.int32, (BK, BQ), 1)
            seen = (key >= lo_ref[...]) & (key <= query)
            scores = jnp.where(jnp.concatenate([seen] * heads, axis=1), scores, NEGATIVE)
        old = m_ref[...]
        new = jnp.maximum(old, jnp.max(scores, axis=0, keepdims=True))
        probs = jnp.exp(scores - new)
        fade = jnp.exp(old - new)
        m_ref[...] = new
        l_ref[...] = l_ref[...] * fade + jnp.sum(probs, axis=0, keepdims=True)
        acc_ref[...] = acc_ref[...] * fade + tn(rows, probs.astype(jnp.bfloat16))

    chunk_loops(bounds_ref, step)
    total = l_ref[...]
    result = jnp.transpose(acc_ref[...] / total)
    out_ref[...] = jnp.concatenate(
        [result[h * BQ : (h + 1) * BQ, WIDTH:] for h in range(heads)], axis=1
    ).astype(jnp.bfloat16)
    lse_ref[...] = jnp.broadcast_to(m_ref[...] + jnp.log(total), lse_ref.shape)


def attention(bounds, lo, q, kv):
    rows, width = q.shape
    heads = width // WIDTH
    blocks = rows // BQ
    return pl.pallas_call(
        attention_kernel,
        grid=(blocks,),
        in_specs=[
            pl.BlockSpec(memory_space=pltpu.SMEM),
            pl.BlockSpec((1, BQ), lambda b: (0, b)),
            pl.BlockSpec((BQ, width), lambda b: (b, 0)),
            pl.BlockSpec(memory_space=pltpu.VMEM),
        ],
        out_specs=[
            pl.BlockSpec((BQ, width), lambda b: (b, 0)),
            pl.BlockSpec((None, 8, heads * BQ), lambda b: (b, 0, 0)),
        ],
        out_shape=[
            jax.ShapeDtypeStruct((rows, width), jnp.bfloat16),
            jax.ShapeDtypeStruct((blocks, 8, heads * BQ), jnp.float32),
        ],
        scratch_shapes=[
            pltpu.VMEM((1, heads * BQ), jnp.float32),
            pltpu.VMEM((1, heads * BQ), jnp.float32),
            pltpu.VMEM((2 * WIDTH, heads * BQ), jnp.float32),
        ],
        compiler_params=pltpu.CompilerParams(vmem_limit_bytes=48 << 20),
        cost_estimate=pl.CostEstimate(
            flops=4 * rows * 4096 * width, bytes_accessed=4 << 20, transcendentals=rows * 4096 * 3
        ),
        name="attention",
    )(bounds, lo, q, kv)


def attention_back_kernel(
    bounds_ref, lo_ref, q_ref, kv_ref, out_ref, dout_ref, lse_ref, dq_ref, dkv_ref, acc_ref
):
    heads = q_ref.shape[1] // WIDTH
    queries = stack_heads(q_ref[...] * 0.125, True)
    douts = stack_heads(dout_ref[...], False)
    outs = stack_heads(out_ref[...], False)
    delta = jnp.sum(
        jnp.transpose(douts.astype(jnp.float32) * outs.astype(jnp.float32)), axis=0, keepdims=True
    )
    lse = lse_ref[:1, :]
    acc_ref[...] = jnp.zeros_like(acc_ref)
    base = LOOK * 1024 + pl.program_id(0) * BQ

    @pl.when(pl.program_id(0) == 0)
    def _():
        dkv_ref[...] = jnp.zeros_like(dkv_ref)

    def step(c, masked):
        start = pl.multiple_of(c * BK, BK)
        rows = kv_ref[pl.ds(start, BK), :]
        scores = nt(rows, queries)
        if masked:
            key = start + lax.broadcasted_iota(jnp.int32, (BK, BQ), 0)
            query = base + lax.broadcasted_iota(jnp.int32, (BK, BQ), 1)
            seen = (key >= lo_ref[...]) & (key <= query)
            scores = jnp.where(jnp.concatenate([seen] * heads, axis=1), scores, NEGATIVE)
        probs = jnp.exp(scores - lse)
        d_scores = (probs * (nt(rows, douts) - delta)).astype(jnp.bfloat16)
        dkv_ref[pl.ds(start, BK), :] += nn(d_scores, queries) + nn(
            probs.astype(jnp.bfloat16), douts
        )
        acc_ref[...] += tn(d_scores, rows)

    chunk_loops(bounds_ref, step)
    result = acc_ref[...] * 0.125
    dq_ref[...] = jnp.concatenate(
        [result[h * BQ : (h + 1) * BQ, :WIDTH] for h in range(heads)], axis=1
    ).astype(jnp.bfloat16)


def attention_back(bounds, lo_row, q, kv, out, dout, lse):
    rows, width = q.shape
    heads = width // WIDTH
    blocks = rows // BQ
    row_block = pl.BlockSpec((BQ, width), lambda b: (b, 0))
    return pl.pallas_call(
        attention_back_kernel,
        grid=(blocks,),
        in_specs=[
            pl.BlockSpec(memory_space=pltpu.SMEM),
            pl.BlockSpec((1, BQ), lambda b: (0, b)),
            row_block,
            pl.BlockSpec(memory_space=pltpu.VMEM),
            row_block,
            row_block,
            pl.BlockSpec((None, 8, heads * BQ), lambda b: (b, 0, 0)),
        ],
        out_specs=[
            row_block,
            pl.BlockSpec(kv.shape, lambda b: (0, 0)),
        ],
        out_shape=[
            jax.ShapeDtypeStruct((rows, width), jnp.bfloat16),
            jax.ShapeDtypeStruct(kv.shape, jnp.float32),
        ],
        scratch_shapes=[pltpu.VMEM((heads * BQ, 2 * WIDTH), jnp.float32)],
        compiler_params=pltpu.CompilerParams(vmem_limit_bytes=48 << 20),
        cost_estimate=pl.CostEstimate(
            flops=10 * rows * 4096 * width, bytes_accessed=8 << 20, transcendentals=rows * 4096 * 3
        ),
        name="attention_back",
    )(bounds, lo_row, q, kv, out, dout, lse)


RING = 4
MESH = pl.DeviceIdType.MESH
VMEM = pl.BlockSpec(memory_space=pltpu.VMEM)


def at_seq(index):
    return {"seq": index}


def at_fsdp(index):
    return {"fsdp": index}


def ring_places(s):
    x, y = lax.div(s, RING), lax.rem(s, RING)

    def place(dx, dy):
        return lax.rem(x + dx, 2) * RING + lax.rem(y + dy, RING)

    return {
        "up": place(0, 1),
        "down": place(0, 3),
        "far": place(0, 2),
        "over": place(1, 0),
        "over_up": place(1, 1),
        "over_down": place(1, 3),
        "over_far": place(1, 2),
    }


def greet(targets):
    barrier = pltpu.get_barrier_semaphore()
    for target in targets:
        pl.semaphore_signal(barrier, inc=1, device_id=target, device_id_type=MESH)
    pl.semaphore_wait(barrier, len(targets))


def send(src, dst, sems, index, target):
    copy = pltpu.make_async_remote_copy(
        src_ref=src,
        dst_ref=dst,
        send_sem=sems[0].at[index],
        recv_sem=sems[1].at[index],
        device_id=target,
        device_id_type=MESH,
    )
    copy.start()
    return copy


def ring_gather(out, s, sems, base):
    p = ring_places(s)
    half = out.shape[1] // 2
    top, bottom = pl.ds(0, half), pl.ds(half, half)
    up, down, over = at_seq(p["up"]), at_seq(p["down"]), at_seq(p["over"])
    own_up = send(out.at[s], out.at[s], sems, base, up)
    own_down = send(out.at[s], out.at[s], sems, base + 1, down)
    own_over = send(out.at[s], out.at[s], sems, base + 2, over)
    own_up.wait_recv()
    block = out.at[p["down"], top]
    far_up = send(block, block, sems, base + 3, up)
    own_down.wait_recv()
    block = out.at[p["up"], bottom]
    far_down = send(block, block, sems, base + 4, down)
    own_over.wait_recv()
    block = out.at[p["over"]]
    over_up = send(block, block, sems, base + 5, up)
    over_down = send(block, block, sems, base + 6, down)
    far_up.wait_recv()
    far_down.wait_recv()
    block = out.at[p["far"]]
    far_over = send(block, block, sems, base + 7, over)
    over_up.wait_recv()
    over_down.wait_recv()
    far_over.wait_recv()
    for copy in (own_up, own_down, own_over, far_up, far_down, over_up, over_down, far_over):
        copy.wait_send()


def ring_scatter(partial, tx, rx, rx_half, s, sems, base):
    p = ring_places(s)
    half = rx_half.shape[1]
    up, down, over = at_seq(p["up"]), at_seq(p["down"]), at_seq(p["over"])

    def put(slot, value):
        tx[slot] = value.astype(tx.dtype)
        return tx.at[slot]

    def wide(ref):
        return ref[...].astype(jnp.float32)

    first = send(put(0, partial(p["over_far"])), rx.at[0], sems, base, over)
    second = send(put(1, partial(p["over_up"])), rx.at[1], sems, base + 1, up)
    third = send(put(2, partial(p["over_down"])), rx.at[2], sems, base + 2, down)
    far = partial(p["far"])
    first.wait_recv()
    put(3, far + wide(rx.at[0]))
    to_down = send(tx.at[3, pl.ds(0, half)], rx_half.at[0], sems, base + 3, down)
    to_up = send(tx.at[3, pl.ds(half, half)], rx_half.at[1], sems, base + 4, up)
    across = partial(p["over"])
    second.wait_recv()
    third.wait_recv()
    fourth = send(
        put(4, across + wide(rx.at[1]) + wide(rx.at[2])), rx.at[3], sems, base + 5, over
    )
    value = partial(p["down"])
    to_down.wait_recv()
    tx[5, half:] = value[half:].astype(tx.dtype)
    tx[5, :half] = (value[:half] + wide(rx_half.at[0])).astype(tx.dtype)
    fifth = send(tx.at[5], rx.at[4], sems, base + 6, down)
    value = partial(p["up"])
    to_up.wait_recv()
    tx[6, :half] = value[:half].astype(tx.dtype)
    tx[6, half:] = (value[half:] + wide(rx_half.at[1])).astype(tx.dtype)
    sixth = send(tx.at[6], rx.at[5], sems, base + 7, up)
    own = partial(s)
    fourth.wait_recv()
    fifth.wait_recv()
    sixth.wait_recv()
    total = own + wide(rx.at[3]) + wide(rx.at[4]) + wide(rx.at[5])
    for copy in (first, second, third, to_down, to_up, fourth, fifth, sixth):
        copy.wait_send()
    return total


def ring_buffers(rows, width):
    return [
        pltpu.VMEM((7, rows, width), jnp.bfloat16),
        pltpu.VMEM((6, rows, width), jnp.bfloat16),
        pltpu.VMEM((2, rows // 2, width), jnp.bfloat16),
    ]


def sem_pair(count):
    return [pltpu.SemaphoreType.DMA((count,)), pltpu.SemaphoreType.DMA((count,))]


def others(me, count):
    return [lax.rem(me + k, count) for k in range(1, count)]


def exchange(blocks, into, me, peers, at, sems, base):
    return [
        send(blocks.at[p], into.at[me], sems, base + k, at(p)) for k, p in enumerate(peers)
    ]


def spread(block, into, me, peers, at, sems, base):
    return [send(block, into.at[me], sems, base + k, at(p)) for k, p in enumerate(peers)]


def compact(blocks, rows):
    total = blocks.shape[0]
    shape = (total // 16 * rows, total)
    source = lax.broadcasted_iota(jnp.int32, shape, 1)
    place = lax.shift_right_logical(source, 4) * rows + (source & 15)
    keep = (place == lax.broadcasted_iota(jnp.int32, shape, 0)) & ((source & 15) < rows)
    return nn(keep.astype(jnp.bfloat16), blocks).astype(jnp.bfloat16)


def expand(rows_in, rows):
    shape = (rows_in.shape[0] // rows * 16, rows_in.shape[0])
    target = lax.broadcasted_iota(jnp.int32, shape, 0)
    place = lax.shift_right_logical(target, 4) * rows + (target & 15)
    keep = (place == lax.broadcasted_iota(jnp.int32, shape, 1)) & ((target & 15) < rows)
    return nn(keep.astype(jnp.bfloat16), rows_in).astype(jnp.bfloat16)


def scale_of(values):
    return lax.rsqrt(jnp.mean(values * values, axis=-1, keepdims=True) + EPS)


def rms_back(d_normed, unit, scale, gain):
    d_unit = d_normed * gain
    return scale * (d_unit - unit * jnp.mean(d_unit * unit, axis=-1, keepdims=True))


SMALL = 3 * WIDTH
KEYS = 4 * WIDTH


def start_kernel(
    tokens_ref, columns_ref, experts_ref, chosen_ref,
    normed_ref, q_ref, kv_ref, weight_ref, small_ref, rows_ref, chosen_out_ref,
    all_ref, columns_in, experts_in, send_sems, recv_sems,
):
    s, g = lax.axis_index("seq"), lax.axis_index("fsdp")
    peers, groups = others(s, 8), others(g, 16)
    sems = (send_sems, recv_sems)
    greet([at_seq(p) for p in peers] + [at_fsdp(p) for p in groups])
    copies = exchange(columns_ref, columns_in, s, peers, at_seq, sems, 8)
    more = spread(chosen_ref, chosen_out_ref, s, peers, at_seq, sems, 37)
    more += exchange(experts_ref, experts_in, s, peers, at_seq, sems, 15)
    all_ref[s] = tokens_ref[...]
    columns_in[s] = columns_ref[s]
    experts_in[s] = experts_ref[s]
    chosen_out_ref[s] = chosen_ref[...]
    for copy in copies:
        copy.wait_recv()
    mine = pl.ds(pl.multiple_of(g * 96, 32), 96)
    weight_ref[mine, :] = compact(columns_in[...].reshape(128, columns_in.shape[2]), 12)
    wide = [
        send(weight_ref.at[mine], weight_ref.at[mine], sems, 22 + k, at_fsdp(p))
        for k, p in enumerate(groups)
    ]
    ring_gather(all_ref, s, sems, 0)
    for copy in more:
        copy.wait_recv()
    rows_ref[...] = compact(experts_in[...].reshape(128, experts_in.shape[2]), 12)
    for copy in wide:
        copy.wait_recv()
    pick = lax.broadcasted_iota(jnp.int32, (8, 2 * WIDTH), 0) + (SMALL - 2 * WIDTH)
    pick = (pick == lax.broadcasted_iota(jnp.int32, (8, 2 * WIDTH), 1)).astype(jnp.bfloat16)
    small_ref[...] = nt(pick, weight_ref[:, 2 * WIDTH : 4 * WIDTH])
    gain = small_ref[0:1, :]

    @pl.loop(0, 8)
    def _(block):
        place = pl.ds(pl.multiple_of(block * 128, 128), 128)
        values = all_ref[block].astype(jnp.float32)
        normed = (values * scale_of(values) * gain).astype(jnp.bfloat16)
        normed_ref[place, :] = normed
        result = nn(normed, weight_ref[...]).astype(jnp.bfloat16)
        q_ref[place, :] = result[:, :SMALL]
        kv_ref[place, :] = result[:, KEYS:]

    for copy in copies + more + wide:
        copy.wait_send()


def start(tokens, columns, experts, chosen):
    own, model = tokens.shape
    rows = 8 * own
    width = columns.shape[2]
    bf16, f32 = jnp.bfloat16, jnp.float32
    return pl.pallas_call(
        start_kernel,
        in_specs=[VMEM] * 4,
        out_specs=[VMEM] * 7,
        out_shape=[
            jax.ShapeDtypeStruct((rows, model), bf16),
            jax.ShapeDtypeStruct((rows, SMALL), bf16),
            jax.ShapeDtypeStruct((rows, width - KEYS), bf16),
            jax.ShapeDtypeStruct((model, width), bf16),
            jax.ShapeDtypeStruct((8, model), f32),
            jax.ShapeDtypeStruct((96, experts.shape[2]), bf16),
            jax.ShapeDtypeStruct((8,) + chosen.shape, f32),
        ],
        scratch_shapes=[
            pltpu.VMEM((8, own, model), bf16),
            pltpu.VMEM(columns.shape, bf16),
            pltpu.VMEM(experts.shape, bf16),
            *sem_pair(44),
        ],
        compiler_params=pltpu.CompilerParams(
            collective_id=1, has_side_effects=True, vmem_limit_bytes=48 << 20
        ),
        name="start",
    )(tokens, columns, experts, chosen)


def window_kernel(kv_ref, out_ref, send_sems, recv_sems):
    g = lax.axis_index("fsdp")
    core = lax.rem(g, 2)
    after, before, partner = lax.rem(g + 2, 16), lax.rem(g + 14, 16), g + 1 - 2 * core
    sems = (send_sems, recv_sems)
    greet([at_fsdp(after), at_fsdp(before), at_fsdp(partner)])
    out_ref[4] = kv_ref[...]
    first = send(kv_ref, out_ref.at[2], sems, 0, at_fsdp(after))
    first.wait_recv()
    second = send(out_ref.at[2], out_ref.at[0], sems, 1, at_fsdp(after))
    third = send(out_ref.at[4 - 2 * core], out_ref.at[3], sems, 2, at_fsdp(partner))
    second.wait_recv()
    fourth = send(out_ref.at[2 - 2 * core], out_ref.at[1], sems, 3, at_fsdp(partner))
    third.wait_recv()
    fourth.wait_recv()
    for copy in (first, second, third, fourth):
        copy.wait_send()


def window_of(kv):
    return pl.pallas_call(
        window_kernel,
        in_specs=[VMEM],
        out_specs=VMEM,
        out_shape=jax.ShapeDtypeStruct((LOOK + 1,) + kv.shape, kv.dtype),
        scratch_shapes=sem_pair(4),
        compiler_params=pltpu.CompilerParams(
            collective_id=2, has_side_effects=True, vmem_limit_bytes=48 << 20
        ),
        name="window",
    )(kv)


def window_back_kernel(d_ref, out_ref, tx, rx, send_sems, recv_sems):
    g = lax.axis_index("fsdp")
    core = lax.rem(g, 2)
    after, before, partner = lax.rem(g + 2, 16), lax.rem(g + 14, 16), g + 1 - 2 * core
    sems = (send_sems, recv_sems)
    odd = core.astype(jnp.float32)
    even = 1.0 - odd
    greet([at_fsdp(after), at_fsdp(before), at_fsdp(partner)])

    def wide(slot):
        return rx[slot].astype(jnp.float32)

    tx[1] = d_ref[1].astype(jnp.bfloat16)
    one = send(tx.at[1], rx.at[1], sems, 1, at_fsdp(partner))
    tx[2] = d_ref[3].astype(jnp.bfloat16)
    two = send(tx.at[2], rx.at[2], sems, 2, at_fsdp(partner))
    one.wait_recv()
    tx[0] = (d_ref[0] + odd * wide(1)).astype(jnp.bfloat16)
    zero = send(tx.at[0], rx.at[0], sems, 0, at_fsdp(before))
    two.wait_recv()
    zero.wait_recv()
    tx[3] = (d_ref[2] + wide(0) + odd * wide(2) + even * wide(1)).astype(jnp.bfloat16)
    three = send(tx.at[3], rx.at[3], sems, 3, at_fsdp(before))
    three.wait_recv()
    out_ref[...] = (d_ref[4] + wide(3) + even * wide(2)).astype(jnp.bfloat16)
    for copy in (zero, one, two, three):
        copy.wait_send()


def window_back(d_window):
    shape = d_window.shape[1:]
    return pl.pallas_call(
        window_back_kernel,
        in_specs=[VMEM],
        out_specs=VMEM,
        out_shape=jax.ShapeDtypeStruct(shape, jnp.bfloat16),
        scratch_shapes=[
            pltpu.VMEM((4,) + shape, jnp.bfloat16),
            pltpu.VMEM((4,) + shape, jnp.bfloat16),
            *sem_pair(4),
        ],
        compiler_params=pltpu.CompilerParams(
            collective_id=3, has_side_effects=True, vmem_limit_bytes=48 << 20
        ),
        name="window_back",
    )(d_window)


def middle_kernel(
    attended_ref, weight_ref, tokens_ref, small_ref, resid_ref, normed_ref,
    tx, rx, rx_half, send_sems, recv_sems,
):
    s = lax.axis_index("seq")
    p = ring_places(s)
    sems = (send_sems, recv_sems)
    greet([at_seq(p["up"]), at_seq(p["down"]), at_seq(p["over"])])

    def partial(place):
        rows = pl.ds(pl.multiple_of(place * 128, 128), 128)
        return nn(attended_ref[rows, :], weight_ref[...])

    branch = ring_scatter(partial, tx, rx, rx_half, s, sems, 0)
    resid = tokens_ref[...].astype(jnp.float32) + branch
    resid_ref[...] = resid
    normed_ref[s] = (resid * scale_of(resid) * small_ref[1:2, :]).astype(jnp.bfloat16)
    ring_gather(normed_ref, s, sems, 8)


def middle(attended, weight, tokens, small):
    own, model = tokens.shape
    return pl.pallas_call(
        middle_kernel,
        in_specs=[VMEM] * 4,
        out_specs=[VMEM] * 2,
        out_shape=[
            jax.ShapeDtypeStruct((own, model), jnp.float32),
            jax.ShapeDtypeStruct((8, own, model), jnp.bfloat16),
        ],
        scratch_shapes=[*ring_buffers(own, model), *sem_pair(16)],
        compiler_params=pltpu.CompilerParams(
            collective_id=4, has_side_effects=True, vmem_limit_bytes=48 << 20
        ),
        name="middle",
    )(attended, weight, tokens, small)


def turn_kernel(
    d_ref, weight_ref, share_ref, probs_ref, chosen_ref, resid_ref, small_ref, cotangent_ref,
    d_resid_ref, branch_ref, logits_ref,
    share_in, tx, rx, rx_half, send_sems, recv_sems,
):
    s = lax.axis_index("seq")
    peers = others(s, 8)
    sems = (send_sems, recv_sems)
    greet([at_seq(p) for p in peers])
    shares = exchange(share_ref, share_in, s, peers, at_seq, sems, 16)
    share_in[s] = share_ref[s]

    def partial(place):
        rows = pl.ds(pl.multiple_of(place * 128, 128), 128)
        return nt(d_ref[rows, :], weight_ref[...])

    d_normed = ring_scatter(partial, tx, rx, rx_half, s, sems, 0)
    for copy in shares:
        copy.wait_recv()
    d_router = jnp.sum(share_in[...], axis=0) * chosen_ref[...]
    probs = probs_ref[...]
    d_logits = probs * (d_router - jnp.sum(probs * d_router, axis=0, keepdims=True))
    d_logits = d_logits.astype(jnp.bfloat16)
    logits_ref[s] = d_logits.astype(jnp.float32)
    spreads = spread(logits_ref.at[s], logits_ref, s, peers, at_seq, sems, 23)
    router = small_ref[...].astype(jnp.bfloat16)
    padded = jnp.concatenate([jnp.zeros((2, 128), jnp.bfloat16), d_logits[:6]], axis=0)
    d_normed = d_normed + tn(padded, router)
    resid = resid_ref[...]
    scale = scale_of(resid)
    d_resid = cotangent_ref[...].astype(jnp.float32) + rms_back(
        d_normed, resid * scale, scale, small_ref[1:2, :]
    )
    d_resid_ref[...] = d_resid
    branch_ref[s] = d_resid.astype(jnp.bfloat16)
    ring_gather(branch_ref, s, sems, 8)
    for copy in spreads:
        copy.wait_recv()
    for copy in shares + spreads:
        copy.wait_send()


def turn(d_gate_up, weight, d_share, probs, chosen, resid, small, cotangent):
    own, model = resid.shape
    return pl.pallas_call(
        turn_kernel,
        in_specs=[VMEM] * 8,
        out_specs=[VMEM] * 3,
        out_shape=[
            jax.ShapeDtypeStruct((own, model), jnp.float32),
            jax.ShapeDtypeStruct((8, own, model), jnp.bfloat16),
            jax.ShapeDtypeStruct(d_share.shape, jnp.float32),
        ],
        scratch_shapes=[
            pltpu.VMEM(d_share.shape, jnp.float32),
            *ring_buffers(own, model),
            *sem_pair(30),
        ],
        compiler_params=pltpu.CompilerParams(
            collective_id=5, has_side_effects=True, vmem_limit_bytes=48 << 20
        ),
        name="turn",
    )(d_gate_up, weight, d_share, probs, chosen, resid, small, cotangent)


def finish_kernel(
    d_ref, weight_ref, grads_ref, experts_ref, d_resid_ref, tokens_ref, small_ref,
    grad_input_ref, columns_out, experts_out,
    grads_in, columns_tx, tx, rx, rx_half, send_sems, recv_sems,
):
    s, g = lax.axis_index("seq"), lax.axis_index("fsdp")
    peers, groups = others(s, 8), others(g, 16)
    sems = (send_sems, recv_sems)
    greet([at_seq(p) for p in peers] + [at_fsdp(p) for p in groups])
    wide = exchange(grads_ref, grads_in, g, groups, at_fsdp, sems, 8)
    grads_in[g] = grads_ref[g]

    def partial(place):
        rows = pl.ds(pl.multiple_of(place * 128, 128), 128)
        return nt(d_ref[rows, :], weight_ref[...])

    d_normed = ring_scatter(partial, tx, rx, rx_half, s, sems, 0)
    for copy in wide:
        copy.wait_recv()
    total = jnp.sum(grads_in[...].astype(jnp.float32), axis=0).astype(jnp.bfloat16)
    columns_tx[...] = expand(total, 12).reshape(columns_tx.shape)
    copies = exchange(columns_tx, columns_out, s, peers, at_seq, sems, 23)
    copies += exchange(experts_ref, experts_out, s, peers, at_seq, sems, 30)
    columns_out[s] = columns_tx[s]
    experts_out[s] = experts_ref[s]
    values = tokens_ref[...].astype(jnp.float32)
    scale = scale_of(values)
    grad_input_ref[...] = d_resid_ref[...] + rms_back(
        d_normed, values * scale, scale, small_ref[0:1, :]
    )
    for copy in copies:
        copy.wait_recv()
    for copy in wide + copies:
        copy.wait_send()


def finish(d_qkv, weight, grads, experts, d_resid, tokens, small):
    own, model = tokens.shape
    columns = jax.ShapeDtypeStruct((8, 16, grads.shape[2]), jnp.bfloat16)
    return pl.pallas_call(
        finish_kernel,
        in_specs=[VMEM] * 7,
        out_specs=[VMEM] * 3,
        out_shape=[
            jax.ShapeDtypeStruct((own, model), jnp.float32),
            columns,
            jax.ShapeDtypeStruct(experts.shape, jnp.bfloat16),
        ],
        scratch_shapes=[
            pltpu.VMEM(grads.shape, jnp.bfloat16),
            pltpu.VMEM(columns.shape, jnp.bfloat16),
            *ring_buffers(own, model),
            *sem_pair(37),
        ],
        compiler_params=pltpu.CompilerParams(
            collective_id=6, has_side_effects=True, vmem_limit_bytes=48 << 20
        ),
        name="finish",
    )(d_qkv, weight, grads, experts, d_resid, tokens, small)


def gather_seq(x):
    return lax.all_gather(x, "seq", axis=0, tiled=True)


def scatter_seq(x):
    return lax.psum_scatter(x.astype(jnp.bfloat16), "seq", scatter_dimension=0, tiled=True)


def gather_fsdp(x, dim=0):
    return lax.all_gather(x, "fsdp", axis=dim, tiled=True)


def scatter_fsdp(x, dim=0):
    return lax.psum_scatter(x.astype(jnp.bfloat16), "fsdp", scatter_dimension=dim, tiled=True)


def head_rows_order(fsdp, seq):
    per = fsdp // seq
    return [
        (f * seq + s, ((f % per) * seq + s) * seq + f // per)
        for f in range(fsdp)
        for s in range(seq)
    ]


def columns_by_owner(fsdp, seq, total):
    inner = total // (fsdp * seq)
    place = np.arange(total).reshape(fsdp, seq, inner).transpose(1, 0, 2).reshape(-1)
    one_hot = np.zeros((total, total), np.float32)
    one_hot[place, np.arange(total)] = 1
    return jnp.asarray(one_hot, jnp.bfloat16)


def pad_rows(x, axis):
    pads = [(0, 0)] * x.ndim
    pads[axis] = (0, 16 - x.shape[axis])
    return jnp.pad(x, pads)


def on_device(
    tokens,
    gain_one,
    w_qkv,
    w_out,
    gain_two,
    w_router,
    w_gate,
    w_up,
    w_down,
    doc_starts,
    routes,
    cotangent,
):
    fsdp, seq = lax.axis_size("fsdp"), lax.axis_size("seq")
    group_index = lax.axis_index("fsdp")
    own, model = tokens.shape
    group_rows = own * seq
    experts, own_model, ff = w_gate.shape
    own_ff = ff // seq
    order = columns_by_owner(fsdp, seq, ff)
    bf16, f32 = jnp.bfloat16, jnp.float32

    grad_all = gather_seq(cotangent)
    down_weight = gather_fsdp(w_down, 1).reshape(experts * own_ff, model)
    out_weight = gather_fsdp(pad_rows(lax.ppermute(w_out, BOTH, head_rows_order(fsdp, seq)), 0)[None])
    out_weight = out_weight[:, :own_model].reshape(fsdp * own_model, model)
    gate_up = nn(
        jnp.concatenate([w_gate, w_up], axis=0).reshape(2 * experts * own_model, ff), order
    ).astype(bf16)
    gate_up = gate_up.reshape(2 * experts, own_model, seq, own_ff)
    gate_up = jnp.transpose(gate_up, (2, 1, 0, 3)).reshape(seq, own_model, 2 * experts * own_ff)
    qkv_parts = jnp.transpose(w_qkv.reshape(own_model, seq, 5 * WIDTH), (1, 0, 2))
    small = jnp.concatenate([gain_one[:, None], gain_two[:, None], w_router], axis=1)
    small = jnp.pad(small, ((0, 0), (0, WIDTH - small.shape[1])))
    columns = jnp.concatenate(
        [
            qkv_parts[:, :, :SMALL],
            jnp.broadcast_to(small[None], (seq,) + small.shape),
            qkv_parts[:, :, SMALL:],
        ],
        axis=2,
    )
    expert_ids = jnp.arange(8, dtype=jnp.int32)
    chosen_own = jnp.sum((routes[None, :, :] == expert_ids[:, None, None]).astype(f32), axis=2)
    normed_one, queries, keyval, weight, small, rows, chosen = start(
        tokens, pad_rows(columns, 1), pad_rows(gate_up, 1), chosen_own
    )
    expert_weight = gather_fsdp(rows)

    window = window_of(keyval).reshape((LOOK + 1) * group_rows, 2 * WIDTH)
    positions = group_index * group_rows + jnp.arange(group_rows, dtype=jnp.int32)
    begins = jnp.max(
        jnp.where(doc_starts[:, None] <= positions[None, :], doc_starts[:, None], 0), axis=0
    )
    lo = begins - (group_index - LOOK) * group_rows
    blocks = group_rows // BQ
    lo_blocks = lo.reshape(blocks, BQ)
    diag = (LOOK * group_rows + jnp.arange(blocks, dtype=jnp.int32) * BQ) // BK
    end = (LOOK * group_rows + (jnp.arange(blocks, dtype=jnp.int32) + 1) * BQ + BK - 1) // BK
    first = jnp.minimum(lo_blocks[:, 0] // BK, diag)
    full = jnp.minimum((lo_blocks[:, -1] + BK - 1) // BK, diag)
    bounds = jnp.stack([first, full, diag, end], axis=1)
    attended, lse = attention(bounds, lo[None, :], queries, window)
    residual, normed_all = middle(attended, out_weight, tokens, small)
    normed_two = lax.dynamic_index_in_dim(normed_all, lax.axis_index("seq"), 0, False)
    normed_all = normed_all.reshape(group_rows, model)

    router = small[2 : 2 + experts].astype(bf16)
    logits = nt(router, normed_all)
    probs = jax.nn.softmax(logits, axis=0)
    chosen_all = jnp.transpose(chosen, (1, 0, 2)).reshape(8, group_rows)[:experts]
    share = jnp.repeat(jnp.transpose(probs * chosen_all), own_ff, axis=1)
    gate_weight, up_weight = jnp.split(expert_weight, 2, axis=1)
    gate_pre = nn(normed_all, gate_weight)
    up_pre = nn(normed_all, up_weight)
    sigmoid = jax.nn.sigmoid(gate_pre)
    silu = gate_pre * sigmoid
    hidden = (silu * up_pre).astype(bf16)
    shared = (hidden.astype(f32) * share).astype(bf16)
    moe_out = scatter_seq(nn(shared, down_weight))
    output = (residual + moe_out.astype(f32)).astype(bf16)
    d_plain = nt(grad_all, down_weight)
    d_share = jnp.sum((d_plain * hidden.astype(f32)).reshape(group_rows, experts, own_ff), axis=2)
    d_share = jnp.transpose(d_share.reshape(seq, own, experts), (0, 2, 1))
    d_share = jnp.pad(d_share, ((0, 0), (0, 8 - experts), (0, 0)))
    d_hidden = d_plain * share
    d_gate = (d_hidden * up_pre * sigmoid * (1.0 + gate_pre * (1.0 - sigmoid))).astype(bf16)
    d_up = (d_hidden * silu).astype(bf16)
    d_gate_up = jnp.concatenate([d_gate, d_up], axis=1)
    probs_own = jnp.transpose(probs.reshape(experts, seq, own), (1, 0, 2))
    probs_own = lax.dynamic_index_in_dim(probs_own, lax.axis_index("seq"), 0, False)
    probs_own = jnp.pad(probs_own, ((0, 8 - experts), (0, 0)))
    d_resid, d_branch_all, d_logits = turn(
        d_gate_up, expert_weight, d_share, probs_own, chosen_own, residual, small, cotangent
    )
    d_branch_all = d_branch_all.reshape(group_rows, model)
    grad_down = tn(shared, grad_all)
    grad_gate_up = tn(normed_all, d_gate_up)
    part_down = scatter_fsdp(grad_down.reshape(experts, own_ff, model), 1)
    part_gate_up = scatter_fsdp(grad_gate_up)

    d_attended = nt(d_branch_all, out_weight).astype(bf16)
    grad_w_out = tn(attended, d_branch_all)
    part_out = scatter_fsdp(pad_rows(grad_w_out.reshape(fsdp, own_model, model), 1))
    d_queries, d_window = attention_back(
        bounds, lo[None, :], queries, window, attended, d_attended, lse
    )
    d_keyval = window_back(d_window.reshape(LOOK + 1, group_rows, 2 * WIDTH))
    d_qkv = jnp.concatenate(
        [d_queries, jnp.zeros((group_rows, WIDTH), bf16), d_keyval], axis=1
    )
    d_logits = jnp.transpose(d_logits, (1, 0, 2)).reshape(8, group_rows)[:experts]
    grad_router = nn(d_logits.astype(bf16), normed_all)
    grads = tn(normed_one, d_qkv)
    grads = jnp.concatenate(
        [
            grads[:, : SMALL + 2],
            jnp.transpose(grad_router),
            grads[:, SMALL + 2 + experts :],
        ],
        axis=1,
    )
    grads = grads.astype(bf16).reshape(fsdp, model // fsdp, -1)
    grad_input, columns, back = finish(
        d_qkv,
        weight,
        grads,
        pad_rows(part_gate_up.reshape(seq, own_model, -1), 1),
        d_resid,
        tokens,
        small,
    )

    shard_down = part_down.astype(f32)
    shard_out = lax.ppermute(
        part_out[0, :own_model], BOTH, [(b, a) for a, b in head_rows_order(fsdp, seq)]
    ).astype(f32)
    columns = columns[:, :own_model].astype(f32)
    shard_qkv = jnp.concatenate([columns[:, :, :SMALL], columns[:, :, KEYS:]], axis=2)
    shard_qkv = jnp.transpose(shard_qkv, (1, 0, 2)).reshape(own_model, -1)
    shard_router = columns[0, :, SMALL + 2 : SMALL + 2 + experts]
    back = back[:, :own_model].reshape(seq, own_model, 2 * experts, own_ff)
    back = jnp.transpose(back, (2, 1, 0, 3)).reshape(2 * experts * own_model, ff)
    back = nt(back, order).reshape(2 * experts, own_model, ff)
    shard_gate, shard_up = back[:experts], back[experts:]

    shard_gain_one = jnp.sum(w_qkv.astype(f32) * shard_qkv, axis=1)
    shard_gain_one = shard_gain_one / gain_one.astype(f32)
    shard_gain_two = jnp.sum(w_router.astype(f32) * shard_router, axis=1)
    shard_gain_two += jnp.sum(w_gate.astype(f32) * shard_gate, axis=(0, 2))
    shard_gain_two += jnp.sum(w_up.astype(f32) * shard_up, axis=(0, 2))
    shard_gain_two = shard_gain_two / gain_two.astype(f32)
    return (
        output,
        grad_input,
        shard_gain_one,
        shard_qkv,
        shard_out,
        shard_gain_two,
        shard_router,
        shard_gate,
        shard_up,
        shard_down,
    )


def solution(mesh):
    rows, vector = P(BOTH, None), P(BOTH)
    middle = P(None, BOTH, None)
    in_specs = (
        rows, vector, rows, rows, vector, rows, middle, middle, middle, P(), rows, rows,
    )
    out_specs = (rows, rows, vector, rows, rows, vector, rows, middle, middle, middle)
    return jax.shard_map(
        on_device, mesh=mesh, in_specs=in_specs, out_specs=out_specs, check_vma=False
    )
```

```python
import functools

import jax
import jax.numpy as jnp
import numpy as np
from jax import lax
from jax.experimental import pallas as pl
from jax.experimental.pallas import tpu as pltpu
from jax.sharding import PartitionSpec as P

WIDTH = 64
LOOK = 4
EXPERTS = 4
EPS = 1e-06
NEGATIVE = -1e30
BQ = 256
BK = 512
BOTH = ("fsdp", "seq")


def nt(a, b):
    return lax.dot_general(a, b, (((1,), (1,)), ((), ())), preferred_element_type=jnp.float32)


def tn(a, b):
    return lax.dot_general(a, b, (((0,), (0,)), ((), ())), preferred_element_type=jnp.float32)


def nn(a, b):
    return jnp.dot(a, b, preferred_element_type=jnp.float32)


def stack_heads(rows, low):
    heads = rows.shape[1] // WIDTH
    zero = jnp.zeros((rows.shape[0], WIDTH), rows.dtype)
    parts = []
    for h in range(heads):
        part = rows[:, h * WIDTH : (h + 1) * WIDTH]
        parts.append(jnp.concatenate([part, zero] if low else [zero, part], axis=1))
    return jnp.concatenate(parts, axis=0)


def chunk_loops(bounds_ref, step):
    b = pl.program_id(0)
    first, full, diag, end = (bounds_ref[b, i] for i in range(4))
    pl.loop(first, full)(lambda c: step(c, True))
    pl.loop(full, diag)(lambda c: step(c, False))
    pl.loop(diag, end)(lambda c: step(c, True))


def attention_kernel(bounds_ref, lo_ref, q_ref, kv_ref, out_ref, lse_ref, m_ref, l_ref, acc_ref):
    heads = q_ref.shape[1] // WIDTH
    queries = stack_heads(q_ref[...] * 0.125, True)
    m_ref[...] = jnp.full_like(m_ref, NEGATIVE)
    l_ref[...] = jnp.zeros_like(l_ref)
    acc_ref[...] = jnp.zeros_like(acc_ref)
    base = LOOK * 1024 + pl.program_id(0) * BQ

    def step(c, masked):
        start = pl.multiple_of(c * BK, BK)
        rows = kv_ref[pl.ds(start, BK), :]
        scores = nt(rows, queries)
        if masked:
            key = start + lax.broadcasted_iota(jnp.int32, (BK, BQ), 0)
            query = base + lax.broadcasted_iota(jnp.int32, (BK, BQ), 1)
            seen = (key >= lo_ref[...]) & (key <= query)
            scores = jnp.where(jnp.concatenate([seen] * heads, axis=1), scores, NEGATIVE)
        old = m_ref[...]
        new = jnp.maximum(old, jnp.max(scores, axis=0, keepdims=True))
        probs = jnp.exp(scores - new)
        fade = jnp.exp(old - new)
        m_ref[...] = new
        l_ref[...] = l_ref[...] * fade + jnp.sum(probs, axis=0, keepdims=True)
        acc_ref[...] = acc_ref[...] * fade + tn(rows, probs.astype(jnp.bfloat16))

    chunk_loops(bounds_ref, step)
    total = l_ref[...]
    result = jnp.transpose(acc_ref[...] / total)
    out_ref[...] = jnp.concatenate(
        [result[h * BQ : (h + 1) * BQ, WIDTH:] for h in range(heads)], axis=1
    ).astype(jnp.bfloat16)
    lse_ref[...] = jnp.broadcast_to(m_ref[...] + jnp.log(total), lse_ref.shape)


def attention(bounds, lo, q, kv):
    rows, width = q.shape
    heads = width // WIDTH
    blocks = rows // BQ
    return pl.pallas_call(
        attention_kernel,
        grid=(blocks,),
        in_specs=[
            pl.BlockSpec(memory_space=pltpu.SMEM),
            pl.BlockSpec((1, BQ), lambda b: (0, b)),
            pl.BlockSpec((BQ, width), lambda b: (b, 0)),
            pl.BlockSpec(memory_space=pltpu.VMEM),
        ],
        out_specs=[
            pl.BlockSpec((BQ, width), lambda b: (b, 0)),
            pl.BlockSpec((None, 8, heads * BQ), lambda b: (b, 0, 0)),
        ],
        out_shape=[
            jax.ShapeDtypeStruct((rows, width), jnp.bfloat16),
            jax.ShapeDtypeStruct((blocks, 8, heads * BQ), jnp.float32),
        ],
        scratch_shapes=[
            pltpu.VMEM((1, heads * BQ), jnp.float32),
            pltpu.VMEM((1, heads * BQ), jnp.float32),
            pltpu.VMEM((2 * WIDTH, heads * BQ), jnp.float32),
        ],
        compiler_params=pltpu.CompilerParams(vmem_limit_bytes=48 << 20),
        cost_estimate=pl.CostEstimate(
            flops=4 * rows * 4096 * width, bytes_accessed=4 << 20, transcendentals=rows * 4096 * 3
        ),
        name="attention",
    )(bounds, lo, q, kv)


def attention_back_kernel(
    bounds_ref, lo_ref, q_ref, kv_ref, out_ref, dout_ref, lse_ref, dq_ref, dkv_ref, acc_ref
):
    heads = q_ref.shape[1] // WIDTH
    queries = stack_heads(q_ref[...] * 0.125, True)
    douts = stack_heads(dout_ref[...], False)
    outs = stack_heads(out_ref[...], False)
    delta = jnp.sum(
        jnp.transpose(douts.astype(jnp.float32) * outs.astype(jnp.float32)), axis=0, keepdims=True
    )
    lse = lse_ref[:1, :]
    acc_ref[...] = jnp.zeros_like(acc_ref)
    base = LOOK * 1024 + pl.program_id(0) * BQ

    @pl.when(pl.program_id(0) == 0)
    def _():
        dkv_ref[...] = jnp.zeros_like(dkv_ref)

    def step(c, masked):
        start = pl.multiple_of(c * BK, BK)
        rows = kv_ref[pl.ds(start, BK), :]
        scores = nt(rows, queries)
        if masked:
            key = start + lax.broadcasted_iota(jnp.int32, (BK, BQ), 0)
            query = base + lax.broadcasted_iota(jnp.int32, (BK, BQ), 1)
            seen = (key >= lo_ref[...]) & (key <= query)
            scores = jnp.where(jnp.concatenate([seen] * heads, axis=1), scores, NEGATIVE)
        probs = jnp.exp(scores - lse)
        d_scores = (probs * (nt(rows, douts) - delta)).astype(jnp.bfloat16)
        dkv_ref[pl.ds(start, BK), :] += nn(d_scores, queries) + nn(
            probs.astype(jnp.bfloat16), douts
        )
        acc_ref[...] += tn(d_scores, rows)

    chunk_loops(bounds_ref, step)
    result = acc_ref[...] * 0.125
    dq_ref[...] = jnp.concatenate(
        [result[h * BQ : (h + 1) * BQ, :WIDTH] for h in range(heads)], axis=1
    ).astype(jnp.bfloat16)


def attention_back(bounds, lo_row, q, kv, out, dout, lse):
    rows, width = q.shape
    heads = width // WIDTH
    blocks = rows // BQ
    row_block = pl.BlockSpec((BQ, width), lambda b: (b, 0))
    return pl.pallas_call(
        attention_back_kernel,
        grid=(blocks,),
        in_specs=[
            pl.BlockSpec(memory_space=pltpu.SMEM),
            pl.BlockSpec((1, BQ), lambda b: (0, b)),
            row_block,
            pl.BlockSpec(memory_space=pltpu.VMEM),
            row_block,
            row_block,
            pl.BlockSpec((None, 8, heads * BQ), lambda b: (b, 0, 0)),
        ],
        out_specs=[
            row_block,
            pl.BlockSpec(kv.shape, lambda b: (0, 0)),
        ],
        out_shape=[
            jax.ShapeDtypeStruct((rows, width), jnp.bfloat16),
            jax.ShapeDtypeStruct(kv.shape, jnp.float32),
        ],
        scratch_shapes=[pltpu.VMEM((heads * BQ, 2 * WIDTH), jnp.float32)],
        compiler_params=pltpu.CompilerParams(vmem_limit_bytes=48 << 20),
        cost_estimate=pl.CostEstimate(
            flops=10 * rows * 4096 * width, bytes_accessed=8 << 20, transcendentals=rows * 4096 * 3
        ),
        name="attention_back",
    )(bounds, lo_row, q, kv, out, dout, lse)


RING = 4
MESH = pl.DeviceIdType.MESH
VMEM = pl.BlockSpec(memory_space=pltpu.VMEM)


def at_seq(index):
    return {"seq": index}


def at_fsdp(index):
    return {"fsdp": index}


def ring_places(s):
    x, y = lax.div(s, RING), lax.rem(s, RING)

    def place(dx, dy):
        return lax.rem(x + dx, 2) * RING + lax.rem(y + dy, RING)

    return {
        "up": place(0, 1),
        "down": place(0, 3),
        "far": place(0, 2),
        "over": place(1, 0),
        "over_up": place(1, 1),
        "over_down": place(1, 3),
        "over_far": place(1, 2),
    }


def greet(targets):
    barrier = pltpu.get_barrier_semaphore()
    for target in targets:
        pl.semaphore_signal(barrier, inc=1, device_id=target, device_id_type=MESH)
    pl.semaphore_wait(barrier, len(targets))


def send(src, dst, sems, index, target):
    copy = pltpu.make_async_remote_copy(
        src_ref=src,
        dst_ref=dst,
        send_sem=sems[0].at[index],
        recv_sem=sems[1].at[index],
        device_id=target,
        device_id_type=MESH,
    )
    copy.start()
    return copy


class Task:
    def __init__(self, steps):
        self.steps, self.done, self.value = steps, False, None

    def step(self):
        if not self.done:
            try:
                next(self.steps)
            except StopIteration as end:
                self.done, self.value = True, end.value


def run(task, *beside):
    while not task.done:
        task.step()
        for other in beside:
            other.step()
    return task.value


def run_all(*tasks):
    while not all(task.done for task in tasks):
        for task in tasks:
            task.step()


def ring_gather(out, s, sems, base):
    p = ring_places(s)
    half = out.shape[1] // 2
    top, bottom = pl.ds(0, half), pl.ds(half, half)
    up, down, over = at_seq(p["up"]), at_seq(p["down"]), at_seq(p["over"])
    own_up = send(out.at[s], out.at[s], sems, base, up)
    own_down = send(out.at[s], out.at[s], sems, base + 1, down)
    own_over = send(out.at[s], out.at[s], sems, base + 2, over)
    yield
    own_up.wait_recv()
    block = out.at[p["down"], top]
    far_up = send(block, block, sems, base + 3, up)
    own_down.wait_recv()
    block = out.at[p["up"], bottom]
    far_down = send(block, block, sems, base + 4, down)
    yield
    own_over.wait_recv()
    block = out.at[p["over"]]
    over_up = send(block, block, sems, base + 5, up)
    over_down = send(block, block, sems, base + 6, down)
    yield
    far_up.wait_recv()
    far_down.wait_recv()
    block = out.at[p["far"]]
    far_over = send(block, block, sems, base + 7, over)
    yield
    over_up.wait_recv()
    over_down.wait_recv()
    yield
    far_over.wait_recv()
    for copy in (own_up, own_down, own_over, far_up, far_down, over_up, over_down, far_over):
        copy.wait_send()


def ring_scatter(partial, tx, rx, rx_half, s, sems, base):
    p = ring_places(s)
    half = rx_half.shape[1]
    up, down, over = at_seq(p["up"]), at_seq(p["down"]), at_seq(p["over"])

    def put(slot, value):
        tx[slot] = value.astype(tx.dtype)
        return tx.at[slot]

    def wide(ref):
        return ref[...].astype(jnp.float32)

    first = send(put(0, partial(p["over_far"])), rx.at[0], sems, base, over)
    second = send(put(1, partial(p["over_up"])), rx.at[1], sems, base + 1, up)
    third = send(put(2, partial(p["over_down"])), rx.at[2], sems, base + 2, down)
    far = partial(p["far"])
    yield
    first.wait_recv()
    put(3, far + wide(rx.at[0]))
    to_down = send(tx.at[3, pl.ds(0, half)], rx_half.at[0], sems, base + 3, down)
    to_up = send(tx.at[3, pl.ds(half, half)], rx_half.at[1], sems, base + 4, up)
    across = partial(p["over"])
    yield
    second.wait_recv()
    third.wait_recv()
    fourth = send(
        put(4, across + wide(rx.at[1]) + wide(rx.at[2])), rx.at[3], sems, base + 5, over
    )
    value = partial(p["down"])
    yield
    to_down.wait_recv()
    tx[5, half:] = value[half:].astype(tx.dtype)
    tx[5, :half] = (value[:half] + wide(rx_half.at[0])).astype(tx.dtype)
    fifth = send(tx.at[5], rx.at[4], sems, base + 6, down)
    value = partial(p["up"])
    to_up.wait_recv()
    tx[6, :half] = value[:half].astype(tx.dtype)
    tx[6, half:] = (value[half:] + wide(rx_half.at[1])).astype(tx.dtype)
    sixth = send(tx.at[6], rx.at[5], sems, base + 7, up)
    own = partial(s)
    yield
    fourth.wait_recv()
    fifth.wait_recv()
    sixth.wait_recv()
    total = own + wide(rx.at[3]) + wide(rx.at[4]) + wide(rx.at[5])
    for copy in (first, second, third, to_down, to_up, fourth, fifth, sixth):
        copy.wait_send()
    return total


def ring_buffers(rows, width):
    return [
        pltpu.VMEM((7, rows, width), jnp.bfloat16),
        pltpu.VMEM((6, rows, width), jnp.bfloat16),
        pltpu.VMEM((2, rows // 2, width), jnp.bfloat16),
    ]


def fsdp_place(g):
    x, z, core = lax.div(g, 8), lax.rem(lax.div(g, 2), RING), lax.rem(g, 2)

    def place(dx, dz, dcore):
        return (
            lax.rem(x + dx, 2) * 8 + lax.rem(z + dz, RING) * 2 + lax.rem(core + dcore, 2)
        )

    return place


def fsdp_neighbours(g):
    place = fsdp_place(g)
    return [at_fsdp(place(*d)) for d in ((1, 0, 0), (0, 1, 0), (0, 3, 0), (0, 0, 1))]


def part_of(ref, rows, cut):
    def view(index, half=None):
        first, count = {None: (0, rows), "top": (0, cut), "bottom": (cut, rows - cut)}[half]
        return ref.at[pl.ds(pl.multiple_of(index * rows + first, 16), count)]

    return view


def fsdp_gather(ref, rows, cut, g, sems, base):
    view, place = part_of(ref, rows, cut), fsdp_place(g)
    over, up, down, pal = fsdp_neighbours(g)
    copies = []

    def go(index, half, sem, target):
        copies.append(send(view(index, half), view(index, half), sems, base + sem, target))
        return copies[-1]

    me = place(0, 0, 0)
    to_over = go(me, None, 16, over)
    to_up, to_down = go(me, None, 0, up), go(me, None, 1, down)
    pals = [go(me, None, 8, pal)]
    yield
    to_over.wait_recv()
    side = place(1, 0, 0)
    side_up, side_down = go(side, None, 2, up), go(side, None, 3, down)
    pals.append(go(side, None, 9, pal))
    yield
    to_up.wait_recv()
    far_up = go(place(0, 3, 0), "top", 4, up)
    pals.append(go(place(0, 3, 0), None, 10, pal))
    to_down.wait_recv()
    far_down = go(place(0, 1, 0), "bottom", 5, down) if cut < rows else None
    pals.append(go(place(0, 1, 0), None, 11, pal))
    yield
    side_up.wait_recv()
    side_far_up = go(place(1, 3, 0), "top", 6, up)
    pals.append(go(place(1, 3, 0), None, 12, pal))
    side_down.wait_recv()
    side_far_down = go(place(1, 1, 0), "bottom", 7, down) if cut < rows else None
    pals.append(go(place(1, 1, 0), None, 13, pal))
    yield
    far_up.wait_recv()
    if far_down is not None:
        far_down.wait_recv()
    pals.append(go(place(0, 2, 0), None, 14, pal))
    yield
    side_far_up.wait_recv()
    if side_far_down is not None:
        side_far_down.wait_recv()
    pals.append(go(place(1, 2, 0), None, 15, pal))
    yield
    for copy in pals:
        copy.wait_recv()
    for copy in copies:
        copy.wait_send()


def fsdp_buffers(rows, cut, width):
    return [
        pltpu.VMEM((8 * rows, width), jnp.bfloat16),
        pltpu.VMEM((2, cut, width), jnp.bfloat16),
        pltpu.VMEM((2, max(rows - cut, 16), width), jnp.bfloat16),
        pltpu.VMEM((5, rows, width), jnp.bfloat16),
    ]


def fsdp_scatter(ref, rows, cut, buffers, g, sems, base):
    pair, tops, bottoms, full = buffers
    view, place = part_of(ref, rows, cut), fsdp_place(g)
    over, up, down, pal = fsdp_neighbours(g)
    copies = []

    def go(src, dst, sem, target):
        copies.append(send(src, dst, sems, base + sem, target))
        return copies[-1]

    def wide(part):
        return part[...].astype(jnp.float32)

    def slot(index):
        return pair.at[pl.ds(pl.multiple_of(lax.div(index, 2) * rows, 16), rows)]

    order = [(1, 2), (0, 2), (1, 3), (1, 1), (0, 3), (0, 1), (1, 0), (0, 0)]
    pals = {}
    for k, (dx, dz) in enumerate(order):
        index = place(dx, dz, 1)
        pals[dx, dz] = go(view(index), slot(index), k, pal)
    yield

    def paired(dx, dz):
        pals[dx, dz].wait_recv()
        return wide(view(place(dx, dz, 0))) + wide(slot(place(dx, dz, 0)))

    halves = {}
    for k, dx in enumerate((1, 0)):
        index = place(dx, 2, 0)
        value = paired(dx, 2)
        view(index)[...] = value.astype(jnp.bfloat16)
        halves[dx, "top"] = go(view(index, "top"), tops.at[dx], 8 + 2 * k, down)
        if cut < rows:
            halves[dx, "bottom"] = go(view(index, "bottom"), bottoms.at[dx], 9 + 2 * k, up)
    yield
    fulls = {}
    for k, dx in enumerate((1, 0)):
        index = place(dx, 3, 0)
        value = paired(dx, 3)
        halves[dx, "top"].wait_recv()
        view(index, "top")[...] = (value[:cut] + wide(tops.at[dx])).astype(jnp.bfloat16)
        if cut < rows:
            view(index, "bottom")[...] = value[cut:].astype(jnp.bfloat16)
        fulls[dx, "down"] = go(view(index), full.at[2 * dx], 12 + 2 * k, down)
        index = place(dx, 1, 0)
        value = paired(dx, 1)
        if cut < rows:
            halves[dx, "bottom"].wait_recv()
            view(index, "top")[...] = value[:cut].astype(jnp.bfloat16)
            view(index, "bottom")[...] = (value[cut:] + wide(bottoms.at[dx])).astype(jnp.bfloat16)
        else:
            view(index)[...] = value.astype(jnp.bfloat16)
        fulls[dx, "up"] = go(view(index), full.at[2 * dx + 1], 13 + 2 * k, up)
        yield
    index = place(1, 0, 0)
    value = paired(1, 0)
    fulls[1, "down"].wait_recv()
    fulls[1, "up"].wait_recv()
    view(index)[...] = (value + wide(full.at[2]) + wide(full.at[3])).astype(jnp.bfloat16)
    last = go(view(index), full.at[4], 16, over)
    value = paired(0, 0)
    yield
    fulls[0, "down"].wait_recv()
    fulls[0, "up"].wait_recv()
    value = value + wide(full.at[0]) + wide(full.at[1])
    yield
    last.wait_recv()
    value = value + wide(full.at[4])
    for copy in copies:
        copy.wait_send()
    return value


def sem_pair(count):
    return [pltpu.SemaphoreType.DMA((count,)), pltpu.SemaphoreType.DMA((count,))]


def others(me, count):
    return [lax.rem(me + k, count) for k in range(1, count)]


def exchange(blocks, into, me, peers, at, sems, base):
    return [
        send(blocks.at[p], into.at[me], sems, base + k, at(p)) for k, p in enumerate(peers)
    ]


def spread(block, into, me, peers, at, sems, base):
    return [send(block, into.at[me], sems, base + k, at(p)) for k, p in enumerate(peers)]


def swap_rows(src, dst, sems, index, target, alone):
    away = pltpu.make_async_remote_copy(
        src_ref=src,
        dst_ref=dst,
        send_sem=sems[0].at[index],
        recv_sem=sems[1].at[index],
        device_id=target,
        device_id_type=MESH,
    )
    here = pltpu.make_async_copy(src, dst, sems[0].at[index])
    pl.when(jnp.logical_not(alone))(away.start)
    pl.when(alone)(here.start)

    def wait():
        pl.when(jnp.logical_not(alone))(away.wait)
        pl.when(alone)(here.wait)

    return wait


def head_holder(g, s):
    return {"fsdp": lax.rem(g, 2) * 8 + s, "seq": lax.div(g, 2)}


def head_owner(g, s):
    return {"fsdp": 2 * s + lax.div(g, 8), "seq": lax.rem(g, 8)}


def greet_all(targets, pair, alone):
    barrier = pltpu.get_barrier_semaphore()
    for target in targets:
        pl.semaphore_signal(barrier, inc=1, device_id=target, device_id_type=MESH)

    @pl.when(jnp.logical_not(alone))
    def _():
        for target in pair:
            pl.semaphore_signal(barrier, inc=1, device_id=target, device_id_type=MESH)

    pl.semaphore_wait(barrier, len(targets) + jnp.where(alone, 0, 2))


def compact(blocks, rows):
    total = blocks.shape[0]
    shape = (total // 16 * rows, total)
    source = lax.broadcasted_iota(jnp.int32, shape, 1)
    place = lax.shift_right_logical(source, 4) * rows + (source & 15)
    keep = (place == lax.broadcasted_iota(jnp.int32, shape, 0)) & ((source & 15) < rows)
    return nn(keep.astype(jnp.bfloat16), blocks).astype(jnp.bfloat16)


def expand(rows_in, rows):
    shape = (rows_in.shape[0] // rows * 16, rows_in.shape[0])
    target = lax.broadcasted_iota(jnp.int32, shape, 0)
    place = lax.shift_right_logical(target, 4) * rows + (target & 15)
    keep = (place == lax.broadcasted_iota(jnp.int32, shape, 1)) & ((target & 15) < rows)
    return nn(keep.astype(jnp.bfloat16), rows_in).astype(jnp.bfloat16)


def unit_order(row_axis):
    mixed = lax.broadcasted_iota(jnp.int32, (512, 512), 1 - row_axis)
    plain = lax.broadcasted_iota(jnp.int32, (512, 512), row_axis)
    f = lax.shift_right_logical(mixed, 5)
    e = lax.shift_right_logical(mixed, 3) & 3
    return (e * 128 + f * 8 + (mixed & 7) == plain).astype(jnp.bfloat16)


def scale_of(values):
    return lax.rsqrt(jnp.mean(values * values, axis=-1, keepdims=True) + EPS)


def rms_back(d_normed, unit, scale, gain):
    d_unit = d_normed * gain
    return scale * (d_unit - unit * jnp.mean(d_unit * unit, axis=-1, keepdims=True))


def rows_at(place, count=128):
    return pl.ds(pl.multiple_of(place * count, count), count)


def kernel_params(collective_id):
    return pltpu.CompilerParams(
        collective_id=collective_id, has_side_effects=True, vmem_limit_bytes=52 << 20
    )


def array(shape, dtype=jnp.bfloat16):
    return jax.ShapeDtypeStruct(shape, dtype)


SMALL = 3 * WIDTH
KEYS = 4 * WIDTH


def start_kernel(
    tokens_ref, columns_ref, experts_ref, down_ref, wout_ref, chosen_ref,
    normed_ref, q_ref, kv_ref, weight_ref, small_ref, gate_up_ref, down_all_ref, wout_all_ref,
    chosen_out_ref,
    all_ref, columns_in, experts_in, mixed, send_sems, recv_sems,
):
    s, g = lax.axis_index("seq"), lax.axis_index("fsdp")
    peers = others(s, 8)
    sems = (send_sems, recv_sems)
    holder, owner = head_holder(g, s), head_owner(g, s)
    alone = (holder["fsdp"] == g) & (holder["seq"] == s)
    greet_all([at_seq(p) for p in peers] + fsdp_neighbours(g), (holder, owner), alone)
    copies = exchange(columns_ref, columns_in, s, peers, at_seq, sems, 8)
    wait_rows = swap_rows(
        wout_ref,
        mixed.at[pl.ds(pl.multiple_of(holder["fsdp"] * 48 + 32, 16), 16)],
        sems, 22, holder, alone,
    )
    copies += exchange(experts_ref, experts_in, s, peers, at_seq, sems, 15)
    all_ref[s] = tokens_ref[...]
    tokens_in = Task(ring_gather(all_ref, s, sems, 0))
    tokens_in.step()
    chosen_copies = spread(chosen_ref, chosen_out_ref, s, peers, at_seq, sems, 23)
    columns_in[s] = columns_ref[s]
    experts_in[s] = experts_ref[s]
    chosen_out_ref[s] = chosen_ref[...]
    mixed[pl.ds(pl.multiple_of(g * 48, 16), 32), :] = down_ref[...]
    for copy in copies[:7]:
        copy.wait_recv()
    weight_ref[rows_at(g, 96), :] = compact(columns_in[...].reshape(128, columns_in.shape[2]), 12)
    columns_gather = Task(fsdp_gather(weight_ref, 96, 48, g, sems, 30))
    columns_gather.step()
    for copy in copies[7:]:
        copy.wait_recv()
    gate_up_ref[rows_at(g, 96), :] = compact(experts_in[...].reshape(128, experts_in.shape[2]), 12)
    gate_up_gather = Task(fsdp_gather(gate_up_ref, 96, 48, g, sems, 47))
    gate_up_gather.step()
    wait_rows()
    mixed_gather = Task(fsdp_gather(mixed, 48, 32, g, sems, 64))
    run(columns_gather, tokens_in, gate_up_gather, mixed_gather)
    pick = lax.broadcasted_iota(jnp.int32, (8, 2 * WIDTH), 0) + (SMALL - 2 * WIDTH)
    pick = (pick == lax.broadcasted_iota(jnp.int32, (8, 2 * WIDTH), 1)).astype(jnp.bfloat16)
    small_ref[...] = nt(pick, weight_ref[:, 2 * WIDTH : 4 * WIDTH])
    gain = small_ref[0:1, :]
    run_all(tokens_in, gate_up_gather, mixed_gather)

    @pl.loop(0, 8)
    def _(block):
        values = all_ref[block].astype(jnp.float32)
        normed = (values * scale_of(values) * gain).astype(jnp.bfloat16)
        normed_ref[rows_at(block), :] = normed
        result = nn(normed, weight_ref[...]).astype(jnp.bfloat16)
        q_ref[rows_at(block), :] = result[:, :SMALL]
        kv_ref[rows_at(block), :] = result[:, KEYS:]

    parts = mixed[...].reshape(16, 48, mixed.shape[1])
    down_all_ref[...] = nn(unit_order(0), parts[:, :32].reshape(512, -1)).astype(jnp.bfloat16)
    wout_all_ref[...] = compact(parts[:, 32:].reshape(256, -1), 12)
    for copy in chosen_copies:
        copy.wait_recv()
    for copy in copies + chosen_copies:
        copy.wait_send()


def start(tokens, columns, experts, down, wout, chosen):
    own, model = tokens.shape
    rows = 8 * own
    width = columns.shape[2]
    return pl.pallas_call(
        start_kernel,
        in_specs=[VMEM] * 6,
        out_specs=[VMEM] * 9,
        out_shape=[
            array((rows, model)),
            array((rows, SMALL)),
            array((rows, width - KEYS)),
            array((model, width)),
            array((8, model), jnp.float32),
            array((model, experts.shape[2])),
            array((512, model)),
            array((192, model)),
            array((8,) + chosen.shape, jnp.float32),
        ],
        scratch_shapes=[
            pltpu.VMEM((8, own, model), jnp.bfloat16),
            pltpu.VMEM(columns.shape, jnp.bfloat16),
            pltpu.VMEM(experts.shape, jnp.bfloat16),
            pltpu.VMEM((16 * 48, model), jnp.bfloat16),
            *sem_pair(81),
        ],
        compiler_params=kernel_params(1),
        name="start",
    )(tokens, columns, experts, down, wout, chosen)


def window_steps(kv_ref, out_ref, g, sems, base):
    core = lax.rem(g, 2)
    after, partner = at_fsdp(lax.rem(g + 2, 16)), at_fsdp(g + 1 - 2 * core)
    out_ref[4] = kv_ref[...]
    first = send(kv_ref, out_ref.at[2], sems, base, after)
    yield
    first.wait_recv()
    second = send(out_ref.at[2], out_ref.at[0], sems, base + 1, after)
    third = send(out_ref.at[4 - 2 * core], out_ref.at[3], sems, base + 2, partner)
    yield
    second.wait_recv()
    fourth = send(out_ref.at[2 - 2 * core], out_ref.at[1], sems, base + 3, partner)
    yield
    third.wait_recv()
    fourth.wait_recv()
    for copy in (first, second, third, fourth):
        copy.wait_send()


def window_greeting(g):
    core = lax.rem(g, 2)
    return [at_fsdp(i) for i in (lax.rem(g + 2, 16), lax.rem(g + 14, 16), g + 1 - 2 * core)]


def ring_greeting(s):
    p = ring_places(s)
    return [at_seq(p["up"]), at_seq(p["down"]), at_seq(p["over"])]


def window_kernel(kv_ref, cotangent_ref, out_ref, all_ref, send_sems, recv_sems):
    s, g = lax.axis_index("seq"), lax.axis_index("fsdp")
    sems = (send_sems, recv_sems)
    greet(window_greeting(g) + ring_greeting(s))
    window = Task(window_steps(kv_ref, out_ref, g, sems, 0))
    window.step()
    all_ref[s] = cotangent_ref[...]
    run_all(window, Task(ring_gather(all_ref, s, sems, 4)))


def window_of(kv, cotangent):
    return pl.pallas_call(
        window_kernel,
        in_specs=[VMEM] * 2,
        out_specs=[VMEM] * 2,
        out_shape=[array((LOOK + 1,) + kv.shape), array((8,) + cotangent.shape)],
        scratch_shapes=sem_pair(12),
        compiler_params=kernel_params(2),
        name="window",
    )(kv, cotangent)


def window_back_steps(d_ref, out_ref, tx, rx, g, sems, base):
    core = lax.rem(g, 2)
    before, partner = at_fsdp(lax.rem(g + 14, 16)), at_fsdp(g + 1 - 2 * core)
    odd = core.astype(jnp.float32)
    even = 1.0 - odd

    def wide(slot):
        return rx[slot].astype(jnp.float32)

    tx[1] = d_ref[1].astype(jnp.bfloat16)
    one = send(tx.at[1], rx.at[1], sems, base + 1, partner)
    tx[2] = d_ref[3].astype(jnp.bfloat16)
    two = send(tx.at[2], rx.at[2], sems, base + 2, partner)
    yield
    one.wait_recv()
    tx[0] = (d_ref[0] + odd * wide(1)).astype(jnp.bfloat16)
    zero = send(tx.at[0], rx.at[0], sems, base, before)
    yield
    two.wait_recv()
    zero.wait_recv()
    tx[3] = (d_ref[2] + wide(0) + odd * wide(2) + even * wide(1)).astype(jnp.bfloat16)
    three = send(tx.at[3], rx.at[3], sems, base + 3, before)
    yield
    three.wait_recv()
    out_ref[...] = (d_ref[4] + wide(3) + even * wide(2)).astype(jnp.bfloat16)
    for copy in (zero, one, two, three):
        copy.wait_send()


def window_back_kernel(
    d_ref, shared_ref, down_ref, resid_ref, out_ref, output_ref,
    wtx, wrx, tx, rx, rx_half, send_sems, recv_sems,
):
    s, g = lax.axis_index("seq"), lax.axis_index("fsdp")
    sems = (send_sems, recv_sems)
    greet(window_greeting(g) + ring_greeting(s))
    window = Task(window_back_steps(d_ref, out_ref, wtx, wrx, g, sems, 8))
    window.step()

    def partial(place):
        return nn(shared_ref[rows_at(place), :], down_ref[...])

    total = run(Task(ring_scatter(partial, tx, rx, rx_half, s, sems, 0)), window)
    output_ref[...] = (resid_ref[...] + total).astype(jnp.bfloat16)
    run(window)


def window_back(d_window, shared, down, resid):
    shape = d_window.shape[1:]
    own, model = resid.shape
    return pl.pallas_call(
        window_back_kernel,
        in_specs=[VMEM] * 4,
        out_specs=[VMEM] * 2,
        out_shape=[array(shape), array((own, model))],
        scratch_shapes=[
            pltpu.VMEM((4,) + shape, jnp.bfloat16),
            pltpu.VMEM((4,) + shape, jnp.bfloat16),
            *ring_buffers(own, model),
            *sem_pair(12),
        ],
        compiler_params=kernel_params(3),
        name="window_back",
    )(d_window, shared, down, resid)


def moe_kernel(
    attended_ref, wout_ref, tokens_ref, small_ref, gate_up_ref, down_ref, cotangent_ref, chosen_ref,
    resid_ref, shared_ref, d_resid_ref, branch_ref, router_ref, part_gate_up_ref, part_down_ref,
    normed_ref, d_ref, grad_gate_up, grad_down, probs_ref, share_tx, share_in, logits_ref,
    tx_a, rx_a, half_a, tx_b, rx_b, half_b,
    pair_a, tops_a, bottoms_a, full_a, pair_b, tops_b, bottoms_b, full_b,
    send_sems, recv_sems,
):
    s, g = lax.axis_index("seq"), lax.axis_index("fsdp")
    p = ring_places(s)
    peers = others(s, 8)
    sems = (send_sems, recv_sems)
    greet([at_seq(q) for q in peers] + fsdp_neighbours(g))
    model = tokens_ref.shape[1]
    units = down_ref.shape[0]
    per = units // EXPERTS

    def branch_part(place):
        return nn(attended_ref[rows_at(place), :], wout_ref[...])

    branch = run(Task(ring_scatter(branch_part, tx_a, rx_a, half_a, s, sems, 0)))
    resid = tokens_ref[...].astype(jnp.float32) + branch
    resid_ref[...] = resid
    gain = small_ref[1:2, :]
    router = small_ref[...].astype(jnp.bfloat16)
    normed_ref[s] = (resid * scale_of(resid) * gain).astype(jnp.bfloat16)
    gather = Task(ring_gather(normed_ref, s, sems, 8))
    gather.step()

    def block(place):
        x = normed_ref[place]
        logits = nt(router, x)
        logits = jnp.concatenate([logits[2 : 2 + EXPERTS], jnp.full((4, 128), NEGATIVE)], axis=0)
        probs = jnp.exp(logits - jnp.max(logits, axis=0, keepdims=True))
        probs = probs / jnp.sum(probs, axis=0, keepdims=True)
        probs_ref[place] = probs
        share = jnp.concatenate([probs * chosen_ref[place], jnp.zeros((120, 128))], axis=0)
        share = jnp.transpose(share)
        plain = nt(cotangent_ref[place], down_ref[...])
        both = nn(x, gate_up_ref[...])
        sums = []
        for e in range(EXPERTS):
            at = slice(e * per, (e + 1) * per)
            gate, up = both[:, at], both[:, units + e * per : units + (e + 1) * per]
            wide = jnp.broadcast_to(share[:, e : e + 1], gate.shape)
            sigmoid = 1.0 / (1.0 + jnp.exp(-gate))
            silu = gate * sigmoid
            hidden = (silu * up).astype(jnp.bfloat16).astype(jnp.float32)
            shared_ref[rows_at(place), at] = (hidden * wide).astype(jnp.bfloat16)
            sums.append(jnp.sum(plain[:, at] * hidden, axis=1, keepdims=True))
            d_hidden = plain[:, at] * wide
            d_gate = d_hidden * up * sigmoid * (1.0 + gate * (1.0 - sigmoid))
            d_ref[rows_at(place), at] = d_gate.astype(jnp.bfloat16)
            d_ref[rows_at(place), units + e * per : units + (e + 1) * per] = (
                d_hidden * silu
            ).astype(jnp.bfloat16)
        sums = jnp.concatenate(sums + [jnp.zeros((128, 128 - EXPERTS))], axis=1)
        share_tx[place] = jnp.transpose(sums)[:8]

    block(s)
    gather.step()
    gather.step()
    block(p["down"])
    block(p["up"])
    gather.step()
    block(p["over"])
    gather.step()
    block(p["far"])
    block(p["over_up"])
    block(p["over_down"])
    run(gather)
    block(p["over_far"])
    shares = exchange(share_tx, share_in, s, peers, at_seq, sems, 24)
    share_in[s] = share_tx[s]

    def weight_grads():
        shared, grad = shared_ref[...], cotangent_ref[...].reshape(8 * 128, model)
        value = tn(shared, grad).astype(jnp.bfloat16)
        yield
        grad_down[...] = nn(unit_order(1), value).astype(jnp.bfloat16)
        down_sum = Task(
            fsdp_scatter(
                grad_down, 32, 16, (pair_b, tops_b, bottoms_b, full_b), g, sems, 55
            )
        )
        down_sum.step()
        yield
        for third in range(3):

            @pl.loop(0, 4)
            def _(j, third=third):
                at = rows_at(third * 4 + j)
                normed = normed_ref[:, :, at].reshape(8 * 128, 128)
                grad_gate_up[at, :] = tn(normed, d_ref[...]).astype(jnp.bfloat16)

            yield
        gate_up_sum = Task(
            fsdp_scatter(
                grad_gate_up, 96, 48, (pair_a, tops_a, bottoms_a, full_a), g, sems, 38
            )
        )
        while not (down_sum.done and gate_up_sum.done):
            gate_up_sum.step()
            down_sum.step()
            yield
        part_gate_up_ref[...] = gate_up_sum.value.astype(jnp.bfloat16)
        part_down_ref[...] = down_sum.value.astype(jnp.bfloat16)

    grads = Task(weight_grads())

    def normed_part(place):
        return nt(d_ref[rows_at(place), :], gate_up_ref[...])

    d_normed = run(Task(ring_scatter(normed_part, tx_b, rx_b, half_b, s, sems, 16)), grads)
    for copy in shares:
        copy.wait_recv()

    d_router = jnp.sum(share_in[...], axis=0) * chosen_ref[s]
    probs = probs_ref[s]
    d_logits = probs * (d_router - jnp.sum(probs * d_router, axis=0, keepdims=True))
    d_logits = d_logits.astype(jnp.bfloat16)
    logits_ref[s] = d_logits.astype(jnp.float32)
    spreads = spread(logits_ref.at[s], logits_ref, s, peers, at_seq, sems, 31)
    padded = jnp.concatenate([jnp.zeros((2, 128), jnp.bfloat16), d_logits[:6]], axis=0)
    d_normed = d_normed + tn(padded, router)
    resid = resid_ref[...]
    scale = scale_of(resid)
    d_resid = cotangent_ref[s].astype(jnp.float32) + rms_back(
        d_normed, resid * scale, scale, gain
    )
    d_resid_ref[...] = d_resid
    branch_ref[s] = d_resid.astype(jnp.bfloat16)
    run_all(Task(ring_gather(branch_ref, s, sems, 72)), grads)
    for copy in spreads:
        copy.wait_recv()
    total = jnp.zeros((8, model), jnp.float32)
    for q in range(8):
        total += nn(logits_ref[q].astype(jnp.bfloat16), normed_ref[q])
    router_ref[...] = total
    for copy in shares + spreads:
        copy.wait_send()


def moe(attended, wout, tokens, small, gate_up, down, cotangent, chosen):
    own, model = tokens.shape
    rows = 8 * own
    width, units = gate_up.shape[1], down.shape[0]
    f32 = jnp.float32
    tiny = pltpu.VMEM((8, 8, own), f32)
    return pl.pallas_call(
        moe_kernel,
        in_specs=[VMEM] * 8,
        out_specs=[VMEM] * 7,
        out_shape=[
            array((own, model), f32),
            array((rows, units)),
            array((own, model), f32),
            array((8, own, model)),
            array((8, model), f32),
            array((model // 16, width)),
            array((units // 16, model)),
        ],
        scratch_shapes=[
            pltpu.VMEM((8, own, model), jnp.bfloat16),
            pltpu.VMEM((rows, width), jnp.bfloat16),
            pltpu.VMEM((model, width), jnp.bfloat16),
            pltpu.VMEM((units, model), jnp.bfloat16),
            tiny,
            tiny,
            tiny,
            tiny,
            *ring_buffers(own, model),
            *ring_buffers(own, model),
            *fsdp_buffers(model // 16, 48, width),
            *fsdp_buffers(units // 16, 16, model),
            *sem_pair(80),
        ],
        compiler_params=kernel_params(4),
        name="moe",
    )(attended, wout, tokens, small, gate_up, down, cotangent, chosen)


def finish_kernel(
    dq_ref, dkv_ref, weight_ref, normed_ref, attended_ref, branch_ref, router_ref, experts_ref,
    d_resid_ref, tokens_ref, small_ref,
    grad_input_ref, columns_out, experts_out, wout_out,
    d_ref, grads, grads_wout, columns_tx, experts_tx, wout_tx, tx, rx, rx_half,
    pair_a, tops_a, bottoms_a, full_a, pair_b, tops_b, bottoms_b, full_b,
    send_sems, recv_sems,
):
    s, g = lax.axis_index("seq"), lax.axis_index("fsdp")
    peers = others(s, 8)
    sems = (send_sems, recv_sems)
    holder, owner = head_holder(g, s), head_owner(g, s)
    alone = (holder["fsdp"] == g) & (holder["seq"] == s)
    greet_all([at_seq(q) for q in peers] + fsdp_neighbours(g), (holder, owner), alone)
    experts_tx[...] = expand(experts_ref[...], 12).reshape(experts_tx.shape)
    copies = exchange(experts_tx, experts_out, s, peers, at_seq, sems, 8)
    experts_out[s] = experts_tx[s]
    d_ref[:, :SMALL] = dq_ref[...]
    d_ref[:, SMALL:KEYS] = jnp.zeros((d_ref.shape[0], WIDTH), jnp.bfloat16)
    d_ref[:, KEYS:] = dkv_ref[...]

    def partial(place):
        return nt(d_ref[rows_at(place), :], weight_ref[...])

    def weight_grads():
        d = d_ref[...]
        lane = lax.broadcasted_iota(jnp.int32, (128, KEYS - 2 * WIDTH), 1)

        @pl.loop(0, normed_ref.shape[1] // 128)
        def _(j):
            at = rows_at(j)
            value = tn(normed_ref[:, at], d)
            router = jnp.concatenate(
                [jnp.zeros((WIDTH + 2, 128)), router_ref[:, at], jnp.zeros((54, 128))], axis=0
            )
            router = jnp.transpose(router)
            grads[at, : 2 * WIDTH] = value[:, : 2 * WIDTH].astype(jnp.bfloat16)
            grads[at, 2 * WIDTH : KEYS] = jnp.where(
                lane < WIDTH, value[:, 2 * WIDTH : KEYS], router
            ).astype(jnp.bfloat16)
            grads[at, KEYS:] = value[:, KEYS:].astype(jnp.bfloat16)

        main = Task(
            fsdp_scatter(grads, 96, 48, (pair_a, tops_a, bottoms_a, full_a), g, sems, 15)
        )
        main.step()
        yield
        value = tn(attended_ref[...], branch_ref[...].reshape(d.shape[0], -1)).astype(jnp.bfloat16)
        grads_wout[...] = expand(value, 12)
        wout = Task(
            fsdp_scatter(grads_wout, 16, 16, (pair_b, tops_b, bottoms_b, full_b), g, sems, 32)
        )
        while not main.done:
            main.step()
            wout.step()
            yield
        columns_tx[...] = expand(main.value.astype(jnp.bfloat16), 12).reshape(columns_tx.shape)
        copies.extend(exchange(columns_tx, columns_out, s, peers, at_seq, sems, 49))
        columns_out[s] = columns_tx[s]
        yield
        while not wout.done:
            wout.step()
            yield
        wout_tx[...] = wout.value.astype(jnp.bfloat16)
        return swap_rows(wout_tx, wout_out, sems, 56, owner, alone)

    weights = Task(weight_grads())
    d_normed = run(Task(ring_scatter(partial, tx, rx, rx_half, s, sems, 0)), weights)
    values = tokens_ref[...].astype(jnp.float32)
    scale = scale_of(values)
    grad_input_ref[...] = d_resid_ref[...] + rms_back(
        d_normed, values * scale, scale, small_ref[0:1, :]
    )
    wait_rows = run(weights)
    wait_rows()
    for copy in copies:
        copy.wait_recv()
    for copy in copies:
        copy.wait_send()


def finish(dq, dkv, weight, normed, attended, branch, router, experts, d_resid, tokens, small):
    own, model = tokens.shape
    rows = dq.shape[0]
    width = weight.shape[1]
    columns = (8, 16, width)
    blocks = (8, 16, experts.shape[1])
    bf16 = jnp.bfloat16
    return pl.pallas_call(
        finish_kernel,
        in_specs=[VMEM] * 11,
        out_specs=[VMEM] * 4,
        out_shape=[
            array((own, model), jnp.float32),
            array(columns),
            array(blocks),
            array((16, model)),
        ],
        scratch_shapes=[
            pltpu.VMEM((rows, width), bf16),
            pltpu.VMEM((model, width), bf16),
            pltpu.VMEM((256, model), bf16),
            pltpu.VMEM(columns, bf16),
            pltpu.VMEM(blocks, bf16),
            pltpu.VMEM((16, model), bf16),
            *ring_buffers(own, model),
            *fsdp_buffers(model // 16, 48, width),
            *fsdp_buffers(16, 16, model),
            *sem_pair(57),
        ],
        compiler_params=kernel_params(5),
        name="finish",
    )(dq, dkv, weight, normed, attended, branch, router, experts, d_resid, tokens, small)


def columns_by_owner(fsdp, seq, total):
    inner = total // (fsdp * seq)
    place = np.arange(total).reshape(fsdp, seq, inner).transpose(1, 0, 2).reshape(-1)
    one_hot = np.zeros((total, total), np.float32)
    one_hot[place, np.arange(total)] = 1
    return jnp.asarray(one_hot, jnp.bfloat16)


def pad_rows(x, axis):
    pads = [(0, 0)] * x.ndim
    pads[axis] = (0, 16 - x.shape[axis])
    return jnp.pad(x, pads)


def on_device(
    tokens,
    gain_one,
    w_qkv,
    w_out,
    gain_two,
    w_router,
    w_gate,
    w_up,
    w_down,
    doc_starts,
    routes,
    cotangent,
):
    seq = lax.axis_size("seq")
    fsdp = lax.axis_size("fsdp")
    group_index = lax.axis_index("fsdp")
    own, model = tokens.shape
    group_rows = own * seq
    experts, own_model, ff = w_gate.shape
    own_ff = ff // seq
    order = columns_by_owner(fsdp, seq, ff)
    bf16, f32 = jnp.bfloat16, jnp.float32

    gate_up = nn(
        jnp.concatenate([w_gate, w_up], axis=0).reshape(2 * experts * own_model, ff), order
    ).astype(bf16)
    gate_up = gate_up.reshape(2 * experts, own_model, seq, own_ff)
    gate_up = jnp.transpose(gate_up, (2, 1, 0, 3)).reshape(seq, own_model, 2 * experts * own_ff)
    qkv_parts = jnp.transpose(w_qkv.reshape(own_model, seq, 5 * WIDTH), (1, 0, 2))
    small = jnp.concatenate([gain_one[:, None], gain_two[:, None], w_router], axis=1)
    small = jnp.pad(small, ((0, 0), (0, WIDTH - small.shape[1])))
    columns = jnp.concatenate(
        [
            qkv_parts[:, :, :SMALL],
            jnp.broadcast_to(small[None], (seq,) + small.shape),
            qkv_parts[:, :, SMALL:],
        ],
        axis=2,
    )
    expert_ids = jnp.arange(8, dtype=jnp.int32)
    chosen = jnp.sum((routes[None, :, :] == expert_ids[:, None, None]).astype(f32), axis=2)
    normed_one, queries, keyval, weight, small, gate_up, down, out_weight, chosen = start(
        tokens,
        pad_rows(columns, 1),
        pad_rows(gate_up, 1),
        w_down.reshape(-1, model),
        pad_rows(w_out, 0),
        chosen,
    )

    window, cotangent_all = window_of(keyval, cotangent)
    window = window.reshape((LOOK + 1) * group_rows, 2 * WIDTH)
    positions = group_index * group_rows + jnp.arange(group_rows, dtype=jnp.int32)
    begins = jnp.max(
        jnp.where(doc_starts[:, None] <= positions[None, :], doc_starts[:, None], 0), axis=0
    )
    lo = begins - (group_index - LOOK) * group_rows
    blocks = group_rows // BQ
    lo_blocks = lo.reshape(blocks, BQ)
    diag = (LOOK * group_rows + jnp.arange(blocks, dtype=jnp.int32) * BQ) // BK
    end = (LOOK * group_rows + (jnp.arange(blocks, dtype=jnp.int32) + 1) * BQ + BK - 1) // BK
    first = jnp.minimum(lo_blocks[:, 0] // BK, diag)
    full = jnp.minimum((lo_blocks[:, -1] + BK - 1) // BK, diag)
    bounds = jnp.stack([first, full, diag, end], axis=1)
    attended, lse = attention(bounds, lo[None, :], queries, window)

    residual, shared, d_resid, d_branch, grad_router, part_gate_up, part_down = moe(
        attended, out_weight, tokens, small, gate_up, down, cotangent_all, chosen
    )

    d_attended = nt(d_branch.reshape(group_rows, model), out_weight).astype(bf16)
    d_queries, d_window = attention_back(
        bounds, lo[None, :], queries, window, attended, d_attended, lse
    )
    d_keyval, output = window_back(
        d_window.reshape(LOOK + 1, group_rows, 2 * WIDTH), shared, down, residual
    )
    grad_input, columns, back, shard_out = finish(
        d_queries, d_keyval, weight, normed_one, attended, d_branch, grad_router, part_gate_up,
        d_resid, tokens, small,
    )

    shard_down = part_down.astype(f32).reshape(experts, -1, model)
    shard_out = shard_out[:own_model].astype(f32)
    columns = columns[:, :own_model].astype(f32)
    shard_qkv = jnp.concatenate([columns[:, :, :SMALL], columns[:, :, KEYS:]], axis=2)
    shard_qkv = jnp.transpose(shard_qkv, (1, 0, 2)).reshape(own_model, -1)
    shard_router = columns[0, :, SMALL + 2 : SMALL + 2 + experts]
    back = back[:, :own_model].reshape(seq, own_model, 2 * experts, own_ff)
    back = jnp.transpose(back, (2, 1, 0, 3)).reshape(2 * experts * own_model, ff)
    back = nt(back, order).reshape(2 * experts, own_model, ff)
    shard_gate, shard_up = back[:experts], back[experts:]

    shard_gain_one = jnp.sum(w_qkv.astype(f32) * shard_qkv, axis=1)
    shard_gain_one = shard_gain_one / gain_one.astype(f32)
    shard_gain_two = jnp.sum(w_router.astype(f32) * shard_router, axis=1)
    shard_gain_two += jnp.sum(w_gate.astype(f32) * shard_gate, axis=(0, 2))
    shard_gain_two += jnp.sum(w_up.astype(f32) * shard_up, axis=(0, 2))
    shard_gain_two = shard_gain_two / gain_two.astype(f32)
    return (
        output,
        grad_input,
        shard_gain_one,
        shard_qkv,
        shard_out,
        shard_gain_two,
        shard_router,
        shard_gate,
        shard_up,
        shard_down,
    )


def solution(mesh):
    rows, vector = P(BOTH, None), P(BOTH)
    middle = P(None, BOTH, None)
    in_specs = (
        rows, vector, rows, rows, vector, rows, middle, middle, middle, P(), rows, rows,
    )
    out_specs = (rows, rows, vector, rows, rows, vector, rows, middle, middle, middle)
    return jax.shard_map(
        on_device, mesh=mesh, in_specs=in_specs, out_specs=out_specs, check_vma=False
    )
```

```python
import functools

import jax
import jax.numpy as jnp
from jax import lax
from jax.experimental import pallas as pl
from jax.experimental.pallas import tpu as pltpu
from jax.sharding import PartitionSpec as P

WIDTH = 64
LOOK = 4
EXPERTS = 4
EPS = 1e-06
NEGATIVE = -1e30
BQ = 256
BK = 1024
BK_BACK = 512
BOTH = ("fsdp", "seq")


def nt(a, b):
    return lax.dot_general(a, b, (((1,), (1,)), ((), ())), preferred_element_type=jnp.float32)


def tn(a, b):
    return lax.dot_general(a, b, (((0,), (0,)), ((), ())), preferred_element_type=jnp.float32)


def nn(a, b):
    return jnp.dot(a, b, preferred_element_type=jnp.float32)


def stack_heads(rows, low):
    heads = rows.shape[1] // WIDTH
    zero = jnp.zeros((rows.shape[0], WIDTH), rows.dtype)
    parts = []
    for h in range(heads):
        part = rows[:, h * WIDTH : (h + 1) * WIDTH]
        parts.append(jnp.concatenate([part, zero] if low else [zero, part], axis=1))
    return jnp.concatenate(parts, axis=0)


def chunk_loops(bounds_ref, step):
    b = pl.program_id(0)
    first, full, diag, end = (bounds_ref[b, i] for i in range(4))
    pl.loop(first, full)(lambda c: step(c, True))
    pl.loop(full, diag)(lambda c: step(c, False))
    pl.loop(diag, end)(lambda c: step(c, True))


def attention_kernel(bounds_ref, lo_ref, q_ref, kv_ref, out_ref, lse_ref, m_ref, l_ref, acc_ref):
    heads = q_ref.shape[1] // WIDTH
    queries = stack_heads(q_ref[...] * 0.125, True)
    m_ref[...] = jnp.full_like(m_ref, NEGATIVE)
    l_ref[...] = jnp.zeros_like(l_ref)
    acc_ref[...] = jnp.zeros_like(acc_ref)
    base = LOOK * 1024 + pl.program_id(0) * BQ

    def step(c, masked):
        start = pl.multiple_of(c * BK, BK)
        rows = kv_ref[pl.ds(start, BK), :]
        scores = nt(rows, queries)
        if masked:
            key = start + lax.broadcasted_iota(jnp.int32, (BK, BQ), 0)
            query = base + lax.broadcasted_iota(jnp.int32, (BK, BQ), 1)
            seen = (key >= lo_ref[...]) & (key <= query)
            scores = jnp.where(jnp.concatenate([seen] * heads, axis=1), scores, NEGATIVE)
        old = m_ref[...]
        new = jnp.maximum(old, jnp.max(scores, axis=0, keepdims=True))
        probs = jnp.exp(scores - new)
        fade = jnp.exp(old - new)
        m_ref[...] = new
        l_ref[...] = l_ref[...] * fade + jnp.sum(probs, axis=0, keepdims=True)
        acc_ref[...] = acc_ref[...] * fade + tn(rows, probs.astype(jnp.bfloat16))

    chunk_loops(bounds_ref, step)
    total = l_ref[...]
    result = jnp.transpose(acc_ref[...] / total)
    out_ref[...] = jnp.concatenate(
        [result[h * BQ : (h + 1) * BQ, WIDTH:] for h in range(heads)], axis=1
    ).astype(jnp.bfloat16)
    lse_ref[...] = jnp.broadcast_to(m_ref[...] + jnp.log(total), lse_ref.shape)


def attention(bounds, lo, q, kv):
    rows, width = q.shape
    heads = width // WIDTH
    blocks = rows // BQ
    return pl.pallas_call(
        attention_kernel,
        grid=(blocks,),
        in_specs=[
            pl.BlockSpec(memory_space=pltpu.SMEM),
            pl.BlockSpec((1, BQ), lambda b: (0, b)),
            pl.BlockSpec((BQ, width), lambda b: (b, 0)),
            pl.BlockSpec(memory_space=pltpu.VMEM),
        ],
        out_specs=[
            pl.BlockSpec((BQ, width), lambda b: (b, 0)),
            pl.BlockSpec((None, 8, heads * BQ), lambda b: (b, 0, 0)),
        ],
        out_shape=[
            jax.ShapeDtypeStruct((rows, width), jnp.bfloat16),
            jax.ShapeDtypeStruct((blocks, 8, heads * BQ), jnp.float32),
        ],
        scratch_shapes=[
            pltpu.VMEM((1, heads * BQ), jnp.float32),
            pltpu.VMEM((1, heads * BQ), jnp.float32),
            pltpu.VMEM((2 * WIDTH, heads * BQ), jnp.float32),
        ],
        compiler_params=pltpu.CompilerParams(vmem_limit_bytes=48 << 20),
        cost_estimate=pl.CostEstimate(
            flops=4 * rows * 4096 * width, bytes_accessed=4 << 20, transcendentals=rows * 4096 * 3
        ),
        name="attention",
    )(bounds, lo, q, kv)


def attention_back_kernel(
    bounds_ref, lo_ref, q_ref, kv_ref, out_ref, dout_ref, lse_ref, dq_ref, dkv_ref, acc_ref
):
    heads = q_ref.shape[1] // WIDTH
    queries = stack_heads(q_ref[...] * 0.125, True)
    douts = stack_heads(dout_ref[...], False)
    outs = stack_heads(out_ref[...], False)
    delta = jnp.sum(
        jnp.transpose(douts.astype(jnp.float32) * outs.astype(jnp.float32)), axis=0, keepdims=True
    )
    lse = lse_ref[:1, :]
    acc_ref[...] = jnp.zeros_like(acc_ref)
    base = LOOK * 1024 + pl.program_id(0) * BQ

    @pl.when(pl.program_id(0) == 0)
    def _():
        dkv_ref[...] = jnp.zeros_like(dkv_ref)

    def step(c, masked):
        start = pl.multiple_of(c * BK_BACK, BK_BACK)
        rows = kv_ref[pl.ds(start, BK_BACK), :]
        scores = nt(rows, queries)
        if masked:
            key = start + lax.broadcasted_iota(jnp.int32, (BK_BACK, BQ), 0)
            query = base + lax.broadcasted_iota(jnp.int32, (BK_BACK, BQ), 1)
            seen = (key >= lo_ref[...]) & (key <= query)
            scores = jnp.where(jnp.concatenate([seen] * heads, axis=1), scores, NEGATIVE)
        probs = jnp.exp(scores - lse)
        d_scores = (probs * (nt(rows, douts) - delta)).astype(jnp.bfloat16)
        dkv_ref[pl.ds(start, BK_BACK), :] += nn(d_scores, queries) + nn(
            probs.astype(jnp.bfloat16), douts
        )
        acc_ref[...] += tn(rows, d_scores)

    chunk_loops(bounds_ref, step)
    result = jnp.transpose(acc_ref[...]) * 0.125
    dq_ref[...] = jnp.concatenate(
        [result[h * BQ : (h + 1) * BQ, :WIDTH] for h in range(heads)], axis=1
    ).astype(jnp.bfloat16)


def attention_back(bounds, lo_row, q, kv, out, dout, lse):
    rows, width = q.shape
    heads = width // WIDTH
    blocks = rows // BQ
    row_block = pl.BlockSpec((BQ, width), lambda b: (b, 0))
    return pl.pallas_call(
        attention_back_kernel,
        grid=(blocks,),
        in_specs=[
            pl.BlockSpec(memory_space=pltpu.SMEM),
            pl.BlockSpec((1, BQ), lambda b: (0, b)),
            row_block,
            pl.BlockSpec(memory_space=pltpu.VMEM),
            row_block,
            row_block,
            pl.BlockSpec((None, 8, heads * BQ), lambda b: (b, 0, 0)),
        ],
        out_specs=[
            row_block,
            pl.BlockSpec(kv.shape, lambda b: (0, 0)),
        ],
        out_shape=[
            jax.ShapeDtypeStruct((rows, width), jnp.bfloat16),
            jax.ShapeDtypeStruct(kv.shape, jnp.float32),
        ],
        scratch_shapes=[pltpu.VMEM((2 * WIDTH, heads * BQ), jnp.float32)],
        compiler_params=pltpu.CompilerParams(vmem_limit_bytes=48 << 20),
        cost_estimate=pl.CostEstimate(
            flops=10 * rows * 4096 * width, bytes_accessed=8 << 20, transcendentals=rows * 4096 * 3
        ),
        name="attention_back",
    )(bounds, lo_row, q, kv, out, dout, lse)


RING = 4
MESH = pl.DeviceIdType.MESH
VMEM = pl.BlockSpec(memory_space=pltpu.VMEM)


def at_seq(index):
    return {"seq": index}


def at_fsdp(index):
    return {"fsdp": index}


def ring_places(s):
    x, y = lax.div(s, RING), lax.rem(s, RING)

    def place(dx, dy):
        return lax.rem(x + dx, 2) * RING + lax.rem(y + dy, RING)

    return {
        "up": place(0, 1),
        "down": place(0, 3),
        "far": place(0, 2),
        "over": place(1, 0),
        "over_up": place(1, 1),
        "over_down": place(1, 3),
        "over_far": place(1, 2),
    }


def greet(targets):
    barrier = pltpu.get_barrier_semaphore()
    for target in targets:
        pl.semaphore_signal(barrier, inc=1, device_id=target, device_id_type=MESH)
    pl.semaphore_wait(barrier, len(targets))


def send(src, dst, sems, index, target):
    copy = pltpu.make_async_remote_copy(
        src_ref=src,
        dst_ref=dst,
        send_sem=sems[0].at[index],
        recv_sem=sems[1].at[index],
        device_id=target,
        device_id_type=MESH,
    )
    copy.start()
    return copy


def steps(*tasks):
    for task in tasks:
        task.step()


class Task:
    def __init__(self, steps):
        self.steps, self.done, self.value = steps, False, None

    def step(self):
        if not self.done:
            try:
                next(self.steps)
            except StopIteration as end:
                self.done, self.value = True, end.value


def run(task, *beside):
    while not task.done:
        task.step()
        for other in beside:
            other.step()
    return task.value


def run_all(*tasks):
    while not all(task.done for task in tasks):
        for task in tasks:
            task.step()


RING_SEMS = 14


def ring_gather(out, s, sems, base):
    p = ring_places(s)
    half = out.shape[1] // 2
    top, bottom = pl.ds(0, half), pl.ds(half, half)
    up, down, over = at_seq(p["up"]), at_seq(p["down"]), at_seq(p["over"])
    copies = []

    def go(place, rows, target):
        block = out.at[place, rows]
        copies.append(send(block, block, sems, base + len(copies), target))
        return copies[-1]

    up_top, down_bottom = go(s, top, up), go(s, bottom, down)
    over_top, over_bottom = go(s, top, over), go(s, bottom, over)
    up_bottom, down_top = go(s, bottom, up), go(s, top, down)
    yield
    up_top.wait_recv()
    far_top = go(p["down"], top, up)
    down_bottom.wait_recv()
    far_bottom = go(p["up"], bottom, down)
    over_top.wait_recv()
    side = [go(p["over"], top, up), go(p["over"], top, down)]
    over_bottom.wait_recv()
    side += [go(p["over"], bottom, up), go(p["over"], bottom, down)]
    up_bottom.wait_recv()
    down_top.wait_recv()
    yield
    far_top.wait_recv()
    side.append(go(p["far"], top, over))
    far_bottom.wait_recv()
    side.append(go(p["far"], bottom, over))
    yield
    for copy in side[:4]:
        copy.wait_recv()
    yield
    for copy in side[4:]:
        copy.wait_recv()
    for copy in copies:
        copy.wait_send()


def ring_scatter(partial, tx, rx, s, sems, base):
    p = ring_places(s)
    half = tx.shape[1] // 2
    top, bottom = pl.ds(0, half), pl.ds(half, half)
    up, down, over = at_seq(p["up"]), at_seq(p["down"]), at_seq(p["over"])
    copies = []

    def cut(value, rows):
        return value[:half] if rows is top else value[half:]

    def go(slot, rows, value, target):
        tx[slot, rows, :] = value.astype(tx.dtype)
        copies.append(
            send(tx.at[slot, rows], rx.at[slot, rows], sems, base + len(copies), target)
        )
        return copies[-1]

    def wide(slot, rows):
        return rx[slot, rows, :].astype(jnp.float32)

    value = partial(p["over_up"])
    second = [go(1, rows, cut(value, rows), up) for rows in (top, bottom)]
    value = partial(p["over_down"])
    third = [go(2, rows, cut(value, rows), down) for rows in (top, bottom)]
    value = partial(p["over_far"])
    first = [go(0, rows, cut(value, rows), over) for rows in (top, bottom)]
    value = partial(p["far"])
    yield
    first[0].wait_recv()
    to_down = go(3, top, cut(value, top) + wide(0, top), down)
    first[1].wait_recv()
    to_up = go(3, bottom, cut(value, bottom) + wide(0, bottom), up)
    to_owner_down, to_owner_up = partial(p["down"]), partial(p["up"])
    fifth = [go(5, bottom, cut(to_owner_down, bottom), down)]
    sixth = [go(6, top, cut(to_owner_up, top), up)]
    value = partial(p["over"])
    yield
    fourth = []
    for k, rows in enumerate((top, bottom)):
        second[k].wait_recv()
        third[k].wait_recv()
        fourth.append(go(4, rows, cut(value, rows) + wide(1, rows) + wide(2, rows), over))
    yield
    to_down.wait_recv()
    fifth.append(go(5, top, cut(to_owner_down, top) + wide(3, top), down))
    to_up.wait_recv()
    sixth.append(go(6, bottom, cut(to_owner_up, bottom) + wide(3, bottom), up))
    value = partial(s)
    yield
    for copy in fourth + fifth + sixth:
        copy.wait_recv()
    value = value + (rx[4].astype(jnp.float32) + rx[5].astype(jnp.float32))
    value = value + rx[6].astype(jnp.float32)
    for copy in copies:
        copy.wait_send()
    return value


def ring_buffers(rows, width):
    return [pltpu.VMEM((7, rows, width), jnp.bfloat16)] * 2


def fsdp_place(g):
    x, z, core = lax.div(g, 8), lax.rem(lax.div(g, 2), RING), lax.rem(g, 2)

    def place(dx, dz, dcore):
        return (
            lax.rem(x + dx, 2) * 8 + lax.rem(z + dz, RING) * 2 + lax.rem(core + dcore, 2)
        )

    return place


def fsdp_neighbours(g):
    place = fsdp_place(g)
    return [at_fsdp(place(*d)) for d in ((1, 0, 0), (0, 1, 0), (0, 3, 0), (0, 0, 1))]


def part_of(ref, rows, cut):
    def view(index, half=None):
        first, count = {None: (0, rows), "top": (0, cut), "bottom": (cut, rows - cut)}[half]
        return ref.at[pl.ds(pl.multiple_of(index * rows + first, 16), count)]

    return view


def fsdp_gather(ref, rows, cut, g, sems, base):
    view, place = part_of(ref, rows, cut), fsdp_place(g)
    over, up, down, pal = fsdp_neighbours(g)
    copies = []

    def go(index, half, sem, target):
        copies.append(send(view(index, half), view(index, half), sems, base + sem, target))
        return copies[-1]

    me = place(0, 0, 0)
    to_over = go(me, None, 16, over)
    to_up, to_down = go(me, None, 0, up), go(me, None, 1, down)
    pals = [go(me, None, 8, pal)]
    yield
    to_over.wait_recv()
    side = place(1, 0, 0)
    side_up, side_down = go(side, None, 2, up), go(side, None, 3, down)
    pals.append(go(side, None, 9, pal))
    yield
    to_up.wait_recv()
    far_up = go(place(0, 3, 0), "top", 4, up)
    pals.append(go(place(0, 3, 0), None, 10, pal))
    to_down.wait_recv()
    far_down = go(place(0, 1, 0), "bottom", 5, down) if cut < rows else None
    pals.append(go(place(0, 1, 0), None, 11, pal))
    yield
    side_up.wait_recv()
    side_far_up = go(place(1, 3, 0), "top", 6, up)
    pals.append(go(place(1, 3, 0), None, 12, pal))
    side_down.wait_recv()
    side_far_down = go(place(1, 1, 0), "bottom", 7, down) if cut < rows else None
    pals.append(go(place(1, 1, 0), None, 13, pal))
    yield
    far_up.wait_recv()
    if far_down is not None:
        far_down.wait_recv()
    pals.append(go(place(0, 2, 0), None, 14, pal))
    yield
    side_far_up.wait_recv()
    if side_far_down is not None:
        side_far_down.wait_recv()
    pals.append(go(place(1, 2, 0), None, 15, pal))
    yield
    for copy in pals:
        copy.wait_recv()
    for copy in copies:
        copy.wait_send()


def fsdp_buffers(rows, cut, width):
    return [
        pltpu.VMEM((8 * rows, width), jnp.bfloat16),
        pltpu.VMEM((2, cut, width), jnp.bfloat16),
        pltpu.VMEM((2, max(rows - cut, 16), width), jnp.bfloat16),
        pltpu.VMEM((5, rows, width), jnp.bfloat16),
    ]


def fsdp_scatter(ref, rows, cut, buffers, g, sems, base):
    pair, tops, bottoms, full = buffers
    view, place = part_of(ref, rows, cut), fsdp_place(g)
    over, up, down, pal = fsdp_neighbours(g)
    copies = []

    def go(src, dst, sem, target):
        copies.append(send(src, dst, sems, base + sem, target))
        return copies[-1]

    def wide(part):
        return part[...].astype(jnp.float32)

    def slot(index):
        return pair.at[pl.ds(pl.multiple_of(lax.div(index, 2) * rows, 16), rows)]

    order = [(1, 2), (0, 2), (1, 3), (1, 1), (0, 3), (0, 1), (1, 0), (0, 0)]
    pals = {}
    for k, (dx, dz) in enumerate(order):
        index = place(dx, dz, 1)
        pals[dx, dz] = go(view(index), slot(index), k, pal)
    yield

    def paired(dx, dz):
        pals[dx, dz].wait_recv()
        return wide(view(place(dx, dz, 0))) + wide(slot(place(dx, dz, 0)))

    halves = {}
    for k, dx in enumerate((1, 0)):
        index = place(dx, 2, 0)
        value = paired(dx, 2)
        view(index)[...] = value.astype(jnp.bfloat16)
        halves[dx, "top"] = go(view(index, "top"), tops.at[dx], 8 + 2 * k, down)
        if cut < rows:
            halves[dx, "bottom"] = go(view(index, "bottom"), bottoms.at[dx], 9 + 2 * k, up)
    yield
    fulls = {}
    for k, dx in enumerate((1, 0)):
        index = place(dx, 3, 0)
        value = paired(dx, 3)
        halves[dx, "top"].wait_recv()
        view(index, "top")[...] = (value[:cut] + wide(tops.at[dx])).astype(jnp.bfloat16)
        if cut < rows:
            view(index, "bottom")[...] = value[cut:].astype(jnp.bfloat16)
        fulls[dx, "down"] = go(view(index), full.at[2 * dx], 12 + 2 * k, down)
        index = place(dx, 1, 0)
        value = paired(dx, 1)
        if cut < rows:
            halves[dx, "bottom"].wait_recv()
            view(index, "top")[...] = value[:cut].astype(jnp.bfloat16)
            view(index, "bottom")[...] = (value[cut:] + wide(bottoms.at[dx])).astype(jnp.bfloat16)
        else:
            view(index)[...] = value.astype(jnp.bfloat16)
        fulls[dx, "up"] = go(view(index), full.at[2 * dx + 1], 13 + 2 * k, up)
        yield
    index = place(1, 0, 0)
    value = paired(1, 0)
    fulls[1, "down"].wait_recv()
    fulls[1, "up"].wait_recv()
    view(index)[...] = (value + wide(full.at[2]) + wide(full.at[3])).astype(jnp.bfloat16)
    last = go(view(index), full.at[4], 16, over)
    value = paired(0, 0)
    yield
    fulls[0, "down"].wait_recv()
    fulls[0, "up"].wait_recv()
    value = value + wide(full.at[0]) + wide(full.at[1])
    yield
    last.wait_recv()
    value = value + wide(full.at[4])
    for copy in copies:
        copy.wait_send()
    return value


def sem_pair(count):
    return [pltpu.SemaphoreType.DMA((count,)), pltpu.SemaphoreType.DMA((count,))]


def others(me, count):
    return [lax.rem(me + k, count) for k in range(1, count)]


def exchange(blocks, into, me, peers, at, sems, base):
    return [
        send(blocks.at[p], into.at[me], sems, base + k, at(p)) for k, p in enumerate(peers)
    ]


def spread(block, into, me, peers, at, sems, base):
    return [send(block, into.at[me], sems, base + k, at(p)) for k, p in enumerate(peers)]


def swap_rows(src, dst, sems, index, target, alone):
    away = pltpu.make_async_remote_copy(
        src_ref=src,
        dst_ref=dst,
        send_sem=sems[0].at[index],
        recv_sem=sems[1].at[index],
        device_id=target,
        device_id_type=MESH,
    )
    here = pltpu.make_async_copy(src, dst, sems[0].at[index])
    pl.when(jnp.logical_not(alone))(away.start)
    pl.when(alone)(here.start)

    def wait():
        pl.when(jnp.logical_not(alone))(away.wait)
        pl.when(alone)(here.wait)

    return wait


def head_holder(g, s):
    return {"fsdp": lax.rem(g, 2) * 8 + s, "seq": lax.div(g, 2)}


def head_owner(g, s):
    return {"fsdp": 2 * s + lax.div(g, 8), "seq": lax.rem(g, 8)}


def greet_all(targets, pair, alone):
    barrier = pltpu.get_barrier_semaphore()
    for target in targets:
        pl.semaphore_signal(barrier, inc=1, device_id=target, device_id_type=MESH)

    @pl.when(jnp.logical_not(alone))
    def _():
        for target in pair:
            pl.semaphore_signal(barrier, inc=1, device_id=target, device_id_type=MESH)

    pl.semaphore_wait(barrier, len(targets) + jnp.where(alone, 0, 2))


def compact(blocks, rows):
    total = blocks.shape[0]
    shape = (total // 16 * rows, total)
    source = lax.broadcasted_iota(jnp.int32, shape, 1)
    place = lax.shift_right_logical(source, 4) * rows + (source & 15)
    keep = (place == lax.broadcasted_iota(jnp.int32, shape, 0)) & ((source & 15) < rows)
    return nn(keep.astype(jnp.bfloat16), blocks).astype(jnp.bfloat16)


def expand(rows_in, rows):
    shape = (rows_in.shape[0] // rows * 16, rows_in.shape[0])
    target = lax.broadcasted_iota(jnp.int32, shape, 0)
    place = lax.shift_right_logical(target, 4) * rows + (target & 15)
    keep = (place == lax.broadcasted_iota(jnp.int32, shape, 1)) & ((target & 15) < rows)
    return nn(keep.astype(jnp.bfloat16), rows_in).astype(jnp.bfloat16)


def unit_order(row_axis):
    mixed = lax.broadcasted_iota(jnp.int32, (512, 512), 1 - row_axis)
    plain = lax.broadcasted_iota(jnp.int32, (512, 512), row_axis)
    f = lax.shift_right_logical(mixed, 5)
    e = lax.shift_right_logical(mixed, 3) & 3
    return (e * 128 + f * 8 + (mixed & 7) == plain).astype(jnp.bfloat16)


def owner_units(s, total, owners):
    shape = (total, total // owners)
    unit = lax.broadcasted_iota(jnp.int32, shape, 0)
    place = lax.broadcasted_iota(jnp.int32, shape, 1)
    source = lax.shift_right_logical(place, 3) * (8 * owners) + s * 8 + (place & 7)
    return (unit == source).astype(jnp.bfloat16)


def scale_of(values):
    return lax.rsqrt(jnp.mean(values * values, axis=-1, keepdims=True) + EPS)


def rms_back(d_normed, unit, scale, gain):
    d_unit = d_normed * gain
    return scale * (d_unit - unit * jnp.mean(d_unit * unit, axis=-1, keepdims=True))


def rows_at(place, count=128):
    return pl.ds(pl.multiple_of(place * count, count), count)


def kernel_params(collective_id):
    return pltpu.CompilerParams(
        collective_id=collective_id, has_side_effects=True, vmem_limit_bytes=52 << 20
    )


def array(shape, dtype=jnp.bfloat16):
    return jax.ShapeDtypeStruct(shape, dtype)


SMALL = 3 * WIDTH
KEYS = 4 * WIDTH


def window_steps(out_ref, rows, g, sems, base):
    core = lax.rem(g, 2)
    after, partner = at_fsdp(lax.rem(g + 2, 16)), at_fsdp(g + 1 - 2 * core)

    def part(index):
        return out_ref.at[index, rows]

    first = send(part(4), part(2), sems, base, after)
    yield
    first.wait_recv()
    second = send(part(2), part(0), sems, base + 1, after)
    third = send(part(4 - 2 * core), part(3), sems, base + 2, partner)
    yield
    second.wait_recv()
    fourth = send(part(2 - 2 * core), part(1), sems, base + 3, partner)
    yield
    third.wait_recv()
    fourth.wait_recv()
    for copy in (first, second, third, fourth):
        copy.wait_send()


def window_greeting(g):
    core = lax.rem(g, 2)
    return [at_fsdp(i) for i in (lax.rem(g + 2, 16), lax.rem(g + 14, 16), g + 1 - 2 * core)]


def start_kernel(
    tokens_ref, columns_ref, experts_ref, wout_ref, chosen_ref, cotangent_ref,
    normed_out, q_ref, window_ref, weight_out, small_ref, rows_ref, wout_all_ref, chosen_out_ref,
    cotangent_out,
    all_ref, normed_ref, weight_ref, columns_in, experts_tx, experts_in, mixed, cotangent_all,
    out_sems, send_sems, recv_sems,
):
    s, g = lax.axis_index("seq"), lax.axis_index("fsdp")
    p = ring_places(s)
    peers = others(s, 8)
    sems = (send_sems, recv_sems)
    holder, owner = head_holder(g, s), head_owner(g, s)
    alone = (holder["fsdp"] == g) & (holder["seq"] == s)
    greet_all(
        [at_seq(q) for q in peers] + fsdp_neighbours(g) + window_greeting(g),
        (holder, owner),
        alone,
    )
    copies = exchange(columns_ref, columns_in, s, peers, at_seq, sems, 0)
    wait_rows = swap_rows(
        wout_ref,
        mixed.at[pl.ds(pl.multiple_of(holder["fsdp"] * 16, 16), 16)],
        sems, 45, holder, alone,
    )
    all_ref[s] = tokens_ref[...]
    tokens_in = Task(ring_gather(all_ref, s, sems, 7))
    tokens_in.step()
    chosen_copies = spread(chosen_ref, chosen_out_ref, s, peers, at_seq, sems, 46)
    chosen_out_ref[s] = chosen_ref[...]
    columns_in[s] = columns_ref[s]
    for copy in copies:
        copy.wait_recv()
    weight_ref[rows_at(g, 96), :] = compact(columns_in[...].reshape(128, columns_in.shape[2]), 12)
    columns_gather = Task(fsdp_gather(weight_ref, 96, 48, g, sems, 21))
    columns_gather.step()
    wait_rows()
    wout_gather = Task(fsdp_gather(mixed, 16, 16, g, sems, 57))
    wout_gather.step()
    cotangent_all[s] = cotangent_ref[...]
    steps(columns_gather, tokens_in, wout_gather, columns_gather, wout_gather)
    experts = experts_ref[...].reshape(128, experts_ref.shape[2])

    @pl.loop(0, 8)
    def _(place):
        units = owner_units(place, experts.shape[1], 8)
        experts_tx[place] = nn(experts, units).astype(jnp.bfloat16)

    copies += exchange(experts_tx, experts_in, s, peers, at_seq, sems, 38)
    experts_in[s] = experts_tx[s]
    steps(columns_gather, wout_gather, tokens_in)
    cotangent_in = Task(ring_gather(cotangent_all, s, sems, 78))
    cotangent_in.step()
    run(columns_gather, wout_gather)
    out_copies = [pltpu.make_async_copy(weight_ref, weight_out, out_sems.at[8])]
    out_copies[0].start()
    pick = lax.broadcasted_iota(jnp.int32, (8, 2 * WIDTH), 0) + (SMALL - 2 * WIDTH)
    pick = (pick == lax.broadcasted_iota(jnp.int32, (8, 2 * WIDTH), 1)).astype(jnp.bfloat16)
    small_ref[...] = nt(pick, weight_ref[:, 2 * WIDTH : 4 * WIDTH])
    gain = small_ref[0:1, :]

    def project(place):
        values = all_ref[place].astype(jnp.float32)
        normed = (values * scale_of(values) * gain).astype(jnp.bfloat16)
        normed_ref[rows_at(place), :] = normed
        result = nn(normed, weight_ref[...]).astype(jnp.bfloat16)
        q_ref[rows_at(place), :] = result[:, :SMALL]
        window_ref[4, rows_at(place), :] = result[:, KEYS:]
        copy = pltpu.make_async_copy(
            normed_ref.at[rows_at(place)],
            normed_out.at[rows_at(place)],
            out_sems.at[len(out_copies) - 1],
        )
        copy.start()
        out_copies.append(copy)

    project(s)
    for name in ("down", "up", "far"):
        project(p[name])
    side = lax.div(s, RING)
    near = Task(window_steps(window_ref, rows_at(side, 512), g, sems, 53))
    near.step()
    project(p["over"])
    tokens_in.step()
    project(p["over_up"])
    project(p["over_down"])
    run(tokens_in)
    project(p["over_far"])
    away = Task(window_steps(window_ref, rows_at(1 - side, 512), g, sems, 74))
    away.step()
    steps(near, cotangent_in, away)
    for copy in copies[7:]:
        copy.wait_recv()
    for e in range(8):
        block = experts_in[:, e * 16 : (e + 1) * 16, :].reshape(128, 128)
        rows_ref[:, e * 128 : (e + 1) * 128] = compact(block, 12)
    run(wout_gather)
    wout_all_ref[...] = compact(mixed[...], 12)
    steps(near, cotangent_in, away)
    run_all(near, away, cotangent_in)
    out_copies.append(pltpu.make_async_copy(cotangent_all, cotangent_out, out_sems.at[9]))
    out_copies[-1].start()
    for copy in chosen_copies:
        copy.wait_recv()
    for copy in copies + chosen_copies:
        copy.wait_send()
    for copy in out_copies:
        copy.wait()


ANY = pl.BlockSpec(memory_space=pl.ANY)


def start(tokens, columns, experts, wout, chosen, cotangent):
    own, model = tokens.shape
    rows = 8 * own
    width = columns.shape[2]
    return pl.pallas_call(
        start_kernel,
        in_specs=[VMEM] * 6,
        out_specs=[ANY, VMEM, VMEM, ANY, VMEM, VMEM, VMEM, VMEM, ANY],
        out_shape=[
            array((rows, model)),
            array((rows, SMALL)),
            array((LOOK + 1, rows, width - KEYS)),
            array((model, width)),
            array((8, model), jnp.float32),
            array((96, experts.shape[2])),
            array((192, model)),
            array((8,) + chosen.shape, jnp.float32),
            array((8, own, model)),
        ],
        scratch_shapes=[
            pltpu.VMEM((8, own, model), jnp.bfloat16),
            pltpu.VMEM((rows, model), jnp.bfloat16),
            pltpu.VMEM((model, width), jnp.bfloat16),
            pltpu.VMEM(columns.shape, jnp.bfloat16),
            pltpu.VMEM((8, 128, 128), jnp.bfloat16),
            pltpu.VMEM((8, 128, 128), jnp.bfloat16),
            pltpu.VMEM((256, model), jnp.bfloat16),
            pltpu.VMEM((8, own, model), jnp.bfloat16),
            pltpu.SemaphoreType.DMA((10,)),
            *sem_pair(92),
        ],
        compiler_params=kernel_params(1),
        name="start",
    )(tokens, columns, experts, wout, chosen, cotangent)


def window_back_steps(d_ref, out_ref, rows, tx, rx, g, sems, base):
    core = lax.rem(g, 2)
    before, partner = at_fsdp(lax.rem(g + 14, 16)), at_fsdp(g + 1 - 2 * core)
    odd = core.astype(jnp.float32)
    even = 1.0 - odd

    def wide(slot):
        return rx[slot, rows, :].astype(jnp.float32)

    def go(slot, value, sem, target):
        tx[slot, rows, :] = value.astype(jnp.bfloat16)
        return send(tx.at[slot, rows], rx.at[slot, rows], sems, base + sem, target)

    one = go(1, d_ref[1, rows, :], 1, partner)
    two = go(2, d_ref[3, rows, :], 2, partner)
    yield
    one.wait_recv()
    zero = go(0, d_ref[0, rows, :] + odd * wide(1), 0, before)
    yield
    two.wait_recv()
    zero.wait_recv()
    value = d_ref[2, rows, :] + wide(0) + odd * wide(2) + even * wide(1)
    three = go(3, value, 3, before)
    yield
    three.wait_recv()
    out_ref[rows, :] = (d_ref[4, rows, :] + wide(3) + even * wide(2)).astype(jnp.bfloat16)
    for copy in (zero, one, two, three):
        copy.wait_send()


def moe_kernel(
    attended_ref, wout_ref, tokens_ref, small_ref, rows_ref, down_rows_ref, cotangent_in, chosen_ref,
    resid_ref, moe_out, d_resid_ref, d_attended_ref, router_ref, grad_wout_ref, part_gate_up_ref,
    part_down_ref,
    normed_ref, shared_ref, d_ref, branch_ref, cotangent_ref, gate_up_ref, down_mixed, down_ref,
    moe_ref, grad_gate_up, grad_down, grad_wout, probs_ref, share_tx, share_in, logits_ref,
    tx_a, rx_a, tx_b, rx_b,
    pair_a, tops_a, bottoms_a, full_a, pair_b, tops_b, bottoms_b, full_b,
    local_sems, send_sems, recv_sems,
):
    s, g = lax.axis_index("seq"), lax.axis_index("fsdp")
    p = ring_places(s)
    peers = others(s, 8)
    sems = (send_sems, recv_sems)
    cotangent_copy = pltpu.make_async_copy(cotangent_in, cotangent_ref, local_sems.at[0])
    cotangent_copy.start()
    greet([at_seq(q) for q in peers] + fsdp_neighbours(g))
    model = tokens_ref.shape[1]
    units = down_ref.shape[0]
    per = units // EXPERTS

    def branch_part(place):
        return nn(attended_ref[rows_at(place), :], wout_ref[...])

    branch_sum = Task(ring_scatter(branch_part, tx_a, rx_a, s, sems, 0))
    branch_sum.step()
    gate_up_ref[rows_at(g, 96), :] = rows_ref[...]
    gate_up_gather = Task(fsdp_gather(gate_up_ref, 96, 48, g, sems, 107))
    gate_up_gather.step()
    down_mixed[rows_at(g, 32), :] = down_rows_ref[...]
    down_gather = Task(fsdp_gather(down_mixed, 32, 16, g, sems, 124))
    down_gather.step()
    steps(gate_up_gather, down_gather, branch_sum)
    branch = run(branch_sum, gate_up_gather, down_gather)
    resid = tokens_ref[...].astype(jnp.float32) + branch
    resid_ref[...] = resid
    gain = small_ref[1:2, :]
    router = small_ref[...].astype(jnp.bfloat16)
    normed_ref[s] = (resid * scale_of(resid) * gain).astype(jnp.bfloat16)
    gather = Task(ring_gather(normed_ref, s, sems, 14))
    gather.step()
    run_all(gate_up_gather, down_gather)
    down_ref[...] = nn(unit_order(0), down_mixed[...]).astype(jnp.bfloat16)
    cotangent_copy.wait()

    def block(place):
        x = normed_ref[place]
        logits = nt(router, x)
        logits = jnp.concatenate([logits[2 : 2 + EXPERTS], jnp.full((4, 128), NEGATIVE)], axis=0)
        probs = jnp.exp(logits - jnp.max(logits, axis=0, keepdims=True))
        probs = probs / jnp.sum(probs, axis=0, keepdims=True)
        probs_ref[place] = probs
        share = jnp.concatenate([probs * chosen_ref[place], jnp.zeros((120, 128))], axis=0)
        share = jnp.transpose(share)
        plain = nt(cotangent_ref[place], down_ref[...])
        both = nn(x, gate_up_ref[...])
        sums = []
        for e in range(EXPERTS):
            at = slice(e * per, (e + 1) * per)
            gate, up = both[:, at], both[:, units + e * per : units + (e + 1) * per]
            wide = jnp.broadcast_to(share[:, e : e + 1], gate.shape)
            sigmoid = 1.0 / (1.0 + jnp.exp(-gate))
            silu = gate * sigmoid
            hidden = (silu * up).astype(jnp.bfloat16).astype(jnp.float32)
            shared_ref[rows_at(place), at] = (hidden * wide).astype(jnp.bfloat16)
            sums.append(jnp.sum(plain[:, at] * hidden, axis=1, keepdims=True))
            d_hidden = plain[:, at] * wide
            d_gate = d_hidden * up * sigmoid * (1.0 + gate * (1.0 - sigmoid))
            d_ref[rows_at(place), at] = d_gate.astype(jnp.bfloat16)
            d_ref[rows_at(place), units + e * per : units + (e + 1) * per] = (
                d_hidden * silu
            ).astype(jnp.bfloat16)
        sums = jnp.concatenate(sums + [jnp.zeros((128, 128 - EXPERTS))], axis=1)
        share_tx[place] = jnp.transpose(sums)[:8]

    block(s)
    gather.step()
    block(p["down"])
    block(p["up"])
    gather.step()
    block(p["over"])
    block(p["far"])
    gather.step()
    late = [p["over_up"], p["over_down"], p["over_far"]]

    moe_copy = pltpu.make_async_copy(moe_ref, moe_out, local_sems.at[1])

    def weight_grads():
        @pl.loop(0, model // 128)
        def _(j):
            normed = normed_ref[:, :, rows_at(j)].reshape(8 * 128, 128)
            grad_gate_up[rows_at(j), :] = tn(normed, d_ref[...]).astype(jnp.bfloat16)

        gate_up_sum = Task(
            fsdp_scatter(
                grad_gate_up, 96, 48, (pair_a, tops_a, bottoms_a, full_a), g, sems, 59
            )
        )
        gate_up_sum.step()
        yield
        gate_up_sum.step()
        shared, grad = shared_ref[...], cotangent_ref[...].reshape(8 * 128, model)
        value = tn(shared, grad).astype(jnp.bfloat16)
        grad_down[...] = nn(unit_order(1), value).astype(jnp.bfloat16)
        down_sum = Task(
            fsdp_scatter(
                grad_down, 32, 16, (pair_b, tops_b, bottoms_b, full_b), g, sems, 76
            )
        )
        down_sum.step()
        yield
        gate_up_sum.step()
        down_sum.step()
        moe_ref[...] = nn(shared_ref[...], down_ref[...]).astype(jnp.bfloat16)
        moe_copy.start()
        yield
        while not (down_sum.done and gate_up_sum.done):
            gate_up_sum.step()
            down_sum.step()
            yield
        part_gate_up_ref[...] = gate_up_sum.value.astype(jnp.bfloat16)
        part_down_ref[...] = down_sum.value.astype(jnp.bfloat16)

    grads = Task(weight_grads())

    def normed_part(place):
        if late:
            late.pop(0)
            if not late:
                run(gather)
            block(place)
        return nt(d_ref[rows_at(place), :], gate_up_ref[...])

    d_normed_sum = Task(ring_scatter(normed_part, tx_b, rx_b, s, sems, 42))
    d_normed_sum.step()
    shares = exchange(share_tx, share_in, s, peers, at_seq, sems, 28)
    share_in[s] = share_tx[s]
    grads.step()
    steps(d_normed_sum, d_normed_sum, grads, d_normed_sum, grads)
    d_normed = run(d_normed_sum)
    for copy in shares:
        copy.wait_recv()

    d_router = jnp.sum(share_in[...], axis=0) * chosen_ref[s]
    probs = probs_ref[s]
    d_logits = probs * (d_router - jnp.sum(probs * d_router, axis=0, keepdims=True))
    d_logits = d_logits.astype(jnp.bfloat16)
    logits_ref[s] = d_logits.astype(jnp.float32)
    spreads = spread(logits_ref.at[s], logits_ref, s, peers, at_seq, sems, 35)
    padded = jnp.concatenate([jnp.zeros((2, 128), jnp.bfloat16), d_logits[:6]], axis=0)
    d_normed = d_normed + tn(padded, router)
    resid = resid_ref[...]
    scale = scale_of(resid)
    d_resid = cotangent_ref[s].astype(jnp.float32) + rms_back(
        d_normed, resid * scale, scale, gain
    )
    d_resid_ref[...] = d_resid
    branch_ref[s] = d_resid.astype(jnp.bfloat16)
    gather = Task(ring_gather(branch_ref, s, sems, 93))
    gather.step()

    grad_wout[...] = jnp.zeros_like(grad_wout)

    def d_attended(place):
        d_branch = branch_ref[place]
        d_attended_ref[rows_at(place), :] = nt(d_branch, wout_ref[...]).astype(jnp.bfloat16)
        grad_wout[...] += tn(attended_ref[rows_at(place), :], d_branch)

    d_attended(s)
    gather.step()
    steps(grads)
    for name in ("down", "up", "over"):
        d_attended(p[name])
    steps(grads, gather)
    for copy in spreads:
        copy.wait_recv()
    total = jnp.zeros((8, model), jnp.float32)
    for q in range(8):
        total += nn(logits_ref[q].astype(jnp.bfloat16), normed_ref[q])
    router_ref[...] = total
    d_attended(p["far"])
    steps(grads, gather)
    d_attended(p["over_up"])
    d_attended(p["over_down"])
    run(grads)
    run(gather)
    d_attended(p["over_far"])
    grad_wout_ref[...] = expand(grad_wout[...].astype(jnp.bfloat16), 12)
    moe_copy.wait()
    for copy in shares + spreads:
        copy.wait_send()


def moe(attended, wout, tokens, small, rows, down_rows, cotangent, chosen):
    own, model = tokens.shape
    group = 8 * own
    width, units = rows.shape[1], 16 * down_rows.shape[0]
    f32, bf16 = jnp.float32, jnp.bfloat16
    tiny = pltpu.VMEM((8, 8, own), f32)
    return pl.pallas_call(
        moe_kernel,
        in_specs=[VMEM] * 6 + [ANY, VMEM],
        out_specs=[VMEM, ANY] + [VMEM] * 6,
        out_shape=[
            array((own, model), f32),
            array((group, model)),
            array((own, model), f32),
            array((group, SMALL)),
            array((8, model), f32),
            array((256, model)),
            array((model // 16, width)),
            array((units // 16, model)),
        ],
        scratch_shapes=[
            pltpu.VMEM((8, own, model), bf16),
            pltpu.VMEM((group, units), bf16),
            pltpu.VMEM((group, width), bf16),
            pltpu.VMEM((8, own, model), bf16),
            pltpu.VMEM((8, own, model), bf16),
            pltpu.VMEM((model, width), bf16),
            pltpu.VMEM((units, model), bf16),
            pltpu.VMEM((units, model), bf16),
            pltpu.VMEM((group, model), bf16),
            pltpu.VMEM((model, width), bf16),
            pltpu.VMEM((units, model), bf16),
            pltpu.VMEM((192, model), f32),
            tiny,
            tiny,
            tiny,
            tiny,
            *ring_buffers(own, model),
            *ring_buffers(own, model),
            *fsdp_buffers(model // 16, 48, width),
            *fsdp_buffers(units // 16, 16, model),
            pltpu.SemaphoreType.DMA((2,)),
            *sem_pair(141),
        ],
        compiler_params=kernel_params(2),
        name="moe",
    )(attended, wout, tokens, small, rows, down_rows, cotangent, chosen)


def finish_kernel(
    dq_ref, d_window_ref, weight_in, normed_in, wout_ref, router_ref, experts_ref, d_resid_ref,
    tokens_ref, small_ref,
    grad_input_ref, query_out, key_out, gate_out, up_out, wout_out,
    weight_ref, normed_ref, d_ref, query_grads, key_grads, wout_grads, query_tx, key_tx, experts_tx,
    experts_in, wout_tx, wtx, wrx, tx, rx,
    pair_a, tops_a, bottoms_a, full_a, pair_b, tops_b, bottoms_b, full_b,
    pair_c, tops_c, bottoms_c, full_c,
    local_sems, send_sems, recv_sems,
):
    s, g = lax.axis_index("seq"), lax.axis_index("fsdp")
    peers = others(s, 8)
    sems = (send_sems, recv_sems)
    normed_copy = pltpu.make_async_copy(normed_in, normed_ref, local_sems.at[0])
    normed_copy.start()
    weight_copy = pltpu.make_async_copy(weight_in, weight_ref, local_sems.at[1])
    weight_copy.start()
    holder, owner = head_holder(g, s), head_owner(g, s)
    alone = (holder["fsdp"] == g) & (holder["seq"] == s)
    greet_all(
        [at_seq(q) for q in peers] + fsdp_neighbours(g) + window_greeting(g),
        (holder, owner),
        alone,
    )
    d_keyval = d_ref.at[:, KEYS:]
    halves = [
        Task(window_back_steps(d_window_ref, d_keyval, pl.ds(k * 512, 512), wtx, wrx, g, sems, 4 * k))
        for k in range(2)
    ]

    def windows():
        for half in halves:
            half.step()

    windows()
    d_ref[:, :SMALL] = dq_ref[...]
    d_ref[:, SMALL:KEYS] = jnp.zeros((d_ref.shape[0], WIDTH), jnp.bfloat16)
    windows()
    experts_tx[...] = expand(experts_ref[...], 12).reshape(experts_tx.shape)
    copies = exchange(experts_tx, experts_in, s, peers, at_seq, sems, 8)
    experts_in[s] = experts_tx[s]
    wout_grads[...] = wout_ref[...]
    wout = Task(
        fsdp_scatter(wout_grads, 16, 16, (pair_b, tops_b, bottoms_b, full_b), g, sems, 32)
    )
    wout.step()
    model = normed_ref.shape[1]
    normed_copy.wait()

    def weight_grad(columns):
        return tn(d_ref[:, columns], normed_ref[...])

    value = weight_grad(slice(0, KEYS))
    row = lax.broadcasted_iota(jnp.int32, (KEYS, 1), 0)
    router = jnp.concatenate(
        [jnp.zeros((SMALL + 2, model)), router_ref[...], jnp.zeros((KEYS - SMALL - 10, model))], axis=0
    )
    query_grads[...] = jnp.transpose(jnp.where(row < SMALL, value, router)).astype(jnp.bfloat16)
    windows()
    query = Task(
        fsdp_scatter(query_grads, 96, 48, (pair_a, tops_a, bottoms_a, full_a), g, sems, 15)
    )
    steps(wout, query, wout, query)
    weight_copy.wait()
    run_all(*halves)

    def partial(place):
        return nt(d_ref[rows_at(place), :], weight_ref[...])

    total = Task(ring_scatter(partial, tx, rx, s, sems, 49))
    total.step()
    key_grads[...] = jnp.transpose(weight_grad(slice(KEYS, KEYS + 2 * WIDTH))).astype(jnp.bfloat16)
    key = Task(fsdp_scatter(key_grads, 96, 48, (pair_c, tops_c, bottoms_c, full_c), g, sems, 63))
    key.step()
    steps(query, key, query, key)
    steps(total, total)
    run(query, key)
    query_tx[...] = expand(query.value.astype(jnp.bfloat16), 12).reshape(query_tx.shape)
    copies.extend(exchange(query_tx, query_out, s, peers, at_seq, sems, 80))
    query_out[s] = query_tx[s]
    steps(key)
    total.step()
    run(key, wout)
    key_tx[...] = expand(key.value.astype(jnp.bfloat16), 12).reshape(key_tx.shape)
    copies.extend(exchange(key_tx, key_out, s, peers, at_seq, sems, 87))
    key_out[s] = key_tx[s]
    run(wout)
    wout_tx[...] = wout.value.astype(jnp.bfloat16)
    wait_rows = swap_rows(wout_tx, wout_out, sems, 94, owner, alone)
    for copy in copies[:7]:
        copy.wait_recv()
    units = experts_ref.shape[1] // 8
    back = jnp.zeros((128, gate_out.shape[2]), jnp.float32)
    for place in range(8):
        block = jnp.concatenate(
            [experts_in[place, :, e * units : (e + 1) * units] for e in range(8)], axis=0
        )
        back += nt(block, owner_units(place, gate_out.shape[2], 8))
    for e in range(EXPERTS):
        gate_out[e] = back[e * 16 : e * 16 + 12]
        up_out[e] = back[(EXPERTS + e) * 16 : (EXPERTS + e) * 16 + 12]
    d_normed = run(total)
    values = tokens_ref[...].astype(jnp.float32)
    scale = scale_of(values)
    grad_input_ref[...] = d_resid_ref[...] + rms_back(
        d_normed, values * scale, scale, small_ref[0:1, :]
    )
    wait_rows()
    for copy in copies[7:]:
        copy.wait_recv()
    for copy in copies:
        copy.wait_send()


def finish(dq, d_window, weight, normed, wout, router, experts, d_resid, tokens, small):
    own, model = tokens.shape
    rows = dq.shape[0]
    width = weight.shape[1]
    blocks = (8, 16, experts.shape[1])
    keyval = d_window.shape[1:]
    bf16, f32 = jnp.bfloat16, jnp.float32
    return pl.pallas_call(
        finish_kernel,
        in_specs=[VMEM, VMEM, ANY, ANY] + [VMEM] * 6,
        out_specs=[VMEM] * 6,
        out_shape=[
            array((own, model), f32),
            array((8, 16, KEYS)),
            array((8, 16, width - KEYS)),
            array((EXPERTS, 12, experts.shape[1]), f32),
            array((EXPERTS, 12, experts.shape[1]), f32),
            array((16, model)),
        ],
        scratch_shapes=[
            pltpu.VMEM(weight.shape, bf16),
            pltpu.VMEM(normed.shape, bf16),
            pltpu.VMEM((rows, width), bf16),
            pltpu.VMEM((model, KEYS), bf16),
            pltpu.VMEM((model, width - KEYS), bf16),
            pltpu.VMEM((256, model), bf16),
            pltpu.VMEM((8, 16, KEYS), bf16),
            pltpu.VMEM((8, 16, width - KEYS), bf16),
            pltpu.VMEM(blocks, bf16),
            pltpu.VMEM(blocks, bf16),
            pltpu.VMEM((16, model), bf16),
            pltpu.VMEM((4,) + keyval, bf16),
            pltpu.VMEM((4,) + keyval, bf16),
            *ring_buffers(own, model),
            *fsdp_buffers(model // 16, 48, KEYS),
            *fsdp_buffers(16, 16, model),
            *fsdp_buffers(model // 16, 48, width - KEYS),
            pltpu.SemaphoreType.DMA((2,)),
            *sem_pair(95),
        ],
        compiler_params=kernel_params(3),
        name="finish",
    )(dq, d_window, weight, normed, wout, router, experts, d_resid, tokens, small)


def pad_rows(x, axis):
    pads = [(0, 0)] * x.ndim
    pads[axis] = (0, 16 - x.shape[axis])
    return jnp.pad(x, pads)


def on_device(
    tokens,
    gain_one,
    w_qkv,
    w_out,
    gain_two,
    w_router,
    w_gate,
    w_up,
    w_down,
    doc_starts,
    routes,
    cotangent,
):
    seq = lax.axis_size("seq")
    group_index = lax.axis_index("fsdp")
    own, model = tokens.shape
    group_rows = own * seq
    experts, own_model, ff = w_gate.shape
    bf16, f32 = jnp.bfloat16, jnp.float32

    gate_up = pad_rows(jnp.concatenate([w_gate, w_up], axis=0), 1)
    qkv_parts = jnp.transpose(w_qkv.reshape(own_model, seq, 5 * WIDTH), (1, 0, 2))
    small = jnp.concatenate([gain_one[:, None], gain_two[:, None], w_router], axis=1)
    small = jnp.pad(small, ((0, 0), (0, WIDTH - small.shape[1])))
    columns = jnp.concatenate(
        [
            qkv_parts[:, :, :SMALL],
            jnp.broadcast_to(small[None], (seq,) + small.shape),
            qkv_parts[:, :, SMALL:],
        ],
        axis=2,
    )
    expert_ids = jnp.arange(8, dtype=jnp.int32)
    chosen = jnp.sum((routes[None, :, :] == expert_ids[:, None, None]).astype(f32), axis=2)
    normed_one, queries, window, weight, small, rows, out_weight, chosen, cotangent_all = start(
        tokens, pad_rows(columns, 1), gate_up, pad_rows(w_out, 0), chosen, cotangent
    )

    window = window.reshape((LOOK + 1) * group_rows, 2 * WIDTH)
    positions = group_index * group_rows + jnp.arange(group_rows, dtype=jnp.int32)
    begins = jnp.max(
        jnp.where(doc_starts[:, None] <= positions[None, :], doc_starts[:, None], 0), axis=0
    )
    lo = begins - (group_index - LOOK) * group_rows
    blocks = group_rows // BQ
    lo_blocks = lo.reshape(blocks, BQ)
    ends = LOOK * group_rows + jnp.arange(blocks, dtype=jnp.int32) * BQ

    def bounds(step):
        diag = ends // step
        first = jnp.minimum(lo_blocks[:, 0] // step, diag)
        full = jnp.minimum((lo_blocks[:, -1] + step - 1) // step, diag)
        return jnp.stack([first, full, diag, (ends + BQ + step - 1) // step], axis=1)

    attended, lse = attention(bounds(BK), lo[None, :], queries, window)

    residual, moe_out, d_resid, d_attended, grad_router, grad_w_out, part_gate_up, part_down = moe(
        attended, out_weight, tokens, small, rows, w_down.reshape(-1, model), cotangent_all, chosen
    )
    moe_out = lax.psum_scatter(moe_out, "seq", scatter_dimension=0, tiled=True)
    output = (residual + moe_out.astype(f32)).astype(bf16)

    d_queries, d_window = attention_back(
        bounds(BK_BACK), lo[None, :], queries, window, attended, d_attended, lse
    )
    grad_input, query_grads, key_grads, shard_gate, shard_up, shard_out = finish(
        d_queries,
        d_window.reshape(LOOK + 1, group_rows, 2 * WIDTH),
        weight, normed_one, grad_w_out, grad_router, part_gate_up, d_resid, tokens, small,
    )

    shard_down = part_down.astype(f32).reshape(experts, -1, model)
    shard_out = shard_out[:own_model].astype(f32)
    shard_qkv = jnp.concatenate([query_grads[:, :own_model, :SMALL], key_grads[:, :own_model]], axis=2)
    shard_qkv = jnp.transpose(shard_qkv, (1, 0, 2)).reshape(own_model, -1).astype(f32)
    shard_router = query_grads[0, :own_model, SMALL + 2 : SMALL + 2 + experts].astype(f32)

    shard_gain_one = jnp.sum(w_qkv.astype(f32) * shard_qkv, axis=1)
    shard_gain_one = shard_gain_one / gain_one.astype(f32)
    shard_gain_two = jnp.sum(w_router.astype(f32) * shard_router, axis=1)
    shard_gain_two += jnp.sum(w_gate.astype(f32) * shard_gate, axis=(0, 2))
    shard_gain_two += jnp.sum(w_up.astype(f32) * shard_up, axis=(0, 2))
    shard_gain_two = shard_gain_two / gain_two.astype(f32)
    return (
        output,
        grad_input,
        shard_gain_one,
        shard_qkv,
        shard_out,
        shard_gain_two,
        shard_router,
        shard_gate,
        shard_up,
        shard_down,
    )


def solution(mesh):
    rows, vector = P(BOTH, None), P(BOTH)
    middle = P(None, BOTH, None)
    in_specs = (
        rows, vector, rows, rows, vector, rows, middle, middle, middle, P(), rows, rows,
    )
    out_specs = (rows, rows, vector, rows, rows, vector, rows, middle, middle, middle)
    return jax.shard_map(
        on_device, mesh=mesh, in_specs=in_specs, out_specs=out_specs, check_vma=False
    )
```

```python
import functools

import jax
import jax.numpy as jnp
from jax import lax
from jax.experimental import pallas as pl
from jax.experimental.pallas import tpu as pltpu
from jax.sharding import PartitionSpec as P

WIDTH = 64
LOOK = 4
EXPERTS = 4
EPS = 1e-06
NEGATIVE = -1e30
BQ = 256
BK = 1024
BK_BACK = 512
BOTH = ("fsdp", "seq")


def nt(a, b):
    return lax.dot_general(a, b, (((1,), (1,)), ((), ())), preferred_element_type=jnp.float32)


def tn(a, b):
    return lax.dot_general(a, b, (((0,), (0,)), ((), ())), preferred_element_type=jnp.float32)


def nn(a, b):
    return jnp.dot(a, b, preferred_element_type=jnp.float32)


def stack_heads(rows, low):
    heads = rows.shape[1] // WIDTH
    zero = jnp.zeros((rows.shape[0], WIDTH), rows.dtype)
    parts = []
    for h in range(heads):
        part = rows[:, h * WIDTH : (h + 1) * WIDTH]
        parts.append(jnp.concatenate([part, zero] if low else [zero, part], axis=1))
    return jnp.concatenate(parts, axis=0)


def chunk_loops(bounds_ref, step):
    b = pl.program_id(0)
    first, full, diag, end = (bounds_ref[b, i] for i in range(4))
    pl.loop(first, full)(lambda c: step(c, True))
    pl.loop(full, diag)(lambda c: step(c, False))
    pl.loop(diag, end)(lambda c: step(c, True))


def attention_kernel(
    bounds_ref, lo_ref, q_ref, kv_ref, out_ref, lse_ref, m_ref, acc_ref, ones_ref
):
    heads = q_ref.shape[1] // WIDTH
    queries = stack_heads(q_ref[...] * 0.125, True)
    m_ref[...] = jnp.full_like(m_ref, NEGATIVE)
    acc_ref[...] = jnp.zeros_like(acc_ref)

    @pl.when(pl.program_id(0) == 0)
    def _():
        lane = lax.broadcasted_iota(jnp.int32, kv_ref.shape, 1)
        ones_ref[...] = jnp.where(lane < WIDTH, jnp.ones_like(kv_ref[...]), kv_ref[...])

    base = LOOK * 1024 + pl.program_id(0) * BQ

    def step(c, masked):
        start = pl.multiple_of(c * BK, BK)
        rows = kv_ref[pl.ds(start, BK), :]
        scores = nt(rows, queries)
        if masked:
            key = start + lax.broadcasted_iota(jnp.int32, (BK, BQ), 0)
            query = base + lax.broadcasted_iota(jnp.int32, (BK, BQ), 1)
            seen = (key >= lo_ref[...]) & (key <= query)
            scores = jnp.where(jnp.concatenate([seen] * heads, axis=1), scores, NEGATIVE)
        old = m_ref[...]
        new = jnp.maximum(old, jnp.max(scores, axis=0, keepdims=True))
        probs = jnp.exp(scores - new).astype(jnp.bfloat16)
        fade = jnp.exp(old - new)
        m_ref[...] = new
        acc_ref[...] = acc_ref[...] * fade + tn(ones_ref[pl.ds(start, BK), :], probs)

    chunk_loops(bounds_ref, step)
    total = acc_ref[:1, :]
    result = jnp.transpose(acc_ref[...] / total)
    out_ref[...] = jnp.concatenate(
        [result[h * BQ : (h + 1) * BQ, WIDTH:] for h in range(heads)], axis=1
    ).astype(jnp.bfloat16)
    lse_ref[...] = jnp.broadcast_to(m_ref[...] + jnp.log(total), lse_ref.shape)


def attention(bounds, lo, q, kv):
    rows, width = q.shape
    heads = width // WIDTH
    blocks = rows // BQ
    return pl.pallas_call(
        attention_kernel,
        grid=(blocks,),
        in_specs=[
            pl.BlockSpec(memory_space=pltpu.SMEM),
            pl.BlockSpec((1, BQ), lambda b: (0, b)),
            pl.BlockSpec((BQ, width), lambda b: (b, 0)),
            pl.BlockSpec(memory_space=pltpu.VMEM),
        ],
        out_specs=[
            pl.BlockSpec((BQ, width), lambda b: (b, 0)),
            pl.BlockSpec((None, 8, heads * BQ), lambda b: (b, 0, 0)),
        ],
        out_shape=[
            jax.ShapeDtypeStruct((rows, width), jnp.bfloat16),
            jax.ShapeDtypeStruct((blocks, 8, heads * BQ), jnp.float32),
        ],
        scratch_shapes=[
            pltpu.VMEM((1, heads * BQ), jnp.float32),
            pltpu.VMEM((2 * WIDTH, heads * BQ), jnp.float32),
            pltpu.VMEM(kv.shape, jnp.bfloat16),
        ],
        compiler_params=pltpu.CompilerParams(vmem_limit_bytes=48 << 20),
        cost_estimate=pl.CostEstimate(
            flops=4 * rows * 4096 * width, bytes_accessed=4 << 20, transcendentals=rows * 4096 * 3
        ),
        name="attention",
    )(bounds, lo, q, kv)


def attention_back_kernel(
    bounds_ref, lo_ref, q_ref, kv_ref, out_ref, dout_ref, lse_ref, dq_ref, dkv_ref, acc_ref
):
    heads = q_ref.shape[1] // WIDTH
    queries = stack_heads(q_ref[...] * 0.125, True)
    douts = stack_heads(dout_ref[...], False)
    outs = stack_heads(out_ref[...], False)
    delta = jnp.sum(
        jnp.transpose(douts.astype(jnp.float32) * outs.astype(jnp.float32)), axis=0, keepdims=True
    )
    lse = lse_ref[:1, :]
    acc_ref[...] = jnp.zeros_like(acc_ref)
    base = LOOK * 1024 + pl.program_id(0) * BQ

    @pl.when(pl.program_id(0) == 0)
    def _():
        dkv_ref[...] = jnp.zeros_like(dkv_ref)

    def step(c, masked):
        start = pl.multiple_of(c * BK_BACK, BK_BACK)
        rows = kv_ref[pl.ds(start, BK_BACK), :]
        scores = nt(rows, queries)
        if masked:
            key = start + lax.broadcasted_iota(jnp.int32, (BK_BACK, BQ), 0)
            query = base + lax.broadcasted_iota(jnp.int32, (BK_BACK, BQ), 1)
            seen = (key >= lo_ref[...]) & (key <= query)
            scores = jnp.where(jnp.concatenate([seen] * heads, axis=1), scores, NEGATIVE)
        probs = jnp.exp(scores - lse)
        d_scores = (probs * (nt(rows, douts) - delta)).astype(jnp.bfloat16)
        dkv_ref[pl.ds(start, BK_BACK), :] += nn(d_scores, queries) + nn(
            probs.astype(jnp.bfloat16), douts
        )
        acc_ref[...] += tn(rows, d_scores)

    chunk_loops(bounds_ref, step)
    result = jnp.transpose(acc_ref[...]) * 0.125
    dq_ref[...] = jnp.concatenate(
        [result[h * BQ : (h + 1) * BQ, :WIDTH] for h in range(heads)], axis=1
    ).astype(jnp.bfloat16)


def attention_back(bounds, lo_row, q, kv, out, dout, lse):
    rows, width = q.shape
    heads = width // WIDTH
    blocks = rows // BQ
    row_block = pl.BlockSpec((BQ, width), lambda b: (b, 0))
    return pl.pallas_call(
        attention_back_kernel,
        grid=(blocks,),
        in_specs=[
            pl.BlockSpec(memory_space=pltpu.SMEM),
            pl.BlockSpec((1, BQ), lambda b: (0, b)),
            row_block,
            pl.BlockSpec(memory_space=pltpu.VMEM),
            row_block,
            row_block,
            pl.BlockSpec((None, 8, heads * BQ), lambda b: (b, 0, 0)),
        ],
        out_specs=[
            row_block,
            pl.BlockSpec(kv.shape, lambda b: (0, 0)),
        ],
        out_shape=[
            jax.ShapeDtypeStruct((rows, width), jnp.bfloat16),
            jax.ShapeDtypeStruct(kv.shape, jnp.float32),
        ],
        scratch_shapes=[pltpu.VMEM((2 * WIDTH, heads * BQ), jnp.float32)],
        compiler_params=pltpu.CompilerParams(vmem_limit_bytes=48 << 20),
        cost_estimate=pl.CostEstimate(
            flops=10 * rows * 4096 * width, bytes_accessed=8 << 20, transcendentals=rows * 4096 * 3
        ),
        name="attention_back",
    )(bounds, lo_row, q, kv, out, dout, lse)


RING = 4
MESH = pl.DeviceIdType.MESH
VMEM = pl.BlockSpec(memory_space=pltpu.VMEM)


def at_seq(index):
    return {"seq": index}


def at_fsdp(index):
    return {"fsdp": index}


def ring_places(s):
    x, y = lax.div(s, RING), lax.rem(s, RING)

    def place(dx, dy):
        return lax.rem(x + dx, 2) * RING + lax.rem(y + dy, RING)

    return {
        "up": place(0, 1),
        "down": place(0, 3),
        "far": place(0, 2),
        "over": place(1, 0),
        "over_up": place(1, 1),
        "over_down": place(1, 3),
        "over_far": place(1, 2),
    }


def greet(targets):
    barrier = pltpu.get_barrier_semaphore()
    for target in targets:
        pl.semaphore_signal(barrier, inc=1, device_id=target, device_id_type=MESH)
    pl.semaphore_wait(barrier, len(targets))


def send(src, dst, sems, index, target):
    copy = pltpu.make_async_remote_copy(
        src_ref=src,
        dst_ref=dst,
        send_sem=sems[0].at[index],
        recv_sem=sems[1].at[index],
        device_id=target,
        device_id_type=MESH,
    )
    copy.start()
    return copy


def steps(*tasks):
    for task in tasks:
        task.step()


class Task:
    def __init__(self, steps):
        self.steps, self.done, self.value = steps, False, None

    def step(self):
        if not self.done:
            try:
                next(self.steps)
            except StopIteration as end:
                self.done, self.value = True, end.value


def run(task, *beside):
    while not task.done:
        task.step()
        for other in beside:
            other.step()
    return task.value


def run_all(*tasks):
    while not all(task.done for task in tasks):
        for task in tasks:
            task.step()


RING_SEMS = 14


def ring_gather(out, s, sems, base):
    p = ring_places(s)
    half = out.shape[1] // 2
    top, bottom = pl.ds(0, half), pl.ds(half, half)
    up, down, over = at_seq(p["up"]), at_seq(p["down"]), at_seq(p["over"])
    copies = []

    def go(place, rows, target):
        block = out.at[place, rows]
        copies.append(send(block, block, sems, base + len(copies), target))
        return copies[-1]

    up_top, down_bottom = go(s, top, up), go(s, bottom, down)
    over_top, over_bottom = go(s, top, over), go(s, bottom, over)
    up_bottom, down_top = go(s, bottom, up), go(s, top, down)
    yield
    up_top.wait_recv()
    far_top = go(p["down"], top, up)
    down_bottom.wait_recv()
    far_bottom = go(p["up"], bottom, down)
    over_top.wait_recv()
    side = [go(p["over"], top, up), go(p["over"], top, down)]
    over_bottom.wait_recv()
    side += [go(p["over"], bottom, up), go(p["over"], bottom, down)]
    up_bottom.wait_recv()
    down_top.wait_recv()
    yield
    far_top.wait_recv()
    side.append(go(p["far"], top, over))
    far_bottom.wait_recv()
    side.append(go(p["far"], bottom, over))
    yield
    for copy in side[:4]:
        copy.wait_recv()
    yield
    for copy in side[4:]:
        copy.wait_recv()
    for copy in copies:
        copy.wait_send()


def ring_scatter(partial, tx, rx, s, sems, base):
    p = ring_places(s)
    half = tx.shape[1] // 2
    top, bottom = pl.ds(0, half), pl.ds(half, half)
    up, down, over = at_seq(p["up"]), at_seq(p["down"]), at_seq(p["over"])
    copies = []

    def cut(value, rows):
        return value[:half] if rows is top else value[half:]

    def go(slot, rows, value, target):
        tx[slot, rows, :] = value.astype(tx.dtype)
        copies.append(
            send(tx.at[slot, rows], rx.at[slot, rows], sems, base + len(copies), target)
        )
        return copies[-1]

    def wide(slot, rows):
        return rx[slot, rows, :].astype(jnp.float32)

    value = partial(p["over_up"])
    second = [go(1, rows, cut(value, rows), up) for rows in (top, bottom)]
    value = partial(p["over_down"])
    third = [go(2, rows, cut(value, rows), down) for rows in (top, bottom)]
    value = partial(p["over_far"])
    first = [go(0, rows, cut(value, rows), over) for rows in (top, bottom)]
    value = partial(p["far"])
    yield
    first[0].wait_recv()
    to_down = go(3, top, cut(value, top) + wide(0, top), down)
    first[1].wait_recv()
    to_up = go(3, bottom, cut(value, bottom) + wide(0, bottom), up)
    to_owner_down, to_owner_up = partial(p["down"]), partial(p["up"])
    fifth = [go(5, bottom, cut(to_owner_down, bottom), down)]
    sixth = [go(6, top, cut(to_owner_up, top), up)]
    value = partial(p["over"])
    yield
    fourth = []
    for k, rows in enumerate((top, bottom)):
        second[k].wait_recv()
        third[k].wait_recv()
        fourth.append(go(4, rows, cut(value, rows) + wide(1, rows) + wide(2, rows), over))
    yield
    to_down.wait_recv()
    fifth.append(go(5, top, cut(to_owner_down, top) + wide(3, top), down))
    to_up.wait_recv()
    sixth.append(go(6, bottom, cut(to_owner_up, bottom) + wide(3, bottom), up))
    value = partial(s)
    yield
    for copy in fourth + fifth + sixth:
        copy.wait_recv()
    value = value + (rx[4].astype(jnp.float32) + rx[5].astype(jnp.float32))
    value = value + rx[6].astype(jnp.float32)
    for copy in copies:
        copy.wait_send()
    return value


def ring_buffers(rows, width):
    return [pltpu.VMEM((7, rows, width), jnp.bfloat16)] * 2


def fsdp_place(g):
    x, z, core = lax.div(g, 8), lax.rem(lax.div(g, 2), RING), lax.rem(g, 2)

    def place(dx, dz, dcore):
        return (
            lax.rem(x + dx, 2) * 8 + lax.rem(z + dz, RING) * 2 + lax.rem(core + dcore, 2)
        )

    return place


def fsdp_neighbours(g):
    place = fsdp_place(g)
    return [at_fsdp(place(*d)) for d in ((1, 0, 0), (0, 1, 0), (0, 3, 0), (0, 0, 1))]


def part_of(ref, rows, cut):
    def view(index, half=None):
        first, count = {None: (0, rows), "top": (0, cut), "bottom": (cut, rows - cut)}[half]
        return ref.at[pl.ds(pl.multiple_of(index * rows + first, 16), count)]

    return view


def fsdp_gather(ref, rows, cut, g, sems, base):
    view, place = part_of(ref, rows, cut), fsdp_place(g)
    over, up, down, pal = fsdp_neighbours(g)
    copies = []

    def go(index, half, sem, target):
        copies.append(send(view(index, half), view(index, half), sems, base + sem, target))
        return copies[-1]

    me = place(0, 0, 0)
    to_over = go(me, None, 16, over)
    to_up, to_down = go(me, None, 0, up), go(me, None, 1, down)
    pals = [go(me, None, 8, pal)]
    yield
    to_over.wait_recv()
    side = place(1, 0, 0)
    side_up, side_down = go(side, None, 2, up), go(side, None, 3, down)
    pals.append(go(side, None, 9, pal))
    yield
    to_up.wait_recv()
    far_up = go(place(0, 3, 0), "top", 4, up)
    pals.append(go(place(0, 3, 0), None, 10, pal))
    to_down.wait_recv()
    far_down = go(place(0, 1, 0), "bottom", 5, down) if cut < rows else None
    pals.append(go(place(0, 1, 0), None, 11, pal))
    yield
    side_up.wait_recv()
    side_far_up = go(place(1, 3, 0), "top", 6, up)
    pals.append(go(place(1, 3, 0), None, 12, pal))
    side_down.wait_recv()
    side_far_down = go(place(1, 1, 0), "bottom", 7, down) if cut < rows else None
    pals.append(go(place(1, 1, 0), None, 13, pal))
    yield
    far_up.wait_recv()
    if far_down is not None:
        far_down.wait_recv()
    pals.append(go(place(0, 2, 0), None, 14, pal))
    yield
    side_far_up.wait_recv()
    if side_far_down is not None:
        side_far_down.wait_recv()
    pals.append(go(place(1, 2, 0), None, 15, pal))
    yield
    for copy in pals:
        copy.wait_recv()
    for copy in copies:
        copy.wait_send()


def fsdp_buffers(rows, cut, width):
    return [
        pltpu.VMEM((8 * rows, width), jnp.bfloat16),
        pltpu.VMEM((2, cut, width), jnp.bfloat16),
        pltpu.VMEM((2, max(rows - cut, 16), width), jnp.bfloat16),
        pltpu.VMEM((5, rows, width), jnp.bfloat16),
    ]


def fsdp_scatter(ref, rows, cut, buffers, g, sems, base):
    pair, tops, bottoms, full = buffers
    view, place = part_of(ref, rows, cut), fsdp_place(g)
    over, up, down, pal = fsdp_neighbours(g)
    copies = []

    def go(src, dst, sem, target):
        copies.append(send(src, dst, sems, base + sem, target))
        return copies[-1]

    def wide(part):
        return part[...].astype(jnp.float32)

    def slot(index):
        return pair.at[pl.ds(pl.multiple_of(lax.div(index, 2) * rows, 16), rows)]

    order = [(1, 2), (0, 2), (1, 3), (1, 1), (0, 3), (0, 1), (1, 0), (0, 0)]
    pals = {}
    for k, (dx, dz) in enumerate(order):
        index = place(dx, dz, 1)
        pals[dx, dz] = go(view(index), slot(index), k, pal)
    yield

    def paired(dx, dz):
        pals[dx, dz].wait_recv()
        return wide(view(place(dx, dz, 0))) + wide(slot(place(dx, dz, 0)))

    halves = {}
    for k, dx in enumerate((1, 0)):
        index = place(dx, 2, 0)
        value = paired(dx, 2)
        view(index)[...] = value.astype(jnp.bfloat16)
        halves[dx, "top"] = go(view(index, "top"), tops.at[dx], 8 + 2 * k, down)
        if cut < rows:
            halves[dx, "bottom"] = go(view(index, "bottom"), bottoms.at[dx], 9 + 2 * k, up)
    yield
    fulls = {}
    for k, dx in enumerate((1, 0)):
        index = place(dx, 3, 0)
        value = paired(dx, 3)
        halves[dx, "top"].wait_recv()
        view(index, "top")[...] = (value[:cut] + wide(tops.at[dx])).astype(jnp.bfloat16)
        if cut < rows:
            view(index, "bottom")[...] = value[cut:].astype(jnp.bfloat16)
        fulls[dx, "down"] = go(view(index), full.at[2 * dx], 12 + 2 * k, down)
        index = place(dx, 1, 0)
        value = paired(dx, 1)
        if cut < rows:
            halves[dx, "bottom"].wait_recv()
            view(index, "top")[...] = value[:cut].astype(jnp.bfloat16)
            view(index, "bottom")[...] = (value[cut:] + wide(bottoms.at[dx])).astype(jnp.bfloat16)
        else:
            view(index)[...] = value.astype(jnp.bfloat16)
        fulls[dx, "up"] = go(view(index), full.at[2 * dx + 1], 13 + 2 * k, up)
        yield
    index = place(1, 0, 0)
    value = paired(1, 0)
    fulls[1, "down"].wait_recv()
    fulls[1, "up"].wait_recv()
    view(index)[...] = (value + wide(full.at[2]) + wide(full.at[3])).astype(jnp.bfloat16)
    last = go(view(index), full.at[4], 16, over)
    value = paired(0, 0)
    yield
    fulls[0, "down"].wait_recv()
    fulls[0, "up"].wait_recv()
    value = value + wide(full.at[0]) + wide(full.at[1])
    yield
    last.wait_recv()
    value = value + wide(full.at[4])
    for copy in copies:
        copy.wait_send()
    return value


def sem_pair(count):
    return [pltpu.SemaphoreType.DMA((count,)), pltpu.SemaphoreType.DMA((count,))]


def others(me, count):
    return [lax.rem(me + k, count) for k in range(1, count)]


def exchange(blocks, into, me, peers, at, sems, base):
    return [
        send(blocks.at[p], into.at[me], sems, base + k, at(p)) for k, p in enumerate(peers)
    ]


def spread(block, into, me, peers, at, sems, base):
    return [send(block, into.at[me], sems, base + k, at(p)) for k, p in enumerate(peers)]


def swap_rows(src, dst, sems, index, target, alone):
    away = pltpu.make_async_remote_copy(
        src_ref=src,
        dst_ref=dst,
        send_sem=sems[0].at[index],
        recv_sem=sems[1].at[index],
        device_id=target,
        device_id_type=MESH,
    )
    here = pltpu.make_async_copy(src, dst, sems[0].at[index])
    pl.when(jnp.logical_not(alone))(away.start)
    pl.when(alone)(here.start)

    def wait():
        pl.when(jnp.logical_not(alone))(away.wait)
        pl.when(alone)(here.wait)

    return wait


def head_holder(g, s):
    return {"fsdp": lax.rem(g, 2) * 8 + s, "seq": lax.div(g, 2)}


def head_owner(g, s):
    return {"fsdp": 2 * s + lax.div(g, 8), "seq": lax.rem(g, 8)}


def greet_all(targets, pair, alone):
    barrier = pltpu.get_barrier_semaphore()
    for target in targets:
        pl.semaphore_signal(barrier, inc=1, device_id=target, device_id_type=MESH)

    @pl.when(jnp.logical_not(alone))
    def _():
        for target in pair:
            pl.semaphore_signal(barrier, inc=1, device_id=target, device_id_type=MESH)

    pl.semaphore_wait(barrier, len(targets) + jnp.where(alone, 0, 2))


def compact(blocks, rows):
    total = blocks.shape[0]
    shape = (total // 16 * rows, total)
    source = lax.broadcasted_iota(jnp.int32, shape, 1)
    place = lax.shift_right_logical(source, 4) * rows + (source & 15)
    keep = (place == lax.broadcasted_iota(jnp.int32, shape, 0)) & ((source & 15) < rows)
    return nn(keep.astype(jnp.bfloat16), blocks).astype(jnp.bfloat16)


def expand(rows_in, rows):
    shape = (rows_in.shape[0] // rows * 16, rows_in.shape[0])
    target = lax.broadcasted_iota(jnp.int32, shape, 0)
    place = lax.shift_right_logical(target, 4) * rows + (target & 15)
    keep = (place == lax.broadcasted_iota(jnp.int32, shape, 1)) & ((target & 15) < rows)
    return nn(keep.astype(jnp.bfloat16), rows_in).astype(jnp.bfloat16)


def unit_order(row_axis):
    mixed = lax.broadcasted_iota(jnp.int32, (512, 512), 1 - row_axis)
    plain = lax.broadcasted_iota(jnp.int32, (512, 512), row_axis)
    f = lax.shift_right_logical(mixed, 5)
    e = lax.shift_right_logical(mixed, 3) & 3
    return (e * 128 + f * 8 + (mixed & 7) == plain).astype(jnp.bfloat16)


def owner_units(s, total, owners):
    shape = (total, total // owners)
    unit = lax.broadcasted_iota(jnp.int32, shape, 0)
    place = lax.broadcasted_iota(jnp.int32, shape, 1)
    source = lax.shift_right_logical(place, 3) * (8 * owners) + s * 8 + (place & 7)
    return (unit == source).astype(jnp.bfloat16)


def scale_of(values):
    return lax.rsqrt(jnp.mean(values * values, axis=-1, keepdims=True) + EPS)


def rms_back(d_normed, unit, scale, gain):
    d_unit = d_normed * gain
    return scale * (d_unit - unit * jnp.mean(d_unit * unit, axis=-1, keepdims=True))


def fold(dst, first_row, column, value, width):
    rows = value.shape[0]
    for k in range(value.shape[1] // width):
        at = pl.ds(pl.multiple_of(first_row + k * rows, 16), rows)
        dst[at, column : column + width] = value[:, k * width : (k + 1) * width]


def unfold(src, first_row, column, rows, groups, width):
    parts = []
    for k in range(groups):
        at = pl.ds(pl.multiple_of(first_row + k * rows, 16), rows)
        parts.append(src[at, column : column + width])
    return jnp.concatenate(parts, axis=1)


def rows_at(place, count=128):
    return pl.ds(pl.multiple_of(place * count, count), count)


def kernel_params(collective_id):
    return pltpu.CompilerParams(
        collective_id=collective_id, has_side_effects=True, vmem_limit_bytes=52 << 20
    )


def array(shape, dtype=jnp.bfloat16):
    return jax.ShapeDtypeStruct(shape, dtype)


SMALL = 3 * WIDTH
KEYS = 4 * WIDTH


def window_steps(out_ref, rows, g, sems, base):
    core = lax.rem(g, 2)
    after, partner = at_fsdp(lax.rem(g + 2, 16)), at_fsdp(g + 1 - 2 * core)

    def part(index):
        return out_ref.at[index, rows]

    first = send(part(4), part(2), sems, base, after)
    yield
    first.wait_recv()
    second = send(part(2), part(0), sems, base + 1, after)
    third = send(part(4 - 2 * core), part(3), sems, base + 2, partner)
    yield
    second.wait_recv()
    fourth = send(part(2 - 2 * core), part(1), sems, base + 3, partner)
    yield
    third.wait_recv()
    fourth.wait_recv()
    for copy in (first, second, third, fourth):
        copy.wait_send()


def window_greeting(g):
    core = lax.rem(g, 2)
    return [at_fsdp(i) for i in (lax.rem(g + 2, 16), lax.rem(g + 14, 16), g + 1 - 2 * core)]


def start_kernel(
    tokens_ref, columns_ref, gate_ref, up_ref, wout_ref, chosen_ref, cotangent_ref,
    normed_out, q_ref, window_ref, weight_out, small_ref, rows_ref, wout_all_ref, chosen_out_ref,
    cotangent_out,
    all_ref, normed_ref, weight_ref, columns_in, experts_tx, experts_in, wout_in, mixed, cotangent_all,
    out_sems, send_sems, recv_sems,
):
    s, g = lax.axis_index("seq"), lax.axis_index("fsdp")
    p = ring_places(s)
    peers = others(s, 8)
    sems = (send_sems, recv_sems)
    holder, owner = head_holder(g, s), head_owner(g, s)
    alone = (holder["fsdp"] == g) & (holder["seq"] == s)
    greet_all(
        [at_seq(q) for q in peers] + fsdp_neighbours(g) + window_greeting(g),
        (holder, owner),
        alone,
    )
    copies = exchange(columns_ref, columns_in, s, peers, at_seq, sems, 0)
    wait_rows = swap_rows(
        wout_ref, wout_in, sems, 45, holder, alone
    )
    all_ref[s] = tokens_ref[...]
    tokens_in = Task(ring_gather(all_ref, s, sems, 7))
    tokens_in.step()
    chosen_copies = spread(chosen_ref, chosen_out_ref, s, peers, at_seq, sems, 46)
    chosen_out_ref[s] = chosen_ref[...]
    columns_in[s] = columns_ref[s]
    for copy in copies:
        copy.wait_recv()
    weight_ref[rows_at(g, 96), : KEYS + 128] = compact(columns_in[...].reshape(128, KEYS + 128), 12)
    wait_rows()
    fold(weight_ref, g * 96, KEYS + 128, wout_in[...], 256)
    columns_gather = Task(fsdp_gather(weight_ref, 96, 48, g, sems, 21))
    columns_gather.step()
    cotangent_all[s] = cotangent_ref[...]
    steps(columns_gather, tokens_in, columns_gather)
    steps(columns_gather, tokens_in)
    cotangent_in = Task(ring_gather(cotangent_all, s, sems, 78))
    cotangent_in.step()
    run(columns_gather)
    out_copies = [pltpu.make_async_copy(weight_ref.at[:, : KEYS + 128], weight_out, out_sems.at[8])]
    out_copies[0].start()
    pick = lax.broadcasted_iota(jnp.int32, (8, 2 * WIDTH), 0) + (SMALL - 2 * WIDTH)
    pick = (pick == lax.broadcasted_iota(jnp.int32, (8, 2 * WIDTH), 1)).astype(jnp.bfloat16)
    small_ref[...] = nt(pick, weight_ref[:, 2 * WIDTH : 4 * WIDTH])
    gain = small_ref[0:1, :]

    def project(place):
        values = all_ref[place].astype(jnp.float32)
        normed = (values * scale_of(values) * gain).astype(jnp.bfloat16)
        normed_ref[rows_at(place), :] = normed
        result = nn(normed, weight_ref[:, : KEYS + 128]).astype(jnp.bfloat16)
        q_ref[rows_at(place), :] = result[:, :SMALL]
        window_ref[4, rows_at(place), :] = result[:, KEYS:]
        copy = pltpu.make_async_copy(
            normed_ref.at[rows_at(place)],
            normed_out.at[rows_at(place)],
            out_sems.at[len(out_copies) - 1],
        )
        copy.start()
        out_copies.append(copy)

    project(s)
    for name in ("down", "up", "far"):
        project(p[name])
    side = lax.div(s, RING)
    near = Task(window_steps(window_ref, rows_at(side, 512), g, sems, 53))
    near.step()
    project(p["over"])
    tokens_in.step()
    project(p["over_up"])
    project(p["over_down"])
    run(tokens_in)
    project(p["over_far"])
    away = Task(window_steps(window_ref, rows_at(1 - side, 512), g, sems, 74))
    away.step()
    cotangent_in.step()
    experts = jnp.concatenate(
        [gate_ref[...].reshape(64, gate_ref.shape[2]), up_ref[...].reshape(64, gate_ref.shape[2])], axis=0
    )

    @pl.loop(0, 8)
    def _(place):
        units = owner_units(place, experts.shape[1], 8)
        experts_tx[place] = nn(experts, units).astype(jnp.bfloat16)

    copies += exchange(experts_tx, experts_in, s, peers, at_seq, sems, 38)
    experts_in[s] = experts_tx[s]
    steps(near, away, cotangent_in)

    @pl.loop(0, 16)
    def _(f):
        mixed[rows_at(f, 16), :] = unfold(weight_ref, f * 96, KEYS + 128, 16, 6, 256)

    wout_all_ref[...] = compact(mixed[...], 12)
    steps(near, away)
    for copy in copies[7:]:
        copy.wait_recv()
    for e in range(8):
        rows = experts_in[:, e * 16 : (e + 1) * 16, :].reshape(128, 128)
        rows_ref[:, e * 128 : (e + 1) * 128] = compact(rows, 12)
    run_all(near, away, cotangent_in)
    out_copies.append(pltpu.make_async_copy(cotangent_all, cotangent_out, out_sems.at[9]))
    out_copies[-1].start()
    for copy in chosen_copies:
        copy.wait_recv()
    for copy in copies + chosen_copies:
        copy.wait_send()
    for copy in out_copies:
        copy.wait()


ANY = pl.BlockSpec(memory_space=pl.ANY)


def start(tokens, columns, gate, up, wout, chosen, cotangent):
    own, model = tokens.shape
    rows = 8 * own
    width = columns.shape[2]
    return pl.pallas_call(
        start_kernel,
        in_specs=[VMEM] * 7,
        out_specs=[ANY, VMEM, VMEM, ANY, VMEM, VMEM, VMEM, VMEM, ANY],
        out_shape=[
            array((rows, model)),
            array((rows, SMALL)),
            array((LOOK + 1, rows, width - KEYS)),
            array((model, width)),
            array((8, model), jnp.float32),
            array((96, gate.shape[2])),
            array((192, model)),
            array((8,) + chosen.shape, jnp.float32),
            array((8, own, model)),
        ],
        scratch_shapes=[
            pltpu.VMEM((8, own, model), jnp.bfloat16),
            pltpu.VMEM((rows, model), jnp.bfloat16),
            pltpu.VMEM((model, width + 256), jnp.bfloat16),
            pltpu.VMEM(columns.shape, jnp.bfloat16),
            pltpu.VMEM((8, 128, 128), jnp.bfloat16),
            pltpu.VMEM((8, 128, 128), jnp.bfloat16),
            pltpu.VMEM(wout.shape, jnp.bfloat16),
            pltpu.VMEM((256, model), jnp.bfloat16),
            pltpu.VMEM((8, own, model), jnp.bfloat16),
            pltpu.SemaphoreType.DMA((10,)),
            *sem_pair(92),
        ],
        compiler_params=kernel_params(1),
        name="start",
    )(tokens, columns, gate, up, wout, chosen, cotangent)


def window_back_steps(d_ref, out_ref, rows, tx, rx, g, sems, base):
    core = lax.rem(g, 2)
    before, partner = at_fsdp(lax.rem(g + 14, 16)), at_fsdp(g + 1 - 2 * core)
    odd = core.astype(jnp.float32)
    even = 1.0 - odd

    def wide(slot):
        return rx[slot, rows, :].astype(jnp.float32)

    def go(slot, value, sem, target):
        tx[slot, rows, :] = value.astype(jnp.bfloat16)
        return send(tx.at[slot, rows], rx.at[slot, rows], sems, base + sem, target)

    one = go(1, d_ref[1, rows, :], 1, partner)
    two = go(2, d_ref[3, rows, :], 2, partner)
    yield
    one.wait_recv()
    zero = go(0, d_ref[0, rows, :] + odd * wide(1), 0, before)
    yield
    two.wait_recv()
    zero.wait_recv()
    value = d_ref[2, rows, :] + wide(0) + odd * wide(2) + even * wide(1)
    three = go(3, value, 3, before)
    yield
    three.wait_recv()
    out_ref[rows, :] = (d_ref[4, rows, :] + wide(3) + even * wide(2)).astype(jnp.bfloat16)
    for copy in (zero, one, two, three):
        copy.wait_send()


def moe_kernel(
    attended_ref, wout_ref, tokens_ref, small_ref, rows_ref, down_rows_ref, cotangent_in, chosen_ref,
    resid_ref, moe_out, d_resid_ref, d_attended_ref, router_ref, bulk_out,
    normed_ref, shared_ref, d_ref, branch_ref, cotangent_ref, gate_up_ref, down_mixed, down_ref,
    moe_ref, bulk, grad_down, grad_wout, grad_wout_low, probs_ref, share_tx, share_in, logits_ref,
    tx_a, rx_a, tx_b, rx_b,
    local_sems, send_sems, recv_sems,
):
    s, g = lax.axis_index("seq"), lax.axis_index("fsdp")
    p = ring_places(s)
    peers = others(s, 8)
    sems = (send_sems, recv_sems)
    cotangent_copy = pltpu.make_async_copy(cotangent_in, cotangent_ref, local_sems.at[0])
    cotangent_copy.start()
    greet([at_seq(q) for q in peers] + fsdp_neighbours(g))
    model = tokens_ref.shape[1]
    units = down_ref.shape[0]
    per = units // EXPERTS

    def branch_part(place):
        return nn(attended_ref[rows_at(place), :], wout_ref[...])

    branch_sum = Task(ring_scatter(branch_part, tx_a, rx_a, s, sems, 0))
    branch_sum.step()
    gate_up_ref[rows_at(g, 96), : 2 * units] = rows_ref[...]
    fold(gate_up_ref, g * 96, 2 * units, down_rows_ref[...], 512)
    weight_gather = Task(fsdp_gather(gate_up_ref, 96, 48, g, sems, 107))
    steps(weight_gather, weight_gather, branch_sum)
    branch = run(branch_sum, weight_gather)
    resid = tokens_ref[...].astype(jnp.float32) + branch
    resid_ref[...] = resid
    gain = small_ref[1:2, :]
    router = small_ref[...].astype(jnp.bfloat16)
    normed_ref[s] = (resid * scale_of(resid) * gain).astype(jnp.bfloat16)
    gather = Task(ring_gather(normed_ref, s, sems, 14))
    gather.step()
    run(weight_gather)

    @pl.loop(0, 16)
    def _(f):
        down_mixed[rows_at(f, 32), :] = unfold(gate_up_ref, f * 96, 2 * units, 32, 3, 512)

    down_ref[...] = nn(unit_order(0), down_mixed[...]).astype(jnp.bfloat16)
    cotangent_copy.wait()

    def block(place):
        x = normed_ref[place]
        logits = nt(router, x)
        logits = jnp.concatenate([logits[2 : 2 + EXPERTS], jnp.full((4, 128), NEGATIVE)], axis=0)
        probs = jnp.exp(logits - jnp.max(logits, axis=0, keepdims=True))
        probs = probs / jnp.sum(probs, axis=0, keepdims=True)
        probs_ref[place] = probs
        share = jnp.concatenate([probs * chosen_ref[place], jnp.zeros((120, 128))], axis=0)
        share = jnp.transpose(share)
        plain = nt(cotangent_ref[place], down_ref[...])
        both = nn(x, gate_up_ref[:, : 2 * units])
        sums = []
        for e in range(EXPERTS):
            at = slice(e * per, (e + 1) * per)
            gate, up = both[:, at], both[:, units + e * per : units + (e + 1) * per]
            wide = jnp.broadcast_to(share[:, e : e + 1], gate.shape)
            sigmoid = 1.0 / (1.0 + jnp.exp(-gate))
            silu = gate * sigmoid
            hidden = (silu * up).astype(jnp.bfloat16).astype(jnp.float32)
            shared_ref[rows_at(place), at] = (hidden * wide).astype(jnp.bfloat16)
            sums.append(jnp.sum(plain[:, at] * hidden, axis=1, keepdims=True))
            d_hidden = plain[:, at] * wide
            d_gate = d_hidden * up * sigmoid * (1.0 + gate * (1.0 - sigmoid))
            d_ref[rows_at(place), at] = d_gate.astype(jnp.bfloat16)
            d_ref[rows_at(place), units + e * per : units + (e + 1) * per] = (
                d_hidden * silu
            ).astype(jnp.bfloat16)
        sums = jnp.concatenate(sums + [jnp.zeros((128, 128 - EXPERTS))], axis=1)
        share_tx[place] = jnp.transpose(sums)[:8]

    block(s)
    gather.step()
    block(p["down"])
    block(p["up"])
    gather.step()
    block(p["over"])
    block(p["far"])
    gather.step()
    late = [p["over_up"], p["over_down"], p["over_far"]]

    moe_copy = pltpu.make_async_copy(moe_ref, moe_out, local_sems.at[1])
    bulk_copies = [
        pltpu.make_async_copy(bulk.at[:, at], bulk_out.at[:, at], local_sems.at[2 + k])
        for k, at in enumerate((pl.ds(0, 2 * units), pl.ds(2 * units, 512), pl.ds(2 * units + 512, 256)))
    ]

    def weight_grads():
        @pl.loop(0, model // 128)
        def _(j):
            normed = normed_ref[:, :, rows_at(j)].reshape(8 * 128, 128)
            bulk[rows_at(j), : 2 * units] = tn(normed, d_ref[...]).astype(jnp.bfloat16)

        bulk_copies[0].start()
        yield
        shared, grad = shared_ref[...], cotangent_ref[...].reshape(8 * 128, model)
        value = tn(shared, grad).astype(jnp.bfloat16)
        grad_down[...] = nn(unit_order(1), value).astype(jnp.bfloat16)

        @pl.loop(0, 16)
        def _(f):
            fold(bulk, f * 96, 2 * units, grad_down[rows_at(f, 32), :], 512)

        bulk_copies[1].start()
        yield
        moe_ref[...] = nn(shared_ref[...], down_ref[...]).astype(jnp.bfloat16)
        moe_copy.start()

    grads = Task(weight_grads())

    def normed_part(place):
        if late:
            late.pop(0)
            if not late:
                run(gather)
            block(place)
        return nt(d_ref[rows_at(place), :], gate_up_ref[:, : 2 * units])

    d_normed_sum = Task(ring_scatter(normed_part, tx_b, rx_b, s, sems, 42))
    d_normed_sum.step()
    shares = exchange(share_tx, share_in, s, peers, at_seq, sems, 28)
    share_in[s] = share_tx[s]
    grads.step()
    steps(d_normed_sum, d_normed_sum, grads, d_normed_sum, grads)
    d_normed = run(d_normed_sum)
    for copy in shares:
        copy.wait_recv()

    d_router = jnp.sum(share_in[...], axis=0) * chosen_ref[s]
    probs = probs_ref[s]
    d_logits = probs * (d_router - jnp.sum(probs * d_router, axis=0, keepdims=True))
    d_logits = d_logits.astype(jnp.bfloat16)
    logits_ref[s] = d_logits.astype(jnp.float32)
    spreads = spread(logits_ref.at[s], logits_ref, s, peers, at_seq, sems, 35)
    padded = jnp.concatenate([jnp.zeros((2, 128), jnp.bfloat16), d_logits[:6]], axis=0)
    d_normed = d_normed + tn(padded, router)
    resid = resid_ref[...]
    scale = scale_of(resid)
    d_resid = cotangent_ref[s].astype(jnp.float32) + rms_back(
        d_normed, resid * scale, scale, gain
    )
    d_resid_ref[...] = d_resid
    branch_ref[s] = d_resid.astype(jnp.bfloat16)
    gather = Task(ring_gather(branch_ref, s, sems, 93))
    gather.step()

    grad_wout[...] = jnp.zeros_like(grad_wout)

    def d_attended(place):
        d_branch = branch_ref[place]
        d_attended_ref[rows_at(place), :] = nt(d_branch, wout_ref[...]).astype(jnp.bfloat16)
        grad_wout[...] += tn(attended_ref[rows_at(place), :], d_branch)

    d_attended(s)
    gather.step()
    steps(grads)
    for name in ("down", "up", "over"):
        d_attended(p[name])
    steps(grads, gather)
    for copy in spreads:
        copy.wait_recv()
    total = jnp.zeros((8, model), jnp.float32)
    for q in range(8):
        total += nn(logits_ref[q].astype(jnp.bfloat16), normed_ref[q])
    router_ref[...] = total
    d_attended(p["far"])
    steps(grads, gather)
    d_attended(p["over_up"])
    d_attended(p["over_down"])
    run(grads)
    run(gather)
    d_attended(p["over_far"])
    grad_wout_low[...] = expand(grad_wout[...].astype(jnp.bfloat16), 12)

    @pl.loop(0, 16)
    def _(f):
        fold(bulk, f * 96, 2 * units + 512, grad_wout_low[rows_at(f, 16), :], 256)

    bulk_copies[2].start()
    moe_copy.wait()
    for copy in bulk_copies:
        copy.wait()
    for copy in shares + spreads:
        copy.wait_send()


def moe(attended, wout, tokens, small, rows, down_rows, cotangent, chosen):
    own, model = tokens.shape
    group = 8 * own
    width, units = rows.shape[1], 16 * down_rows.shape[0]
    f32, bf16 = jnp.float32, jnp.bfloat16
    tiny = pltpu.VMEM((8, 8, own), f32)
    return pl.pallas_call(
        moe_kernel,
        in_specs=[VMEM] * 6 + [ANY, VMEM],
        out_specs=[VMEM, ANY] + [VMEM] * 3 + [ANY],
        out_shape=[
            array((own, model), f32),
            array((group, model)),
            array((own, model), f32),
            array((group, SMALL)),
            array((8, model), f32),
            array((model, width + 768)),
        ],
        scratch_shapes=[
            pltpu.VMEM((8, own, model), bf16),
            pltpu.VMEM((group, units), bf16),
            pltpu.VMEM((group, width), bf16),
            pltpu.VMEM((8, own, model), bf16),
            pltpu.VMEM((8, own, model), bf16),
            pltpu.VMEM((model, width + 512), bf16),
            pltpu.VMEM((units, model), bf16),
            pltpu.VMEM((units, model), bf16),
            pltpu.VMEM((group, model), bf16),
            pltpu.VMEM((model, width + 768), bf16),
            pltpu.VMEM((units, model), bf16),
            pltpu.VMEM((192, model), f32),
            pltpu.VMEM((256, model), bf16),
            tiny,
            tiny,
            tiny,
            tiny,
            *ring_buffers(own, model),
            *ring_buffers(own, model),
            pltpu.SemaphoreType.DMA((5,)),
            *sem_pair(124),
        ],
        compiler_params=kernel_params(2),
        name="moe",
    )(attended, wout, tokens, small, rows, down_rows, cotangent, chosen)


def finish_kernel(
    dq_ref, d_window_ref, weight_in, normed_in, router_ref, bulk_in, d_resid_ref, tokens_ref,
    small_ref,
    grad_input_ref, query_out, key_out, gate_out, up_out, wout_out, down_out,
    weight_ref, normed_ref, bulk, d_ref, key_grads, key_tx, experts_tx, experts_in, wout_tx,
    wtx, wrx, tx, rx,
    pair_a, tops_a, bottoms_a, full_a, pair_b, tops_b, bottoms_b, full_b,
    local_sems, send_sems, recv_sems,
):
    s, g = lax.axis_index("seq"), lax.axis_index("fsdp")
    peers = others(s, 8)
    sems = (send_sems, recv_sems)
    entries = bulk_in.shape[1]
    bulk_copy = pltpu.make_async_copy(bulk_in, bulk.at[:, :entries], local_sems.at[2])
    bulk_copy.start()
    normed_copy = pltpu.make_async_copy(normed_in, normed_ref, local_sems.at[0])
    normed_copy.start()
    weight_copy = pltpu.make_async_copy(weight_in, weight_ref, local_sems.at[1])
    weight_copy.start()
    holder, owner = head_holder(g, s), head_owner(g, s)
    alone = (holder["fsdp"] == g) & (holder["seq"] == s)
    greet_all(
        [at_seq(q) for q in peers] + fsdp_neighbours(g) + window_greeting(g),
        (holder, owner),
        alone,
    )
    d_keyval = d_ref.at[:, KEYS:]
    halves = [
        Task(window_back_steps(d_window_ref, d_keyval, pl.ds(k * 512, 512), wtx, wrx, g, sems, 4 * k))
        for k in range(2)
    ]

    def windows():
        for half in halves:
            half.step()

    windows()
    d_ref[:, :SMALL] = dq_ref[...]
    d_ref[:, SMALL:KEYS] = jnp.zeros((d_ref.shape[0], WIDTH), jnp.bfloat16)
    windows()
    windows()
    model = normed_ref.shape[1]
    normed_copy.wait()

    def weight_grad(columns):
        return tn(d_ref[:, columns], normed_ref[...])

    value = weight_grad(slice(0, KEYS))
    row = lax.broadcasted_iota(jnp.int32, (KEYS, 1), 0)
    router = jnp.concatenate(
        [jnp.zeros((SMALL + 2, model)), router_ref[...], jnp.zeros((KEYS - SMALL - 10, model))], axis=0
    )
    value = jnp.transpose(jnp.where(row < SMALL, value, router)).astype(jnp.bfloat16)
    bulk_copy.wait()
    bulk[:, entries:] = value
    grads = Task(fsdp_scatter(bulk, 96, 48, (pair_a, tops_a, bottoms_a, full_a), g, sems, 15))
    grads.step()
    weight_copy.wait()
    run_all(*halves)

    def partial(place):
        return nt(d_ref[rows_at(place), :], weight_ref[...])

    total = Task(ring_scatter(partial, tx, rx, s, sems, 49))
    total.step()
    key_grads[...] = jnp.transpose(weight_grad(slice(KEYS, KEYS + 2 * WIDTH))).astype(jnp.bfloat16)
    key = Task(fsdp_scatter(key_grads, 96, 48, (pair_b, tops_b, bottoms_b, full_b), g, sems, 63))
    key.step()
    steps(key, grads, key, key, total, grads, key, total)
    run(key)
    key_tx[...] = expand(key.value.astype(jnp.bfloat16), 12).reshape(key_tx.shape)
    copies = exchange(key_tx, key_out, s, peers, at_seq, sems, 87)
    key_out[s] = key_tx[s]
    steps(grads, total)
    value = run(grads)
    units = gate_out.shape[2] // 8
    width = 8 * units
    wide = jnp.concatenate([value[:, :width], value[:, entries:]], axis=1).astype(jnp.bfloat16)
    experts_tx[...] = expand(wide, 12).reshape(experts_tx.shape)
    expert_copies = exchange(experts_tx, experts_in, s, peers, at_seq, sems, 8)
    experts_in[s] = experts_tx[s]
    wout_tx[...] = jnp.concatenate(
        [value[k * 16 : (k + 1) * 16, width + 512 : entries] for k in range(6)], axis=1
    ).astype(jnp.bfloat16)
    wait_rows = swap_rows(wout_tx, wout_out, sems, 94, owner, alone)
    down_out[...] = jnp.concatenate(
        [value[k * 32 : (k + 1) * 32, width : width + 512] for k in range(3)], axis=1
    )
    d_normed = run(total)
    values = tokens_ref[...].astype(jnp.float32)
    scale = scale_of(values)
    grad_input_ref[...] = d_resid_ref[...] + rms_back(
        d_normed, values * scale, scale, small_ref[0:1, :]
    )
    for copy in expert_copies:
        copy.wait_recv()
    query_out[...] = experts_in[:, :, width:]
    back = jnp.zeros((128, gate_out.shape[2]), jnp.float32)
    for place in range(8):
        block = jnp.concatenate(
            [experts_in[place, :, e * units : (e + 1) * units] for e in range(8)], axis=0
        )
        back += nt(block, owner_units(place, gate_out.shape[2], 8))
    for e in range(EXPERTS):
        gate_out[e] = back[e * 16 : e * 16 + 12]
        up_out[e] = back[(EXPERTS + e) * 16 : (EXPERTS + e) * 16 + 12]
    wait_rows()
    for copy in copies:
        copy.wait_recv()
    for copy in copies + expert_copies:
        copy.wait_send()


def finish(dq, d_window, weight, normed, router, bulk, d_resid, tokens, small, units):
    own, model = tokens.shape
    rows = dq.shape[0]
    width = weight.shape[1]
    blocks = (8, 16, units + KEYS)
    keyval = d_window.shape[1:]
    bf16, f32 = jnp.bfloat16, jnp.float32
    return pl.pallas_call(
        finish_kernel,
        in_specs=[VMEM, VMEM, ANY, ANY, VMEM, ANY] + [VMEM] * 3,
        out_specs=[VMEM] * 7,
        out_shape=[
            array((own, model), f32),
            array((8, 16, KEYS)),
            array((8, 16, width - KEYS)),
            array((EXPERTS, 12, units), f32),
            array((EXPERTS, 12, units), f32),
            array((16, model)),
            array((32, model), f32),
        ],
        scratch_shapes=[
            pltpu.VMEM(weight.shape, bf16),
            pltpu.VMEM(normed.shape, bf16),
            pltpu.VMEM((model, bulk.shape[1] + KEYS), bf16),
            pltpu.VMEM((rows, width), bf16),
            pltpu.VMEM((model, width - KEYS), bf16),
            pltpu.VMEM((8, 16, width - KEYS), bf16),
            pltpu.VMEM(blocks, bf16),
            pltpu.VMEM(blocks, bf16),
            pltpu.VMEM((16, model), bf16),
            pltpu.VMEM((4,) + keyval, bf16),
            pltpu.VMEM((4,) + keyval, bf16),
            *ring_buffers(own, model),
            *fsdp_buffers(model // 16, 48, bulk.shape[1] + KEYS),
            *fsdp_buffers(model // 16, 48, width - KEYS),
            pltpu.SemaphoreType.DMA((3,)),
            *sem_pair(95),
        ],
        compiler_params=kernel_params(3),
        name="finish",
    )(dq, d_window, weight, normed, router, bulk, d_resid, tokens, small)


def pad_rows(x, axis):
    pads = [(0, 0)] * x.ndim
    pads[axis] = (0, 16 - x.shape[axis])
    return jnp.pad(x, pads)


def on_device(
    tokens,
    gain_one,
    w_qkv,
    w_out,
    gain_two,
    w_router,
    w_gate,
    w_up,
    w_down,
    doc_starts,
    routes,
    cotangent,
):
    seq = lax.axis_size("seq")
    group_index = lax.axis_index("fsdp")
    own, model = tokens.shape
    group_rows = own * seq
    experts, own_model, ff = w_gate.shape
    bf16, f32 = jnp.bfloat16, jnp.float32

    qkv_parts = jnp.transpose(w_qkv.reshape(own_model, seq, 5 * WIDTH), (1, 0, 2))
    small = jnp.concatenate([gain_one[:, None], gain_two[:, None], w_router], axis=1)
    small = jnp.pad(small, ((0, 0), (0, WIDTH - small.shape[1])))
    columns = jnp.concatenate(
        [
            qkv_parts[:, :, :SMALL],
            jnp.broadcast_to(small[None], (seq,) + small.shape),
            qkv_parts[:, :, SMALL:],
        ],
        axis=2,
    )
    expert_ids = jnp.arange(8, dtype=jnp.int32)
    chosen = jnp.sum((routes[None, :, :] == expert_ids[:, None, None]).astype(f32), axis=2)
    normed_one, queries, window, weight, small, rows, out_weight, chosen, cotangent_all = start(
        tokens,
        pad_rows(columns, 1),
        pad_rows(w_gate, 1),
        pad_rows(w_up, 1),
        pad_rows(w_out, 0),
        chosen,
        cotangent,
    )

    window = window.reshape((LOOK + 1) * group_rows, 2 * WIDTH)
    positions = group_index * group_rows + jnp.arange(group_rows, dtype=jnp.int32)
    begins = jnp.max(
        jnp.where(doc_starts[:, None] <= positions[None, :], doc_starts[:, None], 0), axis=0
    )
    lo = begins - (group_index - LOOK) * group_rows
    blocks = group_rows // BQ
    lo_blocks = lo.reshape(blocks, BQ)
    ends = LOOK * group_rows + jnp.arange(blocks, dtype=jnp.int32) * BQ

    def bounds(step):
        diag = ends // step
        first = jnp.minimum(lo_blocks[:, 0] // step, diag)
        full = jnp.minimum((lo_blocks[:, -1] + step - 1) // step, diag)
        return jnp.stack([first, full, diag, (ends + BQ + step - 1) // step], axis=1)

    attended, lse = attention(bounds(BK), lo[None, :], queries, window)

    residual, moe_out, d_resid, d_attended, grad_router, bulk = moe(
        attended, out_weight, tokens, small, rows, w_down.reshape(-1, model), cotangent_all, chosen
    )
    moe_out = lax.psum_scatter(moe_out, "seq", scatter_dimension=0, tiled=True)
    output = (residual + moe_out.astype(f32)).astype(bf16)

    d_queries, d_window = attention_back(
        bounds(BK_BACK), lo[None, :], queries, window, attended, d_attended, lse
    )
    grad_input, query_grads, key_grads, shard_gate, shard_up, shard_out, shard_down = finish(
        d_queries,
        d_window.reshape(LOOK + 1, group_rows, 2 * WIDTH),
        weight, normed_one, grad_router, bulk, d_resid, tokens, small, ff,
    )

    shard_down = shard_down.reshape(experts, -1, model)
    shard_out = shard_out[:own_model].astype(f32)
    shard_qkv = jnp.concatenate([query_grads[:, :own_model, :SMALL], key_grads[:, :own_model]], axis=2)
    shard_qkv = jnp.transpose(shard_qkv, (1, 0, 2)).reshape(own_model, -1).astype(f32)
    shard_router = query_grads[0, :own_model, SMALL + 2 : SMALL + 2 + experts].astype(f32)

    shard_gain_one = jnp.sum(w_qkv.astype(f32) * shard_qkv, axis=1)
    shard_gain_one = shard_gain_one / gain_one.astype(f32)
    shard_gain_two = jnp.sum(w_router.astype(f32) * shard_router, axis=1)
    shard_gain_two += jnp.sum(w_gate.astype(f32) * shard_gate, axis=(0, 2))
    shard_gain_two += jnp.sum(w_up.astype(f32) * shard_up, axis=(0, 2))
    shard_gain_two = shard_gain_two / gain_two.astype(f32)
    return (
        output,
        grad_input,
        shard_gain_one,
        shard_qkv,
        shard_out,
        shard_gain_two,
        shard_router,
        shard_gate,
        shard_up,
        shard_down,
    )


def solution(mesh):
    rows, vector = P(BOTH, None), P(BOTH)
    middle = P(None, BOTH, None)
    in_specs = (
        rows, vector, rows, rows, vector, rows, middle, middle, middle, P(), rows, rows,
    )
    out_specs = (rows, rows, vector, rows, rows, vector, rows, middle, middle, middle)
    return jax.shard_map(
        on_device, mesh=mesh, in_specs=in_specs, out_specs=out_specs, check_vma=False
    )
```

```python
import functools

import jax
import jax.numpy as jnp
from jax import lax
from jax.experimental import pallas as pl
from jax.experimental.pallas import tpu as pltpu
from jax.sharding import PartitionSpec as P

WIDTH = 64
LOOK = 4
EXPERTS = 4
EPS = 1e-06
NEGATIVE = -1e30
BQ = 256
BK = 1024
BK_BACK = 512
BOTH = ("fsdp", "seq")


def nt(a, b):
    return lax.dot_general(a, b, (((1,), (1,)), ((), ())), preferred_element_type=jnp.float32)


def tn(a, b):
    return lax.dot_general(a, b, (((0,), (0,)), ((), ())), preferred_element_type=jnp.float32)


def nn(a, b):
    return jnp.dot(a, b, preferred_element_type=jnp.float32)


def stack_heads(rows, low):
    heads = rows.shape[1] // WIDTH
    zero = jnp.zeros((rows.shape[0], WIDTH), rows.dtype)
    parts = []
    for h in range(heads):
        part = rows[:, h * WIDTH : (h + 1) * WIDTH]
        parts.append(jnp.concatenate([part, zero] if low else [zero, part], axis=1))
    return jnp.concatenate(parts, axis=0)


def chunk_loops(bounds_ref, step):
    b = pl.program_id(0)
    first, full, diag, end = (bounds_ref[b, i] for i in range(4))
    pl.loop(first, full)(lambda c: step(c, True))
    pl.loop(full, diag)(lambda c: step(c, False))
    pl.loop(diag, end)(lambda c: step(c, True))


def attention_kernel(
    bounds_ref, lo_ref, q_ref, kv_ref, out_ref, lse_ref, m_ref, acc_ref, ones_ref
):
    heads = q_ref.shape[1] // WIDTH
    queries = stack_heads(q_ref[...] * 0.125, True)
    m_ref[...] = jnp.full_like(m_ref, NEGATIVE)
    acc_ref[...] = jnp.zeros_like(acc_ref)

    @pl.when(pl.program_id(0) == 0)
    def _():
        lane = lax.broadcasted_iota(jnp.int32, kv_ref.shape, 1)
        ones_ref[...] = jnp.where(lane < WIDTH, jnp.ones_like(kv_ref[...]), kv_ref[...])

    base = LOOK * 1024 + pl.program_id(0) * BQ

    def step(c, masked):
        start = pl.multiple_of(c * BK, BK)
        rows = kv_ref[pl.ds(start, BK), :]
        scores = nt(rows, queries)
        if masked:
            key = start + lax.broadcasted_iota(jnp.int32, (BK, BQ), 0)
            query = base + lax.broadcasted_iota(jnp.int32, (BK, BQ), 1)
            seen = (key >= lo_ref[...]) & (key <= query)
            scores = jnp.where(jnp.concatenate([seen] * heads, axis=1), scores, NEGATIVE)
        old = m_ref[...]
        new = jnp.maximum(old, jnp.max(scores, axis=0, keepdims=True))
        probs = jnp.exp(scores - new).astype(jnp.bfloat16)
        fade = jnp.exp(old - new)
        m_ref[...] = new
        acc_ref[...] = acc_ref[...] * fade + tn(ones_ref[pl.ds(start, BK), :], probs)

    chunk_loops(bounds_ref, step)
    total = acc_ref[:1, :]
    result = jnp.transpose(acc_ref[...] / total)
    out_ref[...] = jnp.concatenate(
        [result[h * BQ : (h + 1) * BQ, WIDTH:] for h in range(heads)], axis=1
    ).astype(jnp.bfloat16)
    lse_ref[...] = jnp.broadcast_to(m_ref[...] + jnp.log(total), lse_ref.shape)


def attention(bounds, lo, q, kv):
    rows, width = q.shape
    heads = width // WIDTH
    blocks = rows // BQ
    return pl.pallas_call(
        attention_kernel,
        grid=(blocks,),
        in_specs=[
            pl.BlockSpec(memory_space=pltpu.SMEM),
            pl.BlockSpec((1, BQ), lambda b: (0, b)),
            pl.BlockSpec((BQ, width), lambda b: (b, 0)),
            pl.BlockSpec(memory_space=pltpu.VMEM),
        ],
        out_specs=[
            pl.BlockSpec((BQ, width), lambda b: (b, 0)),
            pl.BlockSpec((None, 8, heads * BQ), lambda b: (b, 0, 0)),
        ],
        out_shape=[
            jax.ShapeDtypeStruct((rows, width), jnp.bfloat16),
            jax.ShapeDtypeStruct((blocks, 8, heads * BQ), jnp.float32),
        ],
        scratch_shapes=[
            pltpu.VMEM((1, heads * BQ), jnp.float32),
            pltpu.VMEM((2 * WIDTH, heads * BQ), jnp.float32),
            pltpu.VMEM(kv.shape, jnp.bfloat16),
        ],
        compiler_params=pltpu.CompilerParams(vmem_limit_bytes=48 << 20),
        cost_estimate=pl.CostEstimate(
            flops=4 * rows * 4096 * width, bytes_accessed=4 << 20, transcendentals=rows * 4096 * 3
        ),
        name="attention",
    )(bounds, lo, q, kv)


def attention_back_kernel(
    bounds_ref, lo_ref, q_ref, kv_ref, out_ref, dout_ref, lse_ref, dq_ref, dkv_ref, acc_ref
):
    heads = q_ref.shape[1] // WIDTH
    queries = stack_heads(q_ref[...] * 0.125, True)
    douts = stack_heads(dout_ref[...], False)
    outs = stack_heads(out_ref[...], False)
    delta = jnp.sum(
        jnp.transpose(douts.astype(jnp.float32) * outs.astype(jnp.float32)), axis=0, keepdims=True
    )
    lse = lse_ref[:1, :]
    acc_ref[...] = jnp.zeros_like(acc_ref)
    base = LOOK * 1024 + pl.program_id(0) * BQ

    @pl.when(pl.program_id(0) == 0)
    def _():
        dkv_ref[...] = jnp.zeros_like(dkv_ref)

    def step(c, masked):
        start = pl.multiple_of(c * BK_BACK, BK_BACK)
        rows = kv_ref[pl.ds(start, BK_BACK), :]
        scores = nt(rows, queries)
        if masked:
            key = start + lax.broadcasted_iota(jnp.int32, (BK_BACK, BQ), 0)
            query = base + lax.broadcasted_iota(jnp.int32, (BK_BACK, BQ), 1)
            seen = (key >= lo_ref[...]) & (key <= query)
            scores = jnp.where(jnp.concatenate([seen] * heads, axis=1), scores, NEGATIVE)
        probs = jnp.exp(scores - lse)
        d_scores = (probs * (nt(rows, douts) - delta)).astype(jnp.bfloat16)
        dkv_ref[pl.ds(start, BK_BACK), :] += nn(d_scores, queries) + nn(
            probs.astype(jnp.bfloat16), douts
        )
        acc_ref[...] += tn(rows, d_scores)

    chunk_loops(bounds_ref, step)
    result = jnp.transpose(acc_ref[...]) * 0.125
    dq_ref[...] = jnp.concatenate(
        [result[h * BQ : (h + 1) * BQ, :WIDTH] for h in range(heads)], axis=1
    ).astype(jnp.bfloat16)


def attention_back(bounds, lo_row, q, kv, out, dout, lse):
    rows, width = q.shape
    heads = width // WIDTH
    blocks = rows // BQ
    row_block = pl.BlockSpec((BQ, width), lambda b: (b, 0))
    return pl.pallas_call(
        attention_back_kernel,
        grid=(blocks,),
        in_specs=[
            pl.BlockSpec(memory_space=pltpu.SMEM),
            pl.BlockSpec((1, BQ), lambda b: (0, b)),
            row_block,
            pl.BlockSpec(memory_space=pltpu.VMEM),
            row_block,
            row_block,
            pl.BlockSpec((None, 8, heads * BQ), lambda b: (b, 0, 0)),
        ],
        out_specs=[
            row_block,
            pl.BlockSpec(kv.shape, lambda b: (0, 0)),
        ],
        out_shape=[
            jax.ShapeDtypeStruct((rows, width), jnp.bfloat16),
            jax.ShapeDtypeStruct(kv.shape, jnp.float32),
        ],
        scratch_shapes=[pltpu.VMEM((2 * WIDTH, heads * BQ), jnp.float32)],
        compiler_params=pltpu.CompilerParams(vmem_limit_bytes=48 << 20),
        cost_estimate=pl.CostEstimate(
            flops=10 * rows * 4096 * width, bytes_accessed=8 << 20, transcendentals=rows * 4096 * 3
        ),
        name="attention_back",
    )(bounds, lo_row, q, kv, out, dout, lse)


RING = 4
MESH = pl.DeviceIdType.MESH
VMEM = pl.BlockSpec(memory_space=pltpu.VMEM)


def at_seq(index):
    return {"seq": index}


def at_fsdp(index):
    return {"fsdp": index}


def ring_places(s):
    x, y = lax.div(s, RING), lax.rem(s, RING)

    def place(dx, dy):
        return lax.rem(x + dx, 2) * RING + lax.rem(y + dy, RING)

    return {
        "up": place(0, 1),
        "down": place(0, 3),
        "far": place(0, 2),
        "over": place(1, 0),
        "over_up": place(1, 1),
        "over_down": place(1, 3),
        "over_far": place(1, 2),
    }


def greet(targets):
    barrier = pltpu.get_barrier_semaphore()
    for target in targets:
        pl.semaphore_signal(barrier, inc=1, device_id=target, device_id_type=MESH)
    pl.semaphore_wait(barrier, len(targets))


def send(src, dst, sems, index, target):
    copy = pltpu.make_async_remote_copy(
        src_ref=src,
        dst_ref=dst,
        send_sem=sems[0].at[index],
        recv_sem=sems[1].at[index],
        device_id=target,
        device_id_type=MESH,
    )
    copy.start()
    return copy


def steps(*tasks):
    for task in tasks:
        task.step()


class Task:
    def __init__(self, steps):
        self.steps, self.done, self.value = steps, False, None

    def step(self):
        if not self.done:
            try:
                next(self.steps)
            except StopIteration as end:
                self.done, self.value = True, end.value


def run(task, *beside):
    while not task.done:
        task.step()
        for other in beside:
            other.step()
    return task.value


def run_all(*tasks):
    while not all(task.done for task in tasks):
        for task in tasks:
            task.step()


RING_SEMS = 14


def ring_gather(out, s, sems, base):
    p = ring_places(s)
    half = out.shape[1] // 2
    top, bottom = pl.ds(0, half), pl.ds(half, half)
    up, down, over = at_seq(p["up"]), at_seq(p["down"]), at_seq(p["over"])
    copies = []

    def go(place, rows, target):
        block = out.at[place, rows]
        copies.append(send(block, block, sems, base + len(copies), target))
        return copies[-1]

    up_top, down_bottom = go(s, top, up), go(s, bottom, down)
    over_top, over_bottom = go(s, top, over), go(s, bottom, over)
    up_bottom, down_top = go(s, bottom, up), go(s, top, down)
    yield
    up_top.wait_recv()
    far_top = go(p["down"], top, up)
    down_bottom.wait_recv()
    far_bottom = go(p["up"], bottom, down)
    over_top.wait_recv()
    side = [go(p["over"], top, up), go(p["over"], top, down)]
    over_bottom.wait_recv()
    side += [go(p["over"], bottom, up), go(p["over"], bottom, down)]
    up_bottom.wait_recv()
    down_top.wait_recv()
    yield
    far_top.wait_recv()
    side.append(go(p["far"], top, over))
    far_bottom.wait_recv()
    side.append(go(p["far"], bottom, over))
    yield
    for copy in side[:4]:
        copy.wait_recv()
    yield
    for copy in side[4:]:
        copy.wait_recv()
    for copy in copies:
        copy.wait_send()


def ring_scatter(partial, tx, rx, s, sems, base):
    p = ring_places(s)
    half = tx.shape[1] // 2
    top, bottom = pl.ds(0, half), pl.ds(half, half)
    up, down, over = at_seq(p["up"]), at_seq(p["down"]), at_seq(p["over"])
    copies = []

    def cut(value, rows):
        return value[:half] if rows is top else value[half:]

    def go(slot, rows, value, target):
        tx[slot, rows, :] = value.astype(tx.dtype)
        copies.append(
            send(tx.at[slot, rows], rx.at[slot, rows], sems, base + len(copies), target)
        )
        return copies[-1]

    def wide(slot, rows):
        return rx[slot, rows, :].astype(jnp.float32)

    value = partial(p["over_up"])
    second = [go(1, rows, cut(value, rows), up) for rows in (top, bottom)]
    value = partial(p["over_down"])
    third = [go(2, rows, cut(value, rows), down) for rows in (top, bottom)]
    value = partial(p["over_far"])
    first = [go(0, rows, cut(value, rows), over) for rows in (top, bottom)]
    value = partial(p["far"])
    yield
    first[0].wait_recv()
    to_down = go(3, top, cut(value, top) + wide(0, top), down)
    first[1].wait_recv()
    to_up = go(3, bottom, cut(value, bottom) + wide(0, bottom), up)
    to_owner_down, to_owner_up = partial(p["down"]), partial(p["up"])
    fifth = [go(5, bottom, cut(to_owner_down, bottom), down)]
    sixth = [go(6, top, cut(to_owner_up, top), up)]
    value = partial(p["over"])
    yield
    fourth = []
    for k, rows in enumerate((top, bottom)):
        second[k].wait_recv()
        third[k].wait_recv()
        fourth.append(go(4, rows, cut(value, rows) + wide(1, rows) + wide(2, rows), over))
    yield
    to_down.wait_recv()
    fifth.append(go(5, top, cut(to_owner_down, top) + wide(3, top), down))
    to_up.wait_recv()
    sixth.append(go(6, bottom, cut(to_owner_up, bottom) + wide(3, bottom), up))
    value = partial(s)
    yield
    for copy in fourth + fifth + sixth:
        copy.wait_recv()
    value = value + (rx[4].astype(jnp.float32) + rx[5].astype(jnp.float32))
    value = value + rx[6].astype(jnp.float32)
    for copy in copies:
        copy.wait_send()
    return value


def ring_buffers(rows, width):
    return [pltpu.VMEM((7, rows, width), jnp.bfloat16)] * 2


def fsdp_place(g):
    x, z, core = lax.div(g, 8), lax.rem(lax.div(g, 2), RING), lax.rem(g, 2)

    def place(dx, dz, dcore):
        return (
            lax.rem(x + dx, 2) * 8 + lax.rem(z + dz, RING) * 2 + lax.rem(core + dcore, 2)
        )

    return place


def fsdp_neighbours(g):
    place = fsdp_place(g)
    return [at_fsdp(place(*d)) for d in ((1, 0, 0), (0, 1, 0), (0, 3, 0), (0, 0, 1))]


def part_of(ref, rows, cut):
    def view(index, half=None):
        first, count = {None: (0, rows), "top": (0, cut), "bottom": (cut, rows - cut)}[half]
        return ref.at[pl.ds(pl.multiple_of(index * rows + first, 16), count)]

    return view


def fsdp_gather(ref, rows, cut, g, sems, base):
    view, place = part_of(ref, rows, cut), fsdp_place(g)
    over, up, down, pal = fsdp_neighbours(g)
    copies = []

    def go(index, half, sem, target):
        copies.append(send(view(index, half), view(index, half), sems, base + sem, target))
        return copies[-1]

    me = place(0, 0, 0)
    to_over = go(me, None, 16, over)
    to_up, to_down = go(me, None, 0, up), go(me, None, 1, down)
    pals = [go(me, None, 8, pal)]
    yield
    to_over.wait_recv()
    side = place(1, 0, 0)
    side_up, side_down = go(side, None, 2, up), go(side, None, 3, down)
    pals.append(go(side, None, 9, pal))
    yield
    to_up.wait_recv()
    far_up = go(place(0, 3, 0), "top", 4, up)
    pals.append(go(place(0, 3, 0), None, 10, pal))
    to_down.wait_recv()
    far_down = go(place(0, 1, 0), "bottom", 5, down) if cut < rows else None
    pals.append(go(place(0, 1, 0), None, 11, pal))
    yield
    side_up.wait_recv()
    side_far_up = go(place(1, 3, 0), "top", 6, up)
    pals.append(go(place(1, 3, 0), None, 12, pal))
    side_down.wait_recv()
    side_far_down = go(place(1, 1, 0), "bottom", 7, down) if cut < rows else None
    pals.append(go(place(1, 1, 0), None, 13, pal))
    yield
    far_up.wait_recv()
    if far_down is not None:
        far_down.wait_recv()
    pals.append(go(place(0, 2, 0), None, 14, pal))
    yield
    side_far_up.wait_recv()
    if side_far_down is not None:
        side_far_down.wait_recv()
    pals.append(go(place(1, 2, 0), None, 15, pal))
    yield
    for copy in pals:
        copy.wait_recv()
    for copy in copies:
        copy.wait_send()


def fsdp_buffers(rows, cut, width):
    return [
        pltpu.VMEM((8 * rows, width), jnp.bfloat16),
        pltpu.VMEM((2, cut, width), jnp.bfloat16),
        pltpu.VMEM((2, max(rows - cut, 16), width), jnp.bfloat16),
        pltpu.VMEM((5, rows, width), jnp.bfloat16),
    ]


PAIR_ORDER = [(1, 2), (0, 2), (1, 3), (1, 1), (0, 3), (0, 1), (1, 0), (0, 0)]


def pair_slot(pair, rows, index):
    return pair.at[pl.ds(pl.multiple_of(lax.div(index, 2) * rows, 16), rows)]


def pair_send(ref, rows, pair, g, sems, base):
    view, place = part_of(ref, rows, rows), fsdp_place(g)
    pal = fsdp_neighbours(g)[3]
    return [
        send(view(place(dx, dz, 1)), pair_slot(pair, rows, place(dx, dz, 1)), sems, base + k, pal)
        for k, (dx, dz) in enumerate(PAIR_ORDER)
    ]


def pair_add(ref, rows, pair, copies, g):
    view, place = part_of(ref, rows, rows), fsdp_place(g)
    for copy, (dx, dz) in zip(copies, PAIR_ORDER):
        copy.wait_recv()
        slot, part = pair_slot(pair, rows, place(dx, dz, 0)), view(place(dx, dz, 0))
        value = slot[...].astype(jnp.float32) + part[...].astype(jnp.float32)
        slot[...] = value.astype(pair.dtype)
    for copy in copies:
        copy.wait_send()


def fsdp_scatter(ref, rows, cut, buffers, g, sems, base):
    pair, tops, bottoms, full = buffers
    place = fsdp_place(g)
    if pair is None:
        halved = part_of(ref, rows, cut)

        def view(index, half=None):
            return halved(lax.div(index, 2), half)
    else:
        view = part_of(ref, rows, cut)
    over, up, down, pal = fsdp_neighbours(g)
    copies = []

    def go(src, dst, sem, target):
        copies.append(send(src, dst, sems, base + sem, target))
        return copies[-1]

    def wide(part):
        return part[...].astype(jnp.float32)

    def slot(index):
        return pair.at[pl.ds(pl.multiple_of(lax.div(index, 2) * rows, 16), rows)]

    pals = {}
    if pair is not None:
        for k, (dx, dz) in enumerate(PAIR_ORDER):
            index = place(dx, dz, 1)
            pals[dx, dz] = go(view(index), slot(index), k, pal)
        yield

    def paired(dx, dz):
        if pair is None:
            return wide(view(place(dx, dz, 0)))
        pals[dx, dz].wait_recv()
        return wide(view(place(dx, dz, 0))) + wide(slot(place(dx, dz, 0)))

    halves = {}
    for k, dx in enumerate((1, 0)):
        index = place(dx, 2, 0)
        value = paired(dx, 2)
        view(index)[...] = value.astype(jnp.bfloat16)
        halves[dx, "top"] = go(view(index, "top"), tops.at[dx], 8 + 2 * k, down)
        if cut < rows:
            halves[dx, "bottom"] = go(view(index, "bottom"), bottoms.at[dx], 9 + 2 * k, up)
    yield
    fulls = {}
    for k, dx in enumerate((1, 0)):
        index = place(dx, 3, 0)
        value = paired(dx, 3)
        halves[dx, "top"].wait_recv()
        view(index, "top")[...] = (value[:cut] + wide(tops.at[dx])).astype(jnp.bfloat16)
        if cut < rows:
            view(index, "bottom")[...] = value[cut:].astype(jnp.bfloat16)
        fulls[dx, "down"] = go(view(index), full.at[2 * dx], 12 + 2 * k, down)
        index = place(dx, 1, 0)
        value = paired(dx, 1)
        if cut < rows:
            halves[dx, "bottom"].wait_recv()
            view(index, "top")[...] = value[:cut].astype(jnp.bfloat16)
            view(index, "bottom")[...] = (value[cut:] + wide(bottoms.at[dx])).astype(jnp.bfloat16)
        else:
            view(index)[...] = value.astype(jnp.bfloat16)
        fulls[dx, "up"] = go(view(index), full.at[2 * dx + 1], 13 + 2 * k, up)
        yield
    index = place(1, 0, 0)
    value = paired(1, 0)
    fulls[1, "down"].wait_recv()
    fulls[1, "up"].wait_recv()
    view(index)[...] = (value + wide(full.at[2]) + wide(full.at[3])).astype(jnp.bfloat16)
    last = go(view(index), full.at[4], 16, over)
    value = paired(0, 0)
    yield
    fulls[0, "down"].wait_recv()
    fulls[0, "up"].wait_recv()
    value = value + wide(full.at[0]) + wide(full.at[1])
    yield
    last.wait_recv()
    value = value + wide(full.at[4])
    for copy in copies:
        copy.wait_send()
    return value


def sem_pair(count):
    return [pltpu.SemaphoreType.DMA((count,)), pltpu.SemaphoreType.DMA((count,))]


def others(me, count):
    return [lax.rem(me + k, count) for k in range(1, count)]


def exchange(blocks, into, me, peers, at, sems, base):
    return [
        send(blocks.at[p], into.at[me], sems, base + k, at(p)) for k, p in enumerate(peers)
    ]


def spread(block, into, me, peers, at, sems, base):
    return [send(block, into.at[me], sems, base + k, at(p)) for k, p in enumerate(peers)]


def swap_rows(src, dst, sems, index, target, alone):
    away = pltpu.make_async_remote_copy(
        src_ref=src,
        dst_ref=dst,
        send_sem=sems[0].at[index],
        recv_sem=sems[1].at[index],
        device_id=target,
        device_id_type=MESH,
    )
    here = pltpu.make_async_copy(src, dst, sems[0].at[index])
    pl.when(jnp.logical_not(alone))(away.start)
    pl.when(alone)(here.start)

    def wait():
        pl.when(jnp.logical_not(alone))(away.wait)
        pl.when(alone)(here.wait)

    return wait


def head_holder(g, s):
    return {"fsdp": lax.rem(g, 2) * 8 + s, "seq": lax.div(g, 2)}


def head_owner(g, s):
    return {"fsdp": 2 * s + lax.div(g, 8), "seq": lax.rem(g, 8)}


def greet_all(targets, pair, alone):
    barrier = pltpu.get_barrier_semaphore()
    for target in targets:
        pl.semaphore_signal(barrier, inc=1, device_id=target, device_id_type=MESH)

    @pl.when(jnp.logical_not(alone))
    def _():
        for target in pair:
            pl.semaphore_signal(barrier, inc=1, device_id=target, device_id_type=MESH)

    pl.semaphore_wait(barrier, len(targets) + jnp.where(alone, 0, 2))


def compact(blocks, rows):
    total = blocks.shape[0]
    shape = (total // 16 * rows, total)
    source = lax.broadcasted_iota(jnp.int32, shape, 1)
    place = lax.shift_right_logical(source, 4) * rows + (source & 15)
    keep = (place == lax.broadcasted_iota(jnp.int32, shape, 0)) & ((source & 15) < rows)
    return nn(keep.astype(jnp.bfloat16), blocks).astype(jnp.bfloat16)


def expand(rows_in, rows):
    shape = (rows_in.shape[0] // rows * 16, rows_in.shape[0])
    target = lax.broadcasted_iota(jnp.int32, shape, 0)
    place = lax.shift_right_logical(target, 4) * rows + (target & 15)
    keep = (place == lax.broadcasted_iota(jnp.int32, shape, 1)) & ((target & 15) < rows)
    return nn(keep.astype(jnp.bfloat16), rows_in).astype(jnp.bfloat16)


def unit_order(row_axis):
    mixed = lax.broadcasted_iota(jnp.int32, (512, 512), 1 - row_axis)
    plain = lax.broadcasted_iota(jnp.int32, (512, 512), row_axis)
    f = lax.shift_right_logical(mixed, 5)
    e = lax.shift_right_logical(mixed, 3) & 3
    return (e * 128 + f * 8 + (mixed & 7) == plain).astype(jnp.bfloat16)


def owner_units(s, total, owners):
    shape = (total, total // owners)
    unit = lax.broadcasted_iota(jnp.int32, shape, 0)
    place = lax.broadcasted_iota(jnp.int32, shape, 1)
    source = lax.shift_right_logical(place, 3) * (8 * owners) + s * 8 + (place & 7)
    return (unit == source).astype(jnp.bfloat16)


def scale_of(values):
    return lax.rsqrt(jnp.mean(values * values, axis=-1, keepdims=True) + EPS)


def rms_back(d_normed, unit, scale, gain):
    d_unit = d_normed * gain
    return scale * (d_unit - unit * jnp.mean(d_unit * unit, axis=-1, keepdims=True))


def fold(dst, first_row, column, value, width):
    rows = value.shape[0]
    for k in range(value.shape[1] // width):
        at = pl.ds(pl.multiple_of(first_row + k * rows, 16), rows)
        dst[at, column : column + width] = value[:, k * width : (k + 1) * width]


def unfold(src, first_row, column, rows, groups, width):
    parts = []
    for k in range(groups):
        at = pl.ds(pl.multiple_of(first_row + k * rows, 16), rows)
        parts.append(src[at, column : column + width])
    return jnp.concatenate(parts, axis=1)


def rows_at(place, count=128):
    return pl.ds(pl.multiple_of(place * count, count), count)


def kernel_params(collective_id):
    return pltpu.CompilerParams(
        collective_id=collective_id, has_side_effects=True, vmem_limit_bytes=52 << 20
    )


def array(shape, dtype=jnp.bfloat16):
    return jax.ShapeDtypeStruct(shape, dtype)


SMALL = 3 * WIDTH
KEYS = 4 * WIDTH


def window_steps(out_ref, rows, g, sems, base):
    core = lax.rem(g, 2)
    after, partner = at_fsdp(lax.rem(g + 2, 16)), at_fsdp(g + 1 - 2 * core)

    def part(index):
        return out_ref.at[index, rows]

    first = send(part(4), part(2), sems, base, after)
    yield
    first.wait_recv()
    second = send(part(2), part(0), sems, base + 1, after)
    third = send(part(4 - 2 * core), part(3), sems, base + 2, partner)
    yield
    second.wait_recv()
    fourth = send(part(2 - 2 * core), part(1), sems, base + 3, partner)
    yield
    third.wait_recv()
    fourth.wait_recv()
    for copy in (first, second, third, fourth):
        copy.wait_send()


def window_greeting(g):
    core = lax.rem(g, 2)
    return [at_fsdp(i) for i in (lax.rem(g + 2, 16), lax.rem(g + 14, 16), g + 1 - 2 * core)]


def start_kernel(
    tokens_ref, columns_ref, gate_ref, up_ref, wout_ref, chosen_ref, cotangent_ref,
    normed_out, q_ref, window_ref, weight_out, small_ref, rows_ref, wout_all_ref, chosen_out_ref,
    cotangent_out,
    all_ref, normed_ref, weight_ref, columns_in, experts_tx, experts_in, wout_in, mixed, cotangent_all,
    out_sems, send_sems, recv_sems,
):
    s, g = lax.axis_index("seq"), lax.axis_index("fsdp")
    p = ring_places(s)
    peers = others(s, 8)
    sems = (send_sems, recv_sems)
    holder, owner = head_holder(g, s), head_owner(g, s)
    alone = (holder["fsdp"] == g) & (holder["seq"] == s)
    greet_all(
        [at_seq(q) for q in peers] + fsdp_neighbours(g) + window_greeting(g),
        (holder, owner),
        alone,
    )
    copies = exchange(columns_ref, columns_in, s, peers, at_seq, sems, 0)
    wait_rows = swap_rows(
        wout_ref, wout_in, sems, 45, holder, alone
    )
    all_ref[s] = tokens_ref[...]
    tokens_in = Task(ring_gather(all_ref, s, sems, 7))
    tokens_in.step()
    chosen_copies = spread(chosen_ref, chosen_out_ref, s, peers, at_seq, sems, 46)
    chosen_out_ref[s] = chosen_ref[...]
    columns_in[s] = columns_ref[s]
    for copy in copies:
        copy.wait_recv()
    weight_ref[rows_at(g, 96), : KEYS + 128] = compact(columns_in[...].reshape(128, KEYS + 128), 12)
    wait_rows()
    fold(weight_ref, g * 96, KEYS + 128, wout_in[...], 256)
    columns_gather = Task(fsdp_gather(weight_ref, 96, 48, g, sems, 21))
    columns_gather.step()
    cotangent_all[s] = cotangent_ref[...]
    steps(columns_gather, tokens_in, columns_gather)
    steps(columns_gather, tokens_in)
    cotangent_in = Task(ring_gather(cotangent_all, s, sems, 78))
    cotangent_in.step()
    run(columns_gather)
    out_copies = [pltpu.make_async_copy(weight_ref.at[:, : KEYS + 128], weight_out, out_sems.at[8])]
    out_copies[0].start()
    pick = lax.broadcasted_iota(jnp.int32, (8, 2 * WIDTH), 0) + (SMALL - 2 * WIDTH)
    pick = (pick == lax.broadcasted_iota(jnp.int32, (8, 2 * WIDTH), 1)).astype(jnp.bfloat16)
    small_ref[...] = nt(pick, weight_ref[:, 2 * WIDTH : 4 * WIDTH])
    gain = small_ref[0:1, :]

    def project(place):
        values = all_ref[place].astype(jnp.float32)
        normed = (values * scale_of(values) * gain).astype(jnp.bfloat16)
        normed_ref[rows_at(place), :] = normed
        result = nn(normed, weight_ref[:, : KEYS + 128]).astype(jnp.bfloat16)
        q_ref[rows_at(place), :] = result[:, :SMALL]
        window_ref[4, rows_at(place), :] = result[:, KEYS:]
        copy = pltpu.make_async_copy(
            normed_ref.at[rows_at(place)],
            normed_out.at[rows_at(place)],
            out_sems.at[len(out_copies) - 1],
        )
        copy.start()
        out_copies.append(copy)

    project(s)
    for name in ("down", "up", "far"):
        project(p[name])
    side = lax.div(s, RING)
    near = Task(window_steps(window_ref, rows_at(side, 512), g, sems, 53))
    near.step()
    project(p["over"])
    tokens_in.step()
    project(p["over_up"])
    project(p["over_down"])
    run(tokens_in)
    project(p["over_far"])
    away = Task(window_steps(window_ref, rows_at(1 - side, 512), g, sems, 74))
    away.step()
    cotangent_in.step()
    experts = jnp.concatenate(
        [gate_ref[...].reshape(64, gate_ref.shape[2]), up_ref[...].reshape(64, gate_ref.shape[2])], axis=0
    )

    @pl.loop(0, 8)
    def _(place):
        units = owner_units(place, experts.shape[1], 8)
        experts_tx[place] = nn(experts, units).astype(jnp.bfloat16)

    copies += exchange(experts_tx, experts_in, s, peers, at_seq, sems, 38)
    experts_in[s] = experts_tx[s]
    steps(near, away, cotangent_in)

    @pl.loop(0, 16)
    def _(f):
        mixed[rows_at(f, 16), :] = unfold(weight_ref, f * 96, KEYS + 128, 16, 6, 256)

    wout_all_ref[...] = compact(mixed[...], 12)
    steps(near, away)
    for copy in copies[7:]:
        copy.wait_recv()
    for e in range(8):
        rows = experts_in[:, e * 16 : (e + 1) * 16, :].reshape(128, 128)
        rows_ref[:, e * 128 : (e + 1) * 128] = compact(rows, 12)
    run_all(near, away, cotangent_in)
    out_copies.append(pltpu.make_async_copy(cotangent_all, cotangent_out, out_sems.at[9]))
    out_copies[-1].start()
    for copy in chosen_copies:
        copy.wait_recv()
    for copy in copies + chosen_copies:
        copy.wait_send()
    for copy in out_copies:
        copy.wait()


ANY = pl.BlockSpec(memory_space=pl.ANY)


def start(tokens, columns, gate, up, wout, chosen, cotangent):
    own, model = tokens.shape
    rows = 8 * own
    width = columns.shape[2]
    return pl.pallas_call(
        start_kernel,
        in_specs=[VMEM] * 7,
        out_specs=[ANY, VMEM, VMEM, ANY, VMEM, VMEM, VMEM, VMEM, ANY],
        out_shape=[
            array((rows, model)),
            array((rows, SMALL)),
            array((LOOK + 1, rows, width - KEYS)),
            array((model, width)),
            array((8, model), jnp.float32),
            array((96, gate.shape[2])),
            array((192, model)),
            array((8,) + chosen.shape, jnp.float32),
            array((8, own, model)),
        ],
        scratch_shapes=[
            pltpu.VMEM((8, own, model), jnp.bfloat16),
            pltpu.VMEM((rows, model), jnp.bfloat16),
            pltpu.VMEM((model, width + 256), jnp.bfloat16),
            pltpu.VMEM(columns.shape, jnp.bfloat16),
            pltpu.VMEM((8, 128, 128), jnp.bfloat16),
            pltpu.VMEM((8, 128, 128), jnp.bfloat16),
            pltpu.VMEM(wout.shape, jnp.bfloat16),
            pltpu.VMEM((256, model), jnp.bfloat16),
            pltpu.VMEM((8, own, model), jnp.bfloat16),
            pltpu.SemaphoreType.DMA((10,)),
            *sem_pair(92),
        ],
        compiler_params=kernel_params(1),
        name="start",
    )(tokens, columns, gate, up, wout, chosen, cotangent)


def window_back_steps(d_ref, out_ref, rows, tx, rx, g, sems, base):
    core = lax.rem(g, 2)
    before, partner = at_fsdp(lax.rem(g + 14, 16)), at_fsdp(g + 1 - 2 * core)
    odd = core.astype(jnp.float32)
    even = 1.0 - odd

    def wide(slot):
        return rx[slot, rows, :].astype(jnp.float32)

    def go(slot, value, sem, target):
        tx[slot, rows, :] = value.astype(jnp.bfloat16)
        return send(tx.at[slot, rows], rx.at[slot, rows], sems, base + sem, target)

    one = go(1, d_ref[1, rows, :], 1, partner)
    two = go(2, d_ref[3, rows, :], 2, partner)
    yield
    one.wait_recv()
    zero = go(0, d_ref[0, rows, :] + odd * wide(1), 0, before)
    yield
    two.wait_recv()
    zero.wait_recv()
    value = d_ref[2, rows, :] + wide(0) + odd * wide(2) + even * wide(1)
    three = go(3, value, 3, before)
    yield
    three.wait_recv()
    out_ref[rows, :] = (d_ref[4, rows, :] + wide(3) + even * wide(2)).astype(jnp.bfloat16)
    for copy in (zero, one, two, three):
        copy.wait_send()


def moe_kernel(
    attended_ref, wout_ref, tokens_ref, small_ref, rows_ref, down_rows_ref, cotangent_in, chosen_ref,
    resid_ref, moe_out, d_resid_ref, d_attended_ref, router_ref, grad_wout_ref, bulk_out,
    normed_ref, shared_ref, d_ref, branch_ref, cotangent_ref, gate_up_ref, down_mixed, down_ref,
    moe_ref, bulk, pair, grad_down, grad_wout, probs_ref, share_tx, share_in, logits_ref,
    tx_a, rx_a, tx_b, rx_b,
    local_sems, send_sems, recv_sems,
):
    s, g = lax.axis_index("seq"), lax.axis_index("fsdp")
    p = ring_places(s)
    peers = others(s, 8)
    sems = (send_sems, recv_sems)
    cotangent_copy = pltpu.make_async_copy(cotangent_in, cotangent_ref, local_sems.at[0])
    cotangent_copy.start()
    greet([at_seq(q) for q in peers] + fsdp_neighbours(g))
    model = tokens_ref.shape[1]
    units = down_ref.shape[0]
    per = units // EXPERTS

    def branch_part(place):
        return nn(attended_ref[rows_at(place), :], wout_ref[...])

    branch_sum = Task(ring_scatter(branch_part, tx_a, rx_a, s, sems, 0))
    branch_sum.step()
    gate_up_ref[rows_at(g, 96), : 2 * units] = rows_ref[...]
    fold(gate_up_ref, g * 96, 2 * units, down_rows_ref[...], 512)
    weight_gather = Task(fsdp_gather(gate_up_ref, 96, 48, g, sems, 107))
    steps(weight_gather, weight_gather, branch_sum)
    branch = run(branch_sum, weight_gather)
    resid = tokens_ref[...].astype(jnp.float32) + branch
    resid_ref[...] = resid
    gain = small_ref[1:2, :]
    router = small_ref[...].astype(jnp.bfloat16)
    normed_ref[s] = (resid * scale_of(resid) * gain).astype(jnp.bfloat16)
    gather = Task(ring_gather(normed_ref, s, sems, 14))
    gather.step()
    run(weight_gather)

    @pl.loop(0, 16)
    def _(f):
        down_mixed[rows_at(f, 32), :] = unfold(gate_up_ref, f * 96, 2 * units, 32, 3, 512)

    down_ref[...] = nn(unit_order(0), down_mixed[...]).astype(jnp.bfloat16)
    cotangent_copy.wait()

    def block(place):
        x = normed_ref[place]
        logits = nt(router, x)
        logits = jnp.concatenate([logits[2 : 2 + EXPERTS], jnp.full((4, 128), NEGATIVE)], axis=0)
        probs = jnp.exp(logits - jnp.max(logits, axis=0, keepdims=True))
        probs = probs / jnp.sum(probs, axis=0, keepdims=True)
        probs_ref[place] = probs
        share = jnp.concatenate([probs * chosen_ref[place], jnp.zeros((120, 128))], axis=0)
        share = jnp.transpose(share)
        plain = nt(cotangent_ref[place], down_ref[...])
        both = nn(x, gate_up_ref[:, : 2 * units])
        sums = []
        for e in range(EXPERTS):
            at = slice(e * per, (e + 1) * per)
            gate, up = both[:, at], both[:, units + e * per : units + (e + 1) * per]
            wide = jnp.broadcast_to(share[:, e : e + 1], gate.shape)
            sigmoid = 1.0 / (1.0 + jnp.exp(-gate))
            silu = gate * sigmoid
            hidden = (silu * up).astype(jnp.bfloat16).astype(jnp.float32)
            shared_ref[rows_at(place), at] = (hidden * wide).astype(jnp.bfloat16)
            sums.append(jnp.sum(plain[:, at] * hidden, axis=1, keepdims=True))
            d_hidden = plain[:, at] * wide
            d_gate = d_hidden * up * sigmoid * (1.0 + gate * (1.0 - sigmoid))
            d_ref[rows_at(place), at] = d_gate.astype(jnp.bfloat16)
            d_ref[rows_at(place), units + e * per : units + (e + 1) * per] = (
                d_hidden * silu
            ).astype(jnp.bfloat16)
        sums = jnp.concatenate(sums + [jnp.zeros((128, 128 - EXPERTS))], axis=1)
        share_tx[place] = jnp.transpose(sums)[:8]

    block(s)
    gather.step()
    block(p["down"])
    block(p["up"])
    gather.step()
    block(p["over"])
    block(p["far"])
    gather.step()
    late = [p["over_up"], p["over_down"], p["over_far"]]

    moe_copy = pltpu.make_async_copy(moe_ref, moe_out, local_sems.at[1])
    bulk_copy = pltpu.make_async_copy(pair, bulk_out, local_sems.at[2])

    def weight_grads():
        @pl.loop(0, model // 128)
        def _(j):
            normed = normed_ref[:, :, rows_at(j)].reshape(8 * 128, 128)
            bulk[rows_at(j), : 2 * units] = tn(normed, d_ref[...]).astype(jnp.bfloat16)

        yield
        shared, grad = shared_ref[...], cotangent_ref[...].reshape(8 * 128, model)
        value = tn(shared, grad).astype(jnp.bfloat16)
        grad_down[...] = nn(unit_order(1), value).astype(jnp.bfloat16)

        @pl.loop(0, 16)
        def _(f):
            fold(bulk, f * 96, 2 * units, grad_down[rows_at(f, 32), :], 512)

        pairs = pair_send(bulk, 96, pair, g, sems, 124)
        yield
        moe_ref[...] = nn(shared_ref[...], down_ref[...]).astype(jnp.bfloat16)
        moe_copy.start()
        yield
        pair_add(bulk, 96, pair, pairs, g)
        bulk_copy.start()

    grads = Task(weight_grads())

    def normed_part(place):
        if late:
            late.pop(0)
            if not late:
                run(gather)
            block(place)
        return nt(d_ref[rows_at(place), :], gate_up_ref[:, : 2 * units])

    d_normed_sum = Task(ring_scatter(normed_part, tx_b, rx_b, s, sems, 42))
    d_normed_sum.step()
    shares = exchange(share_tx, share_in, s, peers, at_seq, sems, 28)
    share_in[s] = share_tx[s]
    grads.step()
    steps(d_normed_sum, d_normed_sum, grads, d_normed_sum, grads)
    d_normed = run(d_normed_sum)
    for copy in shares:
        copy.wait_recv()

    d_router = jnp.sum(share_in[...], axis=0) * chosen_ref[s]
    probs = probs_ref[s]
    d_logits = probs * (d_router - jnp.sum(probs * d_router, axis=0, keepdims=True))
    d_logits = d_logits.astype(jnp.bfloat16)
    logits_ref[s] = d_logits.astype(jnp.float32)
    spreads = spread(logits_ref.at[s], logits_ref, s, peers, at_seq, sems, 35)
    padded = jnp.concatenate([jnp.zeros((2, 128), jnp.bfloat16), d_logits[:6]], axis=0)
    d_normed = d_normed + tn(padded, router)
    resid = resid_ref[...]
    scale = scale_of(resid)
    d_resid = cotangent_ref[s].astype(jnp.float32) + rms_back(
        d_normed, resid * scale, scale, gain
    )
    d_resid_ref[...] = d_resid
    branch_ref[s] = d_resid.astype(jnp.bfloat16)
    gather = Task(ring_gather(branch_ref, s, sems, 93))
    gather.step()

    grad_wout[...] = jnp.zeros_like(grad_wout)

    def d_attended(place):
        d_branch = branch_ref[place]
        d_attended_ref[rows_at(place), :] = nt(d_branch, wout_ref[...]).astype(jnp.bfloat16)
        grad_wout[...] += tn(attended_ref[rows_at(place), :], d_branch)

    d_attended(s)
    gather.step()
    steps(grads)
    for name in ("down", "up", "over"):
        d_attended(p[name])
    steps(grads, gather)
    for copy in spreads:
        copy.wait_recv()
    total = jnp.zeros((8, model), jnp.float32)
    for q in range(8):
        total += nn(logits_ref[q].astype(jnp.bfloat16), normed_ref[q])
    router_ref[...] = total
    d_attended(p["far"])
    steps(grads, gather)
    d_attended(p["over_up"])
    d_attended(p["over_down"])
    run(grads)
    run(gather)
    d_attended(p["over_far"])
    grad_wout_ref[...] = expand(grad_wout[...].astype(jnp.bfloat16), 12)
    moe_copy.wait()
    bulk_copy.wait()
    for copy in shares + spreads:
        copy.wait_send()


def moe(attended, wout, tokens, small, rows, down_rows, cotangent, chosen):
    own, model = tokens.shape
    group = 8 * own
    width, units = rows.shape[1], 16 * down_rows.shape[0]
    f32, bf16 = jnp.float32, jnp.bfloat16
    tiny = pltpu.VMEM((8, 8, own), f32)
    return pl.pallas_call(
        moe_kernel,
        in_specs=[VMEM] * 6 + [ANY, VMEM],
        out_specs=[VMEM, ANY] + [VMEM] * 4 + [ANY],
        out_shape=[
            array((own, model), f32),
            array((group, model)),
            array((own, model), f32),
            array((group, SMALL)),
            array((8, model), f32),
            array((256, model)),
            array((model // 2, width + 512)),
        ],
        scratch_shapes=[
            pltpu.VMEM((8, own, model), bf16),
            pltpu.VMEM((group, units), bf16),
            pltpu.VMEM((group, width), bf16),
            pltpu.VMEM((8, own, model), bf16),
            pltpu.VMEM((8, own, model), bf16),
            pltpu.VMEM((model, width + 512), bf16),
            pltpu.VMEM((units, model), bf16),
            pltpu.VMEM((units, model), bf16),
            pltpu.VMEM((group, model), bf16),
            pltpu.VMEM((model, width + 512), bf16),
            pltpu.VMEM((model // 2, width + 512), bf16),
            pltpu.VMEM((units, model), bf16),
            pltpu.VMEM((192, model), f32),
            tiny,
            tiny,
            tiny,
            tiny,
            *ring_buffers(own, model),
            *ring_buffers(own, model),
            pltpu.SemaphoreType.DMA((5,)),
            *sem_pair(132),
        ],
        compiler_params=kernel_params(2),
        name="moe",
    )(attended, wout, tokens, small, rows, down_rows, cotangent, chosen)


def finish_kernel(
    dq_ref, d_window_ref, weight_in, normed_in, router_ref, wout_ref, bulk_in, d_resid_ref, tokens_ref,
    small_ref,
    grad_input_ref, columns_out, gate_out, up_out, wout_out, down_out,
    weight_ref, normed_ref, bulk, d_ref, grads, columns_tx, experts_tx, experts_in, wout_tx,
    wtx, wrx, tx, rx,
    tops_a, bottoms_a, full_a, pair_b, tops_b, bottoms_b, full_b,
    local_sems, send_sems, recv_sems,
):
    s, g = lax.axis_index("seq"), lax.axis_index("fsdp")
    peers = others(s, 8)
    sems = (send_sems, recv_sems)
    bulk_copy = pltpu.make_async_copy(bulk_in, bulk, local_sems.at[2])
    bulk_copy.start()
    normed_copy = pltpu.make_async_copy(normed_in, normed_ref, local_sems.at[0])
    normed_copy.start()
    weight_copy = pltpu.make_async_copy(weight_in, weight_ref, local_sems.at[1])
    weight_copy.start()
    holder, owner = head_holder(g, s), head_owner(g, s)
    alone = (holder["fsdp"] == g) & (holder["seq"] == s)
    greet_all(
        [at_seq(q) for q in peers] + fsdp_neighbours(g) + window_greeting(g),
        (holder, owner),
        alone,
    )
    d_keyval = d_ref.at[:, KEYS:]
    halves = [
        Task(window_back_steps(d_window_ref, d_keyval, pl.ds(k * 512, 512), wtx, wrx, g, sems, 4 * k))
        for k in range(2)
    ]

    def windows():
        for half in halves:
            half.step()

    windows()
    d_ref[:, :SMALL] = dq_ref[...]
    d_ref[:, SMALL:KEYS] = jnp.zeros((d_ref.shape[0], WIDTH), jnp.bfloat16)
    bulk_copy.wait()
    bulk_sum = Task(
        fsdp_scatter(bulk, 96, 48, (None, tops_a, bottoms_a, full_a), g, sems, 15)
    )
    windows()
    normed_copy.wait()
    model = normed_ref.shape[1]

    def weight_grad(columns):
        return tn(d_ref[:, columns], normed_ref[...])

    value = weight_grad(slice(0, KEYS))
    row = lax.broadcasted_iota(jnp.int32, (KEYS, 1), 0)
    router = jnp.concatenate(
        [jnp.zeros((SMALL + 2, model)), router_ref[...], jnp.zeros((KEYS - SMALL - 10, model))], axis=0
    )
    grads[:, :KEYS] = jnp.transpose(jnp.where(row < SMALL, value, router)).astype(jnp.bfloat16)

    @pl.loop(0, 16)
    def _(f):
        fold(grads, f * 96, KEYS + 128, wout_ref[rows_at(f, 16), :], 256)

    windows()
    bulk_sum.step()
    weight_copy.wait()
    run_all(*halves)

    def partial(place):
        return nt(d_ref[rows_at(place), :], weight_ref[...])

    total = Task(ring_scatter(partial, tx, rx, s, sems, 49))
    total.step()
    value = weight_grad(slice(KEYS, KEYS + 2 * WIDTH))
    grads[:, KEYS : KEYS + 128] = jnp.transpose(value).astype(jnp.bfloat16)
    sums = Task(fsdp_scatter(grads, 96, 48, (pair_b, tops_b, bottoms_b, full_b), g, sems, 63))
    sums.step()
    steps(sums, sums, bulk_sum, total, sums, bulk_sum, total, sums, bulk_sum)
    value = run(sums)
    wide = value[:, : KEYS + 128].astype(jnp.bfloat16)
    columns_tx[...] = expand(wide, 12).reshape(columns_tx.shape)
    copies = exchange(columns_tx, columns_out, s, peers, at_seq, sems, 87)
    columns_out[s] = columns_tx[s]
    wout_tx[...] = jnp.concatenate(
        [value[k * 16 : (k + 1) * 16, KEYS + 128 :] for k in range(6)], axis=1
    ).astype(jnp.bfloat16)
    wait_rows = swap_rows(wout_tx, wout_out, sems, 94, owner, alone)
    total.step()
    value = run(bulk_sum)
    width = gate_out.shape[2]
    units = width // 8
    wide = value[:, :width].astype(jnp.bfloat16)
    experts_tx[...] = expand(wide, 12).reshape(experts_tx.shape)
    expert_copies = exchange(experts_tx, experts_in, s, peers, at_seq, sems, 8)
    experts_in[s] = experts_tx[s]
    down_out[...] = jnp.concatenate(
        [value[k * 32 : (k + 1) * 32, width:] for k in range(3)], axis=1
    )
    d_normed = run(total)
    values = tokens_ref[...].astype(jnp.float32)
    scale = scale_of(values)
    grad_input_ref[...] = d_resid_ref[...] + rms_back(
        d_normed, values * scale, scale, small_ref[0:1, :]
    )
    for copy in expert_copies:
        copy.wait_recv()
    back = jnp.zeros((128, gate_out.shape[2]), jnp.float32)
    for place in range(8):
        block = jnp.concatenate(
            [experts_in[place, :, e * units : (e + 1) * units] for e in range(8)], axis=0
        )
        back += nt(block, owner_units(place, gate_out.shape[2], 8))
    for e in range(EXPERTS):
        gate_out[e] = back[e * 16 : e * 16 + 12]
        up_out[e] = back[(EXPERTS + e) * 16 : (EXPERTS + e) * 16 + 12]
    wait_rows()
    for copy in copies:
        copy.wait_recv()
    for copy in copies + expert_copies:
        copy.wait_send()


def finish(dq, d_window, weight, normed, router, wout, bulk, d_resid, tokens, small):
    own, model = tokens.shape
    rows = dq.shape[0]
    width = weight.shape[1]
    units = bulk.shape[1] - 512
    blocks = (8, 16, units)
    keyval = d_window.shape[1:]
    bf16, f32 = jnp.bfloat16, jnp.float32
    return pl.pallas_call(
        finish_kernel,
        in_specs=[VMEM, VMEM, ANY, ANY, VMEM, VMEM, ANY] + [VMEM] * 3,
        out_specs=[VMEM] * 6,
        out_shape=[
            array((own, model), f32),
            array((8, 16, width)),
            array((EXPERTS, 12, units), f32),
            array((EXPERTS, 12, units), f32),
            array((16, model)),
            array((32, model), f32),
        ],
        scratch_shapes=[
            pltpu.VMEM(weight.shape, bf16),
            pltpu.VMEM(normed.shape, bf16),
            pltpu.VMEM(bulk.shape, bf16),
            pltpu.VMEM((rows, width), bf16),
            pltpu.VMEM((model, width + 256), bf16),
            pltpu.VMEM((8, 16, width), bf16),
            pltpu.VMEM(blocks, bf16),
            pltpu.VMEM(blocks, bf16),
            pltpu.VMEM((16, model), bf16),
            pltpu.VMEM((4,) + keyval, bf16),
            pltpu.VMEM((4,) + keyval, bf16),
            *ring_buffers(own, model),
            *fsdp_buffers(model // 16, 48, bulk.shape[1])[1:],
            *fsdp_buffers(model // 16, 48, width + 256),
            pltpu.SemaphoreType.DMA((3,)),
            *sem_pair(95),
        ],
        compiler_params=kernel_params(3),
        name="finish",
    )(dq, d_window, weight, normed, router, wout, bulk, d_resid, tokens, small)


def pad_rows(x, axis):
    pads = [(0, 0)] * x.ndim
    pads[axis] = (0, 16 - x.shape[axis])
    return jnp.pad(x, pads)


def on_device(
    tokens,
    gain_one,
    w_qkv,
    w_out,
    gain_two,
    w_router,
    w_gate,
    w_up,
    w_down,
    doc_starts,
    routes,
    cotangent,
):
    seq = lax.axis_size("seq")
    group_index = lax.axis_index("fsdp")
    own, model = tokens.shape
    group_rows = own * seq
    experts, own_model, ff = w_gate.shape
    bf16, f32 = jnp.bfloat16, jnp.float32

    qkv_parts = jnp.transpose(w_qkv.reshape(own_model, seq, 5 * WIDTH), (1, 0, 2))
    small = jnp.concatenate([gain_one[:, None], gain_two[:, None], w_router], axis=1)
    small = jnp.pad(small, ((0, 0), (0, WIDTH - small.shape[1])))
    columns = jnp.concatenate(
        [
            qkv_parts[:, :, :SMALL],
            jnp.broadcast_to(small[None], (seq,) + small.shape),
            qkv_parts[:, :, SMALL:],
        ],
        axis=2,
    )
    expert_ids = jnp.arange(8, dtype=jnp.int32)
    chosen = jnp.sum((routes[None, :, :] == expert_ids[:, None, None]).astype(f32), axis=2)
    normed_one, queries, window, weight, small, rows, out_weight, chosen, cotangent_all = start(
        tokens,
        pad_rows(columns, 1),
        pad_rows(w_gate, 1),
        pad_rows(w_up, 1),
        pad_rows(w_out, 0),
        chosen,
        cotangent,
    )

    window = window.reshape((LOOK + 1) * group_rows, 2 * WIDTH)
    positions = group_index * group_rows + jnp.arange(group_rows, dtype=jnp.int32)
    begins = jnp.max(
        jnp.where(doc_starts[:, None] <= positions[None, :], doc_starts[:, None], 0), axis=0
    )
    lo = begins - (group_index - LOOK) * group_rows
    blocks = group_rows // BQ
    lo_blocks = lo.reshape(blocks, BQ)
    ends = LOOK * group_rows + jnp.arange(blocks, dtype=jnp.int32) * BQ

    def bounds(step):
        diag = ends // step
        first = jnp.minimum(lo_blocks[:, 0] // step, diag)
        full = jnp.minimum((lo_blocks[:, -1] + step - 1) // step, diag)
        return jnp.stack([first, full, diag, (ends + BQ + step - 1) // step], axis=1)

    attended, lse = attention(bounds(BK), lo[None, :], queries, window)

    residual, moe_out, d_resid, d_attended, grad_router, grad_w_out, bulk = moe(
        attended, out_weight, tokens, small, rows, w_down.reshape(-1, model), cotangent_all, chosen
    )
    moe_out = lax.psum_scatter(moe_out, "seq", scatter_dimension=0, tiled=True)
    output = (residual + moe_out.astype(f32)).astype(bf16)

    d_queries, d_window = attention_back(
        bounds(BK_BACK), lo[None, :], queries, window, attended, d_attended, lse
    )
    grad_input, columns, shard_gate, shard_up, shard_out, shard_down = finish(
        d_queries,
        d_window.reshape(LOOK + 1, group_rows, 2 * WIDTH),
        weight, normed_one, grad_router, grad_w_out, bulk, d_resid, tokens, small,
    )

    shard_down = shard_down.reshape(experts, -1, model)
    shard_out = shard_out[:own_model].astype(f32)
    columns = columns[:, :own_model]
    shard_qkv = jnp.concatenate([columns[:, :, :SMALL], columns[:, :, KEYS:]], axis=2)
    shard_qkv = jnp.transpose(shard_qkv, (1, 0, 2)).reshape(own_model, -1).astype(f32)
    shard_router = columns[0, :, SMALL + 2 : SMALL + 2 + experts].astype(f32)

    shard_gain_one = jnp.sum(w_qkv.astype(f32) * shard_qkv, axis=1)
    shard_gain_one = shard_gain_one / gain_one.astype(f32)
    shard_gain_two = jnp.sum(w_router.astype(f32) * shard_router, axis=1)
    shard_gain_two += jnp.sum(w_gate.astype(f32) * shard_gate, axis=(0, 2))
    shard_gain_two += jnp.sum(w_up.astype(f32) * shard_up, axis=(0, 2))
    shard_gain_two = shard_gain_two / gain_two.astype(f32)
    return (
        output,
        grad_input,
        shard_gain_one,
        shard_qkv,
        shard_out,
        shard_gain_two,
        shard_router,
        shard_gate,
        shard_up,
        shard_down,
    )


def solution(mesh):
    rows, vector = P(BOTH, None), P(BOTH)
    middle = P(None, BOTH, None)
    in_specs = (
        rows, vector, rows, rows, vector, rows, middle, middle, middle, P(), rows, rows,
    )
    out_specs = (rows, rows, vector, rows, rows, vector, rows, middle, middle, middle)
    return jax.shard_map(
        on_device, mesh=mesh, in_specs=in_specs, out_specs=out_specs, check_vma=False
    )
```
